32 devices in a mesh: cell: 2 (over core), gene: 16 (over z, y, x).
Axes of the slice: x: 2, y: 2, z: 4, core: 2. Of those that a mesh axis runs over, the one named last changes fastest.
Arguments:
- encoder_packed_tokens: bfloat16 [2, 15360, 768], P('cell', 'gene'), may hold values from -6 to 6
- token_gene_index: int32 [2, 15360], P('cell', 'gene'), may hold values from -1 to 2559, as said below
- cell_counts: int32 [2, 128], P('cell', 'gene'), may hold values from 40 to 120
- zero_embed: bfloat16 [2560, 768], P('gene'), may hold values from -6 to 6
- random_features: bfloat16 [64, 256], replicated, may hold values from -4 to 4
- input_weight: bfloat16 [768, 512], replicated, may hold values from -0.21875 to 0.21875
- input_bias: float32 [512], replicated, may hold values from -0.15625 to 0.15625
- first_gain: float32 [512], replicated, may hold values from 0.5 to 1.5
- first_shift: float32 [512], replicated, may hold values from -0.15625 to 0.15625
- joint_weight: bfloat16 [512, 1536], replicated, may hold values from -0.25 to 0.25
- joint_bias: float32 [1536], replicated, may hold values from -0.15625 to 0.15625
- output_weight: bfloat16 [512, 512], replicated, may hold values from -1.5 to 1.5
- output_bias: float32 [512], replicated, may hold values from -4 to 4
- second_gain: float32 [512], replicated, may hold values from 0.5 to 1.5
- second_shift: float32 [512], replicated, may hold values from -4 to 4
- upper_weight: bfloat16 [512, 2048], replicated, may hold values from -0.25 to 0.25
- upper_bias: float32 [2048], replicated, may hold values from -4 to 4
- lower_weight: bfloat16 [2048, 512], replicated, may hold values from -0.125 to 0.125
- lower_bias: float32 [512], replicated, may hold values from -4 to 4
- cotangent: bfloat16 [16, 2560, 512], P('cell', 'gene'), may hold values from -6 to 6
Outputs:
- block_out: bfloat16 [16, 2560, 512], P('cell', 'gene')
- token_grad: float32 [2, 15360, 768], P('cell', 'gene')
- zero_grad: float32 [2560, 768], P('gene')
- grad_input_weight: float32 [768, 512], P('gene')
- grad_input_bias: float32 [512], P('gene')
- grad_first_gain: float32 [512], P('gene')
- grad_first_shift: float32 [512], P('gene')
- grad_joint_weight: float32 [512, 1536], P('gene')
- grad_joint_bias: float32 [1536], P('gene')
- grad_output_weight: float32 [512, 512], P('gene')
- grad_output_bias: float32 [512], P('gene')
- grad_second_gain: float32 [512], P('gene')
- grad_second_shift: float32 [512], P('gene')
- grad_upper_weight: float32 [512, 2048], P('gene')
- grad_upper_bias: float32 [2048], P('gene')
- grad_lower_weight: float32 [2048, 512], P('gene')
- grad_lower_bias: float32 [512], P('gene')
The draws below stay inside these ranges and needn't reach their ends.
Inputs may be any that keep to these rules, and one draw needn't show every extreme that they name: `token_gene_index`: row (a, s) holds only genes of s * 160 to (s + 1) * 160 - 1; each cell's genes in a row are distinct and ascending; the empty slots after the row's tokens hold -1.
All inputs are finite; a program needn't handle non-finite values.
Results may differ from the reference program's by a relative error of at most 0.019.
Values sent between devices are 32-bit elements; how exact they have to be, the bound alone decides.
No kernel may reach another device: no remote copies, remote signals or barrier semaphores. Data moves between devices by JAX's collectives and lax.ppermute only.
A program may use at most 192 MiB of HBM per device.

```python
import jax
import jax.numpy as jnp
from jax import lax

ENCODER_WIDTH = 768
D = 512
HEADS = 8
HEAD = 64
FF = 2048
FEATS = 256
CELLS_DEV = 8
G_DEV = 160
PACKED_ROW_SLOTS = 960
CELL_GROUPS = 2
GENE_BLOCKS = 16
CELL_TOTAL = 16
GENE_POSITIONS = 2560


def packing(seed_key):
    lowest = G_DEV // 4
    largest = 3 * G_DEV // 4
    count_key, order_key = jax.random.split(seed_key)
    counts = jax.random.randint(count_key, (CELL_GROUPS, GENE_BLOCKS, CELLS_DEV), lowest, largest + 1)
    counts = counts.at[0, 0, 0].set(largest)
    scores = jax.random.randint(order_key, (CELL_GROUPS, GENE_BLOCKS, CELLS_DEV, G_DEV), 0, 1 << 20) * G_DEV
    scores = scores + jnp.arange(G_DEV, dtype=jnp.int32)
    ranks = jnp.argsort(jnp.argsort(scores, axis=-1, stable=True), axis=-1, stable=True).astype(jnp.int32)
    picked_slots = ranks < counts[..., None]
    within = jnp.cumsum(picked_slots.astype(jnp.int32), axis=-1) - 1
    offsets = jnp.cumsum(counts, axis=-1) - counts
    slot_position = within + offsets[..., None]
    packed_row_index = jnp.arange(CELL_GROUPS, dtype=jnp.int32)[:, None, None, None] * GENE_BLOCKS + jnp.arange(GENE_BLOCKS, dtype=jnp.int32)[None, :, None, None]
    flattened_slot = jnp.where(picked_slots, packed_row_index * PACKED_ROW_SLOTS + slot_position, CELL_GROUPS * GENE_BLOCKS * PACKED_ROW_SLOTS)
    every_gene = jnp.arange(GENE_BLOCKS, dtype=jnp.int32)[None, :, None, None] * G_DEV + jnp.arange(G_DEV, dtype=jnp.int32)
    every_gene = jnp.broadcast_to(every_gene, picked_slots.shape)
    gene_table = jnp.full((CELL_GROUPS * GENE_BLOCKS * PACKED_ROW_SLOTS,), -1, jnp.int32).at[flattened_slot.reshape(-1)].set(every_gene.reshape(-1), mode='drop')
    return (counts, gene_table)


def draw_token_gene_index(key, part):
    counts, gene_table = packing(key)
    return gene_table.reshape(CELL_GROUPS, GENE_BLOCKS * PACKED_ROW_SLOTS)


def draw_cell_counts(key, part):
    counts, gene_table = packing(key)
    return counts.reshape(CELL_GROUPS, GENE_BLOCKS * CELLS_DEV)


def block_levels(key, extent, cuts, smallest, top_value):
    gain = 1.0
    for axis_at, shards_of in cuts:
        heights = jax.random.uniform(jax.random.fold_in(jax.random.fold_in(key, 6), axis_at), (shards_of,), jnp.float32, smallest / len(cuts), top_value / len(cuts))
        gain = gain * jnp.repeat(jnp.exp(heights), extent[axis_at] // shards_of).reshape((-1,) + (1,) * (len(extent) - 1 - axis_at))
    return gain


def gaussian(stream_key, dims, width, most, pieces=(), held_as=jnp.bfloat16):
    array = jax.random.normal(stream_key, dims, jnp.float32) * width
    if len(pieces) > 0:
        array = block_levels(stream_key, dims, pieces, -0.22, 0.18) * array
    return jnp.clip(array, min=-most, max=most).astype(held_as)


def setup_inputs(seed: int = 0) -> dict:
    keys = jax.random.split(jax.random.key(seed), 21)
    encoder_packed_tokens = gaussian(keys[0], (CELL_GROUPS, GENE_BLOCKS * PACKED_ROW_SLOTS, ENCODER_WIDTH), 1.0, 6.0, ((0, 2), (1, 16)))
    token_gene_index = draw_token_gene_index(jax.random.fold_in(keys[20], 71), 0)
    cell_counts = draw_cell_counts(jax.random.fold_in(keys[20], 71), 0)
    zero_embed = gaussian(keys[3], (GENE_POSITIONS, ENCODER_WIDTH), 1.0, 6.0, ((0, 16),))
    random_features = gaussian(keys[4], (HEAD, FEATS), 1.0, 4.0)
    input_weight = gaussian(keys[5], (ENCODER_WIDTH, D), ENCODER_WIDTH ** -0.5, 0.21875)
    input_bias = gaussian(keys[6], (D,), 0.01, 0.15625, (), jnp.float32)
    first_gain = jnp.clip(1.0 + 0.1 * jax.random.normal(keys[7], (D,), jnp.float32), 0.5, 1.5)
    first_shift = gaussian(keys[8], (D,), 0.01, 0.15625, (), jnp.float32)
    joint_weight = gaussian(keys[9], (D, 3 * D), D ** -0.5, 0.25)
    joint_bias = gaussian(keys[10], (3 * D,), 0.01, 0.15625, (), jnp.float32)
    output_weight = gaussian(keys[11], (D, D), (1.0 * (GENE_POSITIONS // D) ** 0.5 * D ** -0.5), 1.5)
    output_bias = gaussian(keys[12], (D,), 0.3, 4.0, (), jnp.float32)
    second_gain = jnp.clip(1.0 + 0.1 * jax.random.normal(keys[13], (D,), jnp.float32), 0.5, 1.5)
    second_shift = gaussian(keys[14], (D,), 0.3, 4.0, (), jnp.float32)
    upper_weight = gaussian(keys[15], (D, FF), D ** -0.5, 0.25)
    upper_bias = gaussian(keys[16], (FF,), 0.3, 4.0, (), jnp.float32)
    lower_weight = gaussian(keys[17], (FF, D), FF ** -0.5, 0.125)
    lower_bias = gaussian(keys[18], (D,), 0.3, 4.0, (), jnp.float32)
    cotangent = gaussian(keys[19], (CELL_TOTAL, GENE_POSITIONS, D), 1.0, 6.0, ((0, 2), (1, 16)))
    return dict(encoder_packed_tokens=encoder_packed_tokens, token_gene_index=token_gene_index, cell_counts=cell_counts, zero_embed=zero_embed, random_features=random_features, input_weight=input_weight, input_bias=input_bias, first_gain=first_gain, first_shift=first_shift, joint_weight=joint_weight, joint_bias=joint_bias, output_weight=output_weight, output_bias=output_bias, second_gain=second_gain, second_shift=second_shift, upper_weight=upper_weight, upper_bias=upper_bias, lower_weight=lower_weight, lower_bias=lower_bias, cotangent=cotangent)


@jax.custom_vjp
def low(v):
    return lax.optimization_barrier(v.astype(jnp.bfloat16)).astype(jnp.float32)

@jax.custom_vjp
def low_back(v):
    return v

def low_keep(v):
    return (low(v), None)

def low_pass(kept, grad):
    return (grad,)

def back_keep(v):
    return (v, None)

def back_low(kept, grad):
    return (low(grad),)
low.defvjp(low_keep, low_pass)
low_back.defvjp(back_keep, back_low)

def product(left, right):
    return jnp.dot(left, right, precision=lax.Precision.HIGHEST)

def layer_norm(values, gain_vector, shift_vector):
    centred = values - lax.optimization_barrier(jnp.mean(values, axis=-1, keepdims=True))
    spread = lax.optimization_barrier(jnp.mean(centred * centred, axis=-1, keepdims=True))
    return centred * lax.rsqrt(spread + 1e-05) * gain_vector + shift_vector

def feature_map(heads_in, random_features):
    factor = HEAD ** (-0.25)
    projected = low_back(jnp.einsum('ghd,dm->ghm', heads_in, random_features, precision=lax.Precision.HIGHEST))
    squared = lax.optimization_barrier(jnp.sum(heads_in * heads_in, axis=-1, keepdims=True))
    return low(jnp.exp(factor * projected - 0.5 * factor * factor * squared) * FEATS ** (-0.5))

def cell_forward(weights, gene_rows):
    random_features, input_weight, input_bias, first_gain, first_shift, joint_weight, joint_bias, output_weight, output_bias, second_gain, second_shift, upper_weight, upper_bias, lower_weight, lower_bias = weights
    hidden = low_back(product(gene_rows, input_weight) + input_bias)
    normed = low(layer_norm(hidden, first_gain, first_shift))
    joint = low(low_back(product(normed, joint_weight) + joint_bias))
    query = joint[:, :D].reshape(GENE_POSITIONS, HEADS, HEAD)
    key_part = joint[:, D:2 * D].reshape(GENE_POSITIONS, HEADS, HEAD)
    value_portion = joint[:, 2 * D:].reshape(GENE_POSITIONS, HEADS, HEAD)
    query_features = feature_map(query, random_features)
    key_features = feature_map(key_part, random_features)
    key_value_summary = jnp.einsum('elu,elz->luz', key_features, value_portion, precision=lax.Precision.HIGHEST)
    total = lax.optimization_barrier(jnp.sum(key_features, axis=0))
    attention_numerator = low_back(jnp.einsum('sji,jiz->sjz', query_features, key_value_summary, precision=lax.Precision.HIGHEST))
    denominator = jnp.einsum('ghm,hm->gh', query_features, total, precision=lax.Precision.HIGHEST)
    attention = low((attention_numerator / denominator[:, :, None]).reshape(GENE_POSITIONS, D))
    middle = hidden + low_back(product(attention, output_weight) + output_bias)
    normed_two = low(layer_norm(middle, second_gain, second_shift))
    upper = low_back(product(normed_two, upper_weight) + upper_bias)
    active = low(jax.nn.gelu(upper, approximate=False))
    return middle + low_back(product(active, lower_weight) + lower_bias)

def slot_targets(token_gene_index, cell_counts):
    counts = cell_counts.reshape(CELL_GROUPS, GENE_BLOCKS, CELLS_DEV)
    cell_ends = jnp.cumsum(counts, axis=-1)
    slot_indices = jnp.arange(PACKED_ROW_SLOTS, dtype=jnp.int32)
    segment = lax.optimization_barrier(jnp.sum((slot_indices[None, None, :, None] >= cell_ends[:, :, None, :]).astype(jnp.int32), axis=-1))
    cell_number = jnp.arange(CELL_GROUPS, dtype=jnp.int32)[:, None, None] * CELLS_DEV + segment
    device_genes = token_gene_index.reshape(CELL_GROUPS, GENE_BLOCKS, PACKED_ROW_SLOTS)
    target_slot = jnp.where(segment < CELLS_DEV, cell_number * GENE_POSITIONS + device_genes, CELL_TOTAL * GENE_POSITIONS)
    return target_slot.reshape(CELL_GROUPS * GENE_BLOCKS * PACKED_ROW_SLOTS).astype(jnp.int32)

def reference(encoder_packed_tokens, token_gene_index, cell_counts, zero_embed, random_features, input_weight, input_bias, first_gain, first_shift, joint_weight, joint_bias, output_weight, output_bias, second_gain, second_shift, upper_weight, upper_bias, lower_weight, lower_bias, cotangent):
    target_slot = slot_targets(token_gene_index, cell_counts)
    marks = jnp.zeros((CELL_TOTAL * GENE_POSITIONS,), jnp.float32).at[target_slot].add(1.0, mode='drop')
    vacant = (1.0 - marks)[:, None]

    def forward(incoming_tokens, zeros_in, weights):
        scattered_tokens = jnp.zeros((CELL_TOTAL * GENE_POSITIONS, ENCODER_WIDTH), jnp.float32).at[target_slot].add(incoming_tokens.reshape(CELL_GROUPS * GENE_BLOCKS * PACKED_ROW_SLOTS, ENCODER_WIDTH), mode='drop')
        gene_rows = scattered_tokens + vacant * jnp.tile(zeros_in, (CELL_TOTAL, 1))

        def through(carry, cell_rows):
            return (carry, jax.checkpoint(cell_forward)(weights, cell_rows))
        unused, outputs = lax.scan(through, jnp.zeros((), jnp.float32), gene_rows.reshape(CELL_TOTAL, GENE_POSITIONS, ENCODER_WIDTH))
        return outputs
    weights = tuple((member.astype(jnp.float32) for member in (random_features, input_weight, input_bias, first_gain, first_shift, joint_weight, joint_bias, output_weight, output_bias, second_gain, second_shift, upper_weight, upper_bias, lower_weight, lower_bias)))
    outputs, pullback = jax.vjp(forward, encoder_packed_tokens.astype(jnp.float32), zero_embed.astype(jnp.float32), weights)
    token_grad, zero_grad, grads = pullback(cotangent.astype(jnp.float32))
    return (outputs.astype(jnp.bfloat16), token_grad, zero_grad, grads[1], grads[2], grads[3], grads[4], grads[5], grads[6], grads[7], grads[8], grads[9], grads[10], grads[11], grads[12], grads[13], grads[14])
```

```python
import jax
import jax.numpy as jnp
from jax import lax
from jax.experimental import pallas as pl
from jax.sharding import PartitionSpec as P

epsilon = 1e-05
highest = lax.Precision.HIGHEST


def normalize(values, gain_vector, shift_vector):
    centred = values - jnp.mean(values, axis=-1, keepdims=True)
    inverse = lax.rsqrt(jnp.mean(centred * centred, axis=-1, keepdims=True) + epsilon)
    scaled = centred * inverse
    return (scaled * gain_vector + shift_vector, scaled, inverse)


def normalize_back(grad_in, scaled, inverse, gain_vector):
    weighted = grad_in * gain_vector
    return inverse * (
        weighted
        - jnp.mean(weighted, axis=-1, keepdims=True)
        - scaled * jnp.mean(weighted * scaled, axis=-1, keepdims=True)
    )


def feature_map(heads_in, random_features, factor):
    projected = jnp.einsum(
        "cghd,dm->cghm", heads_in, random_features, preferred_element_type=jnp.float32
    )
    widened = heads_in.astype(jnp.float32)
    squared = jnp.sum(widened * widened, axis=-1, keepdims=True)
    feature_count = random_features.shape[1]
    return jnp.exp(factor * projected - 0.5 * factor * factor * squared) * feature_count ** (-0.5)


def feature_back(grad_feat, feature_values, heads_in, random_features, factor):
    weighted = grad_feat * feature_values
    projected_grad = (weighted * factor).astype(jnp.bfloat16)
    through = jnp.einsum(
        "cghm,dm->cghd", projected_grad, random_features, preferred_element_type=jnp.float32
    )
    return through - factor * factor * heads_in.astype(jnp.float32) * jnp.sum(
        weighted, axis=-1, keepdims=True
    )


def swap(value, axis, size, bit):
    return lax.ppermute(value, axis, [(i, i ^ bit) for i in range(size)])


def rounded(value):
    def kernel(wide_ref, low_ref):
        low_ref[...] = wide_ref[...].astype(jnp.bfloat16)

    return pl.pallas_call(
        kernel, out_shape=jax.ShapeDtypeStruct(value.shape, jnp.bfloat16), name="rounded"
    )(value)


def fence(value):
    return lax.optimization_barrier(value)


def sum_over_planes(mine_first, size, plane):
    high = [1 << b for b in range(size.bit_length()) if plane <= (1 << b) < size]
    mine = mine_first[0] + swap(mine_first[1], "gene", size, high[0])
    for bit in high[1:]:
        mine = mine + swap(mine, "gene", size, bit)
    return mine, swap(mine, "gene", size, high[0])


def local(
    encoder_packed_tokens,
    token_gene_index,
    cell_counts,
    zero_embed,
    random_features,
    input_weight,
    input_bias,
    first_gain,
    first_shift,
    joint_weight,
    joint_bias,
    output_weight,
    output_bias,
    second_gain,
    second_shift,
    upper_weight,
    upper_bias,
    lower_weight,
    lower_bias,
    cotangent,
):
    size = lax.axis_size("gene")
    plane = 4
    bf16 = jnp.bfloat16
    f32 = jnp.float32
    me = lax.axis_index("gene")
    core = lax.axis_index("cell")
    place = me % plane
    half_at = (me // plane) % 2
    cells_here, device_genes, width = cotangent.shape
    row_length = encoder_packed_tokens.shape[1]
    width_in = encoder_packed_tokens.shape[2]
    head_size, features = random_features.shape
    heads = width // head_size
    factor = head_size ** (-0.25)
    group = cells_here // plane
    first_gene = me * device_genes
    cell_ends = jnp.cumsum(cell_counts[0])
    slot_indices = jnp.arange(row_length, dtype=jnp.int32)
    segment = jnp.sum((slot_indices[:, None] >= cell_ends[None, :]).astype(jnp.int32), axis=1)
    living = segment < cells_here
    target_slot = jnp.where(living, segment * device_genes + token_gene_index[0] - first_gene, -1)
    places = jnp.arange(cells_here * device_genes, dtype=jnp.int32)
    select = target_slot[:, None] == places[None, :]
    scattered = jnp.einsum(
        "rt,ri->ti", select.astype(bf16), encoder_packed_tokens[0], preferred_element_type=f32
    )
    vacant = 1.0 - jnp.sum(select.astype(f32), axis=0)
    gene_rows = scattered + vacant[:, None] * jnp.tile(zero_embed.astype(f32), (cells_here, 1))
    gene_rows = gene_rows.astype(bf16)
    hidden_home = jnp.dot(gene_rows, input_weight, preferred_element_type=f32) + input_bias
    order = place ^ jnp.arange(plane)

    def out_and_in(home):
        parts = home.reshape(plane, group, device_genes, -1)[order]
        return jnp.stack([parts[0]] + [swap(parts[r], "gene", size, r) for r in range(1, plane)])

    def back_home(blocks):
        parts = jnp.stack(
            [blocks[0]] + [swap(blocks[r], "gene", size, r) for r in range(1, plane)]
        )
        return parts[order].reshape(cells_here, device_genes, -1)

    tokens = plane * group * device_genes
    cells_first = (1, 0, 2, 3)

    def by_cell(blocks):
        return blocks.transpose(cells_first).reshape(tokens, -1)

    def by_block(rows):
        return rows.reshape(group, plane, device_genes, -1).transpose(cells_first)

    hidden = by_cell(out_and_in(hidden_home))
    grad_out = fence(by_cell(out_and_in(cotangent.astype(f32))))
    grad_low = grad_out.astype(bf16)
    normed, scaled_one, inverse_one = normalize(hidden, first_gain, first_shift)
    normed_low = normed.astype(bf16)
    joint = (jnp.dot(normed_low, joint_weight, preferred_element_type=f32) + joint_bias).astype(bf16)
    per_cell = plane * device_genes
    split = (group, per_cell, heads, head_size)
    query = joint[:, :width].reshape(split)
    key_part = joint[:, width : 2 * width].reshape(split)
    value_part = joint[:, 2 * width :].reshape(split)
    query_low = feature_map(query, random_features, factor).astype(bf16)
    key_low = feature_map(key_part, random_features, factor).astype(bf16)

    def pack(summary, total):
        both = jnp.concatenate(
            [
                summary.reshape(group, 2, heads // 2 * head_size, features),
                jnp.pad(total.reshape(group, 2, heads // 2, features), ((0, 0), (0, 0), (0, 4), (0, 0))),
            ],
            axis=2,
        )
        return both[:, half_at ^ jnp.arange(2)]

    def unpack(pair):
        both = jnp.stack(pair)[half_at ^ jnp.arange(2)]
        rows = heads // 2 * head_size
        summary = both[:, :rows].reshape(heads, head_size, features)
        total = both[:, rows : rows + heads // 2].reshape(heads, features)
        return summary, total

    def over_genes(summary, total):
        packed = pack(summary, total)
        done = [unpack(sum_over_planes(packed[c], size, plane)) for c in range(group)]
        return jnp.stack([d[0] for d in done]), jnp.stack([d[1] for d in done])

    summary, total = over_genes(
        jnp.einsum("cghd,cghm->chdm", value_part, key_low, preferred_element_type=f32),
        jnp.sum(key_low, axis=1, dtype=f32),
    )
    summary_low = fence(summary).astype(bf16)
    total_low = fence(total).astype(bf16)
    numerator = jnp.einsum("cghm,chdm->cghd", query_low, summary_low, preferred_element_type=f32)
    denominator = jnp.einsum("cghm,chm->cgh", query_low, total_low, preferred_element_type=f32)
    attention = numerator / denominator[..., None]
    attention_low = attention.reshape(tokens, width).astype(bf16)
    middle = hidden + (
        jnp.dot(attention_low, output_weight, preferred_element_type=f32) + output_bias
    )
    normed_two, scaled_two, inverse_two = normalize(middle, second_gain, second_shift)
    normed_two_low = normed_two.astype(bf16)
    upper = jnp.dot(normed_two_low, upper_weight, preferred_element_type=f32) + upper_bias
    cumulative = 0.5 * (1.0 + lax.erf(upper * 0.7071067811865476))
    active_low = (upper * cumulative).astype(bf16)
    result = middle + jnp.dot(active_low, lower_weight, preferred_element_type=f32)
    block_out = (back_home(by_block(result)) + lower_bias).astype(bf16)
    grad_active = jnp.einsum("td,fd->tf", grad_low, lower_weight, preferred_element_type=f32)
    density = jnp.exp(-0.5 * upper * upper) * 0.3989422804014327
    upper_low = (grad_active * (cumulative + upper * density)).astype(bf16)
    grad_normed_two = jnp.einsum("tf,df->td", upper_low, upper_weight, preferred_element_type=f32)
    grad_middle = grad_out + normalize_back(grad_normed_two, scaled_two, inverse_two, second_gain)
    branch_low = grad_middle.astype(bf16)
    grad_attention = jnp.einsum(
        "td,ed->te", branch_low, output_weight, preferred_element_type=f32
    ).reshape(split)
    numerator_low = (grad_attention / denominator[..., None]).astype(bf16)
    grad_denominator = -jnp.sum(grad_attention * attention, axis=-1) / denominator
    grad_summary, grad_total = over_genes(
        jnp.einsum("cghd,cghm->chdm", numerator_low, query_low, preferred_element_type=f32),
        jnp.einsum("cghm,cgh->chm", query_low.astype(f32), grad_denominator, precision=highest),
    )
    grad_summary_low = fence(grad_summary).astype(bf16)
    grad_query_feat = (
        jnp.einsum("cghd,chdm->cghm", numerator_low, summary_low, preferred_element_type=f32)
        + grad_denominator[..., None] * total[:, None]
    )
    grad_key_feat = (
        jnp.einsum("cghd,chdm->cghm", value_part, grad_summary_low, preferred_element_type=f32)
        + grad_total[:, None]
    )
    grad_value = jnp.einsum(
        "cghm,chdm->cghd", key_low, grad_summary_low, preferred_element_type=f32
    )
    grad_query = feature_back(
        grad_query_feat, query_low.astype(f32), query, random_features, factor
    )
    grad_key = feature_back(grad_key_feat, key_low.astype(f32), key_part, random_features, factor)
    joint_low = jnp.concatenate(
        [
            grad_query.reshape(tokens, width),
            grad_key.reshape(tokens, width),
            grad_value.reshape(tokens, width),
        ],
        axis=1,
    ).astype(bf16)
    grad_normed = jnp.einsum("te,de->td", joint_low, joint_weight, preferred_element_type=f32)
    grad_hidden = grad_middle + normalize_back(grad_normed, scaled_one, inverse_one, first_gain)
    hidden_round = fence(grad_hidden.astype(bf16)).astype(f32)
    hidden_low = rounded(back_home(by_block(hidden_round)).reshape(cells_here * device_genes, width))

    def core_half(matrix):
        halves = jnp.stack(jnp.split(matrix, 2, axis=1))
        return halves[core] + swap(halves[1 - core], "cell", 2, 1)

    def shards(matrix):
        rows = matrix.shape[0] // size
        return matrix.reshape(size, rows * matrix.shape[1] // 256, 256)

    def scatter_sum(bundle, bits):
        rest = bundle[me ^ jnp.arange(size)]
        rest = rest.reshape((2,) * (size.bit_length() - 1) + rest.shape[1:])
        left = list(range(size.bit_length() - 2, -1, -1))
        for bit in bits:
            at = left.index(bit)
            left.pop(at)
            rest = lax.index_in_dim(rest, 0, at, keepdims=False) + swap(
                lax.index_in_dim(rest, 1, at, keepdims=False), "gene", size, 1 << bit
            )
        return rest

    grad_lower_weight = jnp.einsum("tf,td->fd", active_low, grad_low, preferred_element_type=f32)
    grad_upper_weight = jnp.einsum("td,tf->df", normed_two_low, upper_low, preferred_element_type=f32)
    grad_output_weight = jnp.einsum("te,td->ed", attention_low, branch_low, preferred_element_type=f32)
    grad_joint_weight = jnp.einsum("td,te->de", normed_low, joint_low, preferred_element_type=f32)
    grad_input_weight = jnp.einsum("ti,td->id", gene_rows, hidden_low, preferred_element_type=f32)
    small = [
        jnp.sum(hidden_low, axis=0, dtype=f32),
        jnp.sum(grad_normed * scaled_one, axis=0),
        jnp.sum(grad_normed, axis=0),
        jnp.sum(joint_low, axis=0, dtype=f32),
        jnp.sum(branch_low, axis=0, dtype=f32),
        jnp.sum(grad_normed_two * scaled_two, axis=0),
        jnp.sum(grad_normed_two, axis=0),
        jnp.sum(upper_low, axis=0, dtype=f32),
        jnp.sum(grad_out, axis=0),
    ]
    small_lengths = [v.shape[0] // size for v in small]
    vectors = jnp.concatenate([v.reshape(size, -1) for v in small], axis=1)
    vectors = vectors + swap(vectors, "cell", 2, 1)
    pad = (-vectors.shape[1]) % 256
    vectors = jnp.pad(vectors, ((0, 0), (0, pad))).reshape(size, -1, 256)
    log = size.bit_length() - 1
    mats_one = [grad_lower_weight, grad_upper_weight, grad_output_weight]
    mats_two = [grad_joint_weight, grad_input_weight]
    bundle_one = jnp.concatenate([shards(core_half(m)) for m in mats_one], axis=1)
    bundle_two = jnp.concatenate([shards(core_half(m)) for m in mats_two] + [vectors], axis=1)
    done_one = scatter_sum(bundle_one, list(range(log)))
    done_two = scatter_sum(bundle_two, list(range(log)))
    other_one = swap(done_one, "cell", 2, 1)
    other_two = swap(done_two, "cell", 2, 1)

    def open_bundle(mine, other, mats):
        first = jnp.where(core == 0, mine, other)
        second = jnp.where(core == 0, other, mine)
        out = []
        at = 0
        for m in mats:
            rows = m.shape[0] // size
            count = rows * m.shape[1] // 2 // 256
            out.append(
                jnp.concatenate(
                    [b[at : at + count].reshape(rows, m.shape[1] // 2) for b in (first, second)],
                    axis=1,
                )
            )
            at += count
        return out, at

    (g_lower, g_upper, g_output), at = open_bundle(done_one, other_one, mats_one)
    (g_joint, g_input), at = open_bundle(done_two, other_two, mats_two)
    flat = done_two[at:].reshape(-1)
    small_out = []
    at = 0
    for length in small_lengths:
        small_out.append(flat[at : at + length])
        at += length
    picked = jnp.einsum("rt,td->rd", select.astype(bf16), hidden_low, preferred_element_type=f32)
    token_grad = jnp.einsum(
        "rd,id->ri", picked.astype(bf16), input_weight, preferred_element_type=f32
    ).reshape(1, row_length, width_in)
    zero_hidden = jnp.sum(
        (vacant[:, None] * hidden_low.astype(f32)).reshape(cells_here, device_genes, width), axis=0
    )
    zero_hidden = zero_hidden + swap(zero_hidden, "cell", 2, 1)
    zero_grad = jnp.einsum("td,id->ti", zero_hidden, input_weight.astype(f32), precision=highest)
    return (
        block_out,
        token_grad,
        zero_grad,
        g_input,
        small_out[0],
        small_out[1],
        small_out[2],
        g_joint,
        small_out[3],
        g_output,
        small_out[4],
        small_out[5],
        small_out[6],
        g_upper,
        small_out[7],
        g_lower,
        small_out[8],
    )


def solution(mesh):
    return jax.shard_map(
        local,
        mesh=mesh,
        in_specs=(
            P("cell", "gene", None),
            P("cell", "gene"),
            P("cell", "gene"),
            P("gene", None),
            P(),
            P(),
            P(),
            P(),
            P(),
            P(),
            P(),
            P(),
            P(),
            P(),
            P(),
            P(),
            P(),
            P(),
            P(),
            P("cell", "gene", None),
        ),
        out_specs=(
            P("cell", "gene", None),
            P("cell", "gene", None),
            P("gene", None),
            P("gene", None),
            P("gene"),
            P("gene"),
            P("gene"),
            P("gene", None),
            P("gene"),
            P("gene", None),
            P("gene"),
            P("gene"),
            P("gene"),
            P("gene", None),
            P("gene"),
            P("gene", None),
            P("gene"),
        ),
        check_vma=False,
    )
```

```python
import functools
import math

import jax
import jax.numpy as jnp
from jax import lax
from jax.experimental import pallas as pl
from jax.experimental.pallas import tpu as pltpu
from jax.sharding import PartitionSpec as P

epsilon = 1e-05
f32 = jnp.float32
bf16 = jnp.bfloat16
plane = 4
tile = 2


def nn(left, right):
    return jnp.dot(left, right, preferred_element_type=f32)


def nt(left, right):
    return lax.dot_general(left, right, (((1,), (1,)), ((), ())), preferred_element_type=f32)


def tn(left, right):
    return lax.dot_general(left, right, (((0,), (0,)), ((), ())), preferred_element_type=f32)


def col_sum(values):
    return jnp.sum(values, axis=0, keepdims=True)


def norm_parts(values):
    centred = values - jnp.mean(values, axis=-1, keepdims=True)
    inverse = lax.rsqrt(jnp.mean(centred * centred, axis=-1, keepdims=True) + epsilon)
    return centred * inverse, inverse


def norm_back(grad_in, scaled, inverse, gain):
    weighted = grad_in * gain
    return inverse * (
        weighted
        - jnp.mean(weighted, axis=-1, keepdims=True)
        - scaled * jnp.mean(weighted * scaled, axis=-1, keepdims=True)
    )


def whole(shape):
    return pl.BlockSpec(shape, lambda *at: (0,) * len(shape))


placed_at = []


def near(shape, dtype=f32):
    return pltpu.VMEM(shape, dtype)


def far(shape, dtype=f32):
    return pltpu.HBM(shape, dtype)


def free(shape, dtype=f32):
    return jax.ShapeDtypeStruct(shape, dtype)


def placed(order, log):
    return lambda number: sum(((number >> bit) & 1) << (log - 1 - i) for i, bit in enumerate(order))


def call(kernel, name, grid, in_specs, outs, out_specs, scratch, *args, after=(), mib=60):
    first = 1 + len(in_specs)

    def body(*refs):
        kernel(*refs[:first], *refs[first + len(after) :])

    def held(array):
        for other, space in placed_at:
            if array is other:
                return pltpu.with_memory_space_constraint(array, space)
        return array

    made = pl.pallas_call(
        body,
        name=name,
        grid_spec=pltpu.PrefetchScalarGridSpec(
            num_scalar_prefetch=1,
            grid=grid,
            in_specs=list(in_specs) + [pl.BlockSpec(memory_space=pl.ANY)] * len(after),
            out_specs=out_specs,
            scratch_shapes=scratch,
        ),
        out_shape=outs,
        compiler_params=pltpu.CompilerParams(
            vmem_limit_bytes=mib << 20, dimension_semantics=("arbitrary",) * len(grid)
        ),
        cost_estimate=pl.CostEstimate(flops=1000, bytes_accessed=1000, transcendentals=0),
    )(args[0], *(held(a) for a in args[1:]), *(held(a) for a in after))
    several = isinstance(outs, (list, tuple))
    for out, array in zip(outs if several else [outs], made if several else [made]):
        if getattr(out, "memory_space", None) in (pltpu.VMEM, pltpu.HBM):
            placed_at.append((array, out.memory_space))
    return made


def swap(value, axis, size, bit):
    return lax.ppermute(value, axis, [(i, i ^ bit) for i in range(size)])


def rows_kernel(ids, tokens, index, zero, weight, bias, h0, h1, h2, h3, rows_out, vacant_out, *, group, j):
    genes = zero.shape[0]
    first_gene = ids[0] * genes
    slots = index.shape[1]
    slot = lax.broadcasted_iota(jnp.int32, (genes, slots), 1)
    gene = lax.broadcasted_iota(jnp.int32, (genes, slots), 0)
    match = (index[...] - first_gene) == gene
    for r in (3, 1, 2, 0):
        cell = (ids[2] ^ r) * group + j
        here = match & (slot >= ids[8 + cell]) & (slot < ids[9 + cell])
        chosen = jnp.where(here, 1.0, 0.0)
        vacant = 1.0 - jnp.sum(chosen, axis=1, keepdims=True)
        rows = nn(chosen.astype(bf16), tokens[...]) + vacant * zero[...].astype(f32)
        rows = rows.astype(bf16)
        rows_out[r] = rows
        vacant_out[r] = jnp.broadcast_to(vacant, (genes, 128))
        (h0, h1, h2, h3)[r][...] = nn(rows, weight[...]) + bias[...]


def rows_call(ids, j, group, tokens, index, zero, weight, bias, after=()):
    genes, width_in = zero.shape
    width = weight.shape[1]
    outs = [free((genes, width))] * plane + [
        far((plane, genes, width_in), bf16),
        far((plane, genes, 128)),
    ]
    ins = [tokens, index, zero, weight, bias]
    return call(
        functools.partial(rows_kernel, group=group, j=j),
        "gene_rows",
        (1,),
        [whole(a.shape) for a in ins],
        outs,
        [whole(o.shape) for o in outs],
        [],
        ids,
        *ins,
        after=after,
        mib=20,
    )


def cotangent_kernel(ids, cot, c0, c1, c2, c3):
    for r, out in enumerate((c0, c1, c2, c3)):
        for j in range(out.shape[0]):
            out[j] = cot[(ids[2] ^ r) * out.shape[0] + j].astype(f32)


def cotangent_call(ids, group, cot, after=()):
    _, genes, width = cot.shape
    outs = [free((group, genes, width))] * plane
    return call(
        cotangent_kernel,
        "wide_cotangent",
        (1,),
        [whole(cot.shape)],
        outs,
        [whole(o.shape) for o in outs],
        [],
        ids,
        cot,
        after=after,
        mib=14,
    )


def hold_kernel(ids, *refs):
    count = len(refs) // 2
    for given, held in zip(refs[:count], refs[count:]):
        held[...] = given[...]


def hold_call(ids, *arrays, after=()):
    outs = [near(a.shape, a.dtype) for a in arrays]
    return call(
        hold_kernel,
        "hold",
        (1,),
        [whole(a.shape) for a in arrays],
        outs,
        [whole(a.shape) for a in arrays],
        [],
        ids,
        *arrays,
        after=after,
        mib=12,
    )


def add_kernel(ids, mine, came, out):
    out[...] = mine[...] + came[...]


def add_call(ids, mine, came, out=free, after=()):
    return call(
        add_kernel,
        "add",
        (1,),
        [whole(mine.shape)] * 2,
        out(mine.shape),
        whole(mine.shape),
        [],
        ids,
        mine,
        came,
        after=after,
        mib=8,
    )


def split_kernel(ids, mine, came, keep, send, *, extra):
    half = keep.shape[0] - extra
    keep[:half, :] = mine[:half, :] + came[:half, :]
    send[:half, :] = mine[half : 2 * half, :] + came[half : 2 * half, :]
    if extra:
        both = mine[2 * half :, :] + came[2 * half :, :]
        keep[half:, :] = both
        send[half:, :] = both


def split_call(ids, mine, came, extra=0, after=()):
    rows, cols = mine.shape
    shape = ((rows - extra) // 2 + extra, cols)
    return call(
        functools.partial(split_kernel, extra=extra),
        "add_halves",
        (1,),
        [whole(mine.shape)] * 2,
        [near(shape), free(shape)],
        [whole(shape)] * 2,
        [],
        ids,
        mine,
        came,
        after=after,
        mib=16,
    )


def phi_of(u, feature_matrix, factor):
    features = feature_matrix.shape[1] // 2
    wide = u.astype(f32)
    square = (wide * wide * (0.5 * factor)).astype(bf16)
    power = nn(jnp.concatenate([u, square], axis=1), feature_matrix[...])
    scale = factor * math.log2(math.e)
    return jnp.exp2(power * scale - 0.5 * math.log2(features)).astype(bf16)


def put_summary(out, pair, pairs, both, totals, head_size, features):
    half = pair // (pairs // 2)
    at = (pair % (pairs // 2)) * 2
    base = pairs * head_size
    for i in range(2):
        cols = slice(i * features, (i + 1) * features)
        out[half, (at + i) * head_size : (at + i + 1) * head_size, :] = both[
            i * head_size : (i + 1) * head_size, cols
        ]
        out[half, base + at + i : base + at + i + 1, :] = totals[i][:, cols]


def block_matrix(matrix, mine, other, flip, pairs, head_size, features, with_totals):
    base = pairs * head_size
    for pair in range(pairs):
        half = pair // (pairs // 2)
        at = (pair % (pairs // 2)) * 2
        first = (flip ^ half) == 0

        def take(lo, hi):
            return jnp.where(first, mine[lo:hi, :], other[lo:hi, :])

        nothing = jnp.zeros((head_size, features), bf16)
        for i in range(2):
            rows = slice(i * head_size, (i + 1) * head_size)
            part = take((at + i) * head_size, (at + i + 1) * head_size).astype(bf16)
            matrix[pair, rows, i * features : (i + 1) * features] = part
            matrix[pair, rows, (1 - i) * features : (2 - i) * features] = nothing
            if with_totals:
                rows = slice((2 + i) * head_size, (3 + i) * head_size)
                total = take(base + at + i, base + at + i + 1)
                spread = jnp.broadcast_to(total, (head_size, features)).astype(bf16)
                matrix[pair, rows, i * features : (i + 1) * features] = spread
                matrix[pair, rows, (1 - i) * features : (2 - i) * features] = nothing


def payload_shape(heads, head_size, features):
    rows = heads // 2 * head_size + heads // 2
    return (rows + (-rows) % 8, features)


def key_kernel(
    ids, h0, h1, h2, h3, weight, bias, gain, shift, feats, normed, joint, phi, mine, sent, out, *, factor
):
    genes, width = h0.shape
    features = feats.shape[1] // 2
    pair_width = feats.shape[0] // 2
    pairs = width // pair_width
    for r, block in enumerate((h0, h1, h2, h3)):
        scaled, _ = norm_parts(block[...])
        normed[r * genes : (r + 1) * genes, :] = (scaled * gain[...] + shift[...]).astype(bf16)
    for part in (1, 2, 0):
        cols = slice(part * width, (part + 1) * width)
        joint[:, cols] = (nn(normed[...], weight[:, cols]) + bias[:, cols]).astype(bf16)
    rows_used = pairs * (pair_width // 2) + pairs
    spare = out.shape[1] - rows_used
    if spare:
        for i in range(2):
            out[i, rows_used:, :] = jnp.zeros((spare, features), f32)
    for pair in range(pairs):
        at = width + pair * pair_width
        low = phi_of(joint[:, at : at + pair_width], feats, factor)
        phi[:, pair * 2 * features : (pair + 1) * 2 * features] = low
        value = joint[:, width + at : width + at + pair_width]
        total = col_sum(low.astype(f32))
        put_summary(out, pair, pairs, tn(value, low), (total, total), pair_width // 2, features)
    mine[...] = out[ids[3]]
    sent[...] = out[1 - ids[3]]


def key_call(ids, hidden, weight, bias, gain, shift, feats, factor, after=()):
    genes, width = hidden[0].shape
    tokens = plane * genes
    features = feats.shape[1] // 2
    heads = 2 * width // (feats.shape[0] // 2)
    pay = payload_shape(heads, width // heads, features)
    outs = [
        far((tokens, width), bf16),
        near((tokens, 3 * width), bf16),
        far((tokens, heads * features), bf16),
        near(pay),
        free(pay),
    ]
    ins = list(hidden) + [weight, bias, gain, shift, feats]
    return call(
        functools.partial(key_kernel, factor=factor),
        "key_summary",
        (1,),
        [whole(a.shape) for a in ins],
        outs,
        [whole(o.shape) for o in outs],
        [pltpu.VMEM((2, *pay), f32)],
        ids,
        *ins,
        after=after,
        mib=24,
    )


def query_kernel(ids, joint, feats, phi, *, factor):
    features = feats.shape[1] // 2
    pair_width = feats.shape[0] // 2
    for pair in range(joint.shape[1] // pair_width):
        u = joint[:, pair * pair_width : (pair + 1) * pair_width]
        phi[:, pair * 2 * features : (pair + 1) * 2 * features] = phi_of(u, feats, factor)


def query_call(ids, joint, feats, factor, after=()):
    tokens, wide = joint.shape
    width = wide // 3
    features = feats.shape[1] // 2
    heads = 2 * width // (feats.shape[0] // 2)
    step = tokens // tile
    return call(
        functools.partial(query_kernel, factor=factor),
        "query_features",
        (tile,),
        [pl.BlockSpec((step, width), lambda at, ids: (at, 0)), whole(feats.shape)],
        near((tokens, heads * features), bf16),
        pl.BlockSpec((step, heads * features), lambda at, ids: (at, 0)),
        [],
        ids,
        joint,
        feats,
        after=after,
        mib=16,
    )


def gelu_parts(x):
    expo = jnp.exp2(x * x * (-0.5 * math.log2(math.e)))
    t = 1.0 / (1.0 + (0.3275911 * math.sqrt(0.5)) * jnp.abs(x))
    poly = t * (
        0.5 * 0.254829592
        + t
        * (
            0.5 * -0.284496736
            + t * (0.5 * 1.421413741 + t * (0.5 * -1.453152027 + t * (0.5 * 1.061405429)))
        )
    )
    tail = poly * expo
    return jnp.where(x > 0, 1.0 - tail, tail), expo * 0.3989422804014327


def feed_kernel(
    ids, h0, h1, h2, h3, c0, c1, c2, c3, phi, mine, other, w_out, b_out, gain, shift, w_up, b_up, w_low, b_low,
    g0, g1, g2, g3, active, d_upper, normed, attention, d_middle, d_branch, d_num, cot_low, mine_out, sent_out, sums, up_sums,
    pay, matrix, acc, hid, cot, att_wide, recip, scaled_ref, back, result,
):
    step = pl.program_id(0)
    genes, width = h0.shape
    features = phi.shape[1] // matrix.shape[0] // 2
    pairs = matrix.shape[0]
    pair_width = width // pairs
    head_size = pair_width // 2
    chunk = 512

    @pl.when(step == 0)
    def _():
        block_matrix(matrix, mine, other, ids[3], pairs, head_size, features, True)
        acc[...] = jnp.zeros_like(acc)
        sums[...] = jnp.zeros_like(sums)
        up_sums[...] = jnp.zeros_like(up_sums)

    for k in range(plane // tile):

        @pl.when(step == k)
        def _():
            for i in range(tile):
                rows = slice(i * genes, (i + 1) * genes)
                hid[rows, :] = (h0, h1, h2, h3)[k * tile + i][...]
                cot[rows, :] = (c0, c1, c2, c3)[k * tile + i][...]

    cot_low[...] = cot[...].astype(bf16)
    for pair in range(pairs):
        cols = slice(pair * pair_width, (pair + 1) * pair_width)
        both = nt(phi[:, pair * 2 * features : (pair + 1) * 2 * features], matrix[pair])
        inverse = 1.0 / both[:, pair_width:]
        quotient = both[:, :pair_width] * inverse
        att_wide[:, cols] = quotient
        recip[:, cols] = inverse
        attention[:, cols] = quotient.astype(bf16)
    mid = hid[...] + nn(attention[...], w_out[...]) + b_out[...]
    result[...] = mid + b_low[...]
    scaled, inverse = norm_parts(mid)
    scaled_ref[...] = scaled
    normed[...] = (scaled * gain[...] + shift[...]).astype(bf16)
    back[...] = jnp.zeros_like(back)

    for at in range(w_up.shape[1] // chunk):
        cols = slice(at * chunk, (at + 1) * chunk)
        upper = nn(normed[...], w_up[:, cols]) + b_up[:, cols]
        grad_active = nt(cot_low[...], w_low[cols, :])
        cumulative, density = gelu_parts(upper)
        active[:, cols] = (upper * cumulative).astype(bf16)
        low = (grad_active * (cumulative + upper * density)).astype(bf16)
        d_upper[:, cols] = low
        up_sums[:, cols] += col_sum(low.astype(f32))
        back[...] += nt(low, w_up[:, cols])
        result[...] += nn(active[:, cols], w_low[cols, :])
    for k in range(plane // tile):

        @pl.when(step == k)
        def _():
            for i in range(tile):
                (g0, g1, g2, g3)[k * tile + i][...] = result[i * genes : (i + 1) * genes, :]

    grad_normed = back[...]
    scaled = scaled_ref[...]
    grad_mid = cot[...] + norm_back(grad_normed, scaled, inverse, gain[...])
    d_middle[...] = grad_mid
    branch = grad_mid.astype(bf16)
    d_branch[...] = branch
    sums[0:1, :] += col_sum(grad_normed * scaled)
    sums[1:2, :] += col_sum(grad_normed)
    sums[2:3, :] += col_sum(branch.astype(f32))
    sums[3:4, :] += col_sum(cot[...])
    back[...] = nt(branch, w_out[...])
    row = lax.broadcasted_iota(jnp.int32, (2 * pair_width, pair_width), 0) // head_size % 2
    col = lax.broadcasted_iota(jnp.int32, (2 * pair_width, pair_width), 1) // head_size
    ones = jnp.where(row == col, 1.0, 0.0).astype(bf16)
    for pair in range(pairs):
        cols = slice(pair * pair_width, (pair + 1) * pair_width)
        grad = back[:, cols]
        inverse = recip[:, cols]
        product = grad * att_wide[:, cols]
        high = product.astype(bf16)
        low = (product - high.astype(f32)).astype(bf16)
        total = nn(jnp.concatenate([high, low], axis=1), ones)
        at = pair * 2 * pair_width
        d_num[:, at : at + pair_width] = (grad * inverse).astype(bf16)
        d_num[:, at + pair_width : at + 2 * pair_width] = (
            total * inverse * (-1.0 / head_size)
        ).astype(bf16)
        acc[pair] += tn(
            d_num[:, at : at + 2 * pair_width],
            phi[:, pair * 2 * features : (pair + 1) * 2 * features],
        )

    @pl.when(step == plane // tile - 1)
    def _():
        rows_used = pairs * head_size + pairs
        spare = pay.shape[1] - rows_used
        if spare:
            for i in range(2):
                pay[i, rows_used:, :] = jnp.zeros((spare, features), f32)
        for pair in range(pairs):
            totals = [
                acc[pair, pair_width + i * head_size : pair_width + i * head_size + 1, :]
                * float(head_size)
                for i in range(2)
            ]
            put_summary(pay, pair, pairs, acc[pair], totals, head_size, features)
        mine_out[...] = pay[ids[3]]
        sent_out[...] = pay[1 - ids[3]]


def feed_call(
    ids, j, hidden, cots, phi, mine, other, w_out, b_out, gain, shift, w_up, b_up, w_low, b_low, heads, after=()
):
    genes, width = hidden[0].shape
    tokens = plane * genes
    step = tile * genes
    features = phi.shape[1] // heads
    wide = w_up.shape[1]
    pairs = heads // 2
    pay = payload_shape(heads, width // heads, features)

    def rows(cols):
        return pl.BlockSpec((step, cols), lambda at, ids: (at, 0))

    ins = list(hidden) + list(cots) + [phi, mine, other, w_out, b_out, gain, shift, w_up, b_up, w_low, b_low]
    in_specs = [whole(a.shape) for a in ins]
    in_specs[2 * plane] = rows(phi.shape[1])
    for r in range(plane):
        in_specs[plane + r] = pl.BlockSpec((None, genes, width), lambda at, ids: (j, 0, 0))
    outs = [(free((genes, width)), whole((genes, width)))] * plane + [
        (near((tokens, wide), bf16), rows(wide)),
        (near((tokens, wide), bf16), rows(wide)),
        (near((tokens, width), bf16), rows(width)),
        (near((tokens, width), bf16), rows(width)),
        (near((tokens, width)), rows(width)),
        (near((tokens, width), bf16), rows(width)),
        (near((tokens, 2 * width), bf16), rows(2 * width)),
        (near((tokens, width), bf16), rows(width)),
        (near(pay), whole(pay)),
        (free(pay), whole(pay)),
        (near((8, width)), whole((8, width))),
        (near((1, wide)), whole((1, wide))),
    ]
    return call(
        feed_kernel,
        "feed_forward",
        (plane // tile,),
        in_specs,
        [o[0] for o in outs],
        [o[1] for o in outs],
        [
            pltpu.VMEM((2, *pay), f32),
            pltpu.VMEM((pairs, 2 * width // pairs, 2 * features), bf16),
            pltpu.VMEM((pairs, 2 * width // pairs, 2 * features), f32),
        ]
        + [pltpu.VMEM((step, width), f32)] * 7,
        ids,
        *ins,
        after=after,
        mib=22,
    )


def feature_back(grad_feat, phi, u, back_matrix, factor):
    pair_width = u.shape[1]
    low = (grad_feat * phi.astype(f32) * factor).astype(bf16)
    both = nn(low, back_matrix[...])
    return both[:, :pair_width] - factor * u.astype(f32) * both[:, pair_width:]


def d_query_kernel(ids, d_num, phi, query, mine, other, back_matrix, weight, d_query, d_normed, sums, matrix, *, factor):
    step = pl.program_id(0)
    pairs = matrix.shape[0]
    features = phi.shape[1] // pairs // 2
    width = query.shape[1]
    pair_width = width // pairs

    @pl.when(step == 0)
    def _():
        block_matrix(matrix, mine, other, ids[3], pairs, pair_width // 2, features, True)
        sums[...] = jnp.zeros_like(sums)

    for pair in range(pairs):
        cols = slice(pair * pair_width, (pair + 1) * pair_width)
        grad_feat = nn(d_num[:, pair * 2 * pair_width : (pair + 1) * 2 * pair_width], matrix[pair])
        grad = feature_back(
            grad_feat,
            phi[:, pair * 2 * features : (pair + 1) * 2 * features],
            query[:, cols],
            back_matrix,
            factor,
        )
        d_query[:, cols] = grad.astype(bf16)
    low = d_query[...]
    d_normed[...] = nt(low, weight[...])
    sums[...] += col_sum(low.astype(f32))


def d_query_call(ids, d_num, phi, joint, mine, other, back_matrix, weight, factor, after=()):
    tokens = joint.shape[0]
    width = joint.shape[1] // 3
    pair_width = back_matrix.shape[1] // 2
    pairs = width // pair_width
    step = tokens // plane * tile
    features = back_matrix.shape[0] // 2

    def rows(cols):
        return pl.BlockSpec((step, cols), lambda at, ids: (at, 0))

    return call(
        functools.partial(d_query_kernel, factor=factor),
        "query_gradient",
        (plane // tile,),
        [
            rows(2 * width),
            rows(phi.shape[1]),
            rows(width),
            whole(mine.shape),
            whole(other.shape),
            whole(back_matrix.shape),
            whole((width, width)),
        ],
        [near((tokens, width), bf16), near((tokens, width)), near((1, width))],
        [rows(width), rows(width), whole((1, width))],
        [pltpu.VMEM((pairs, 2 * pair_width, 2 * features), bf16)],
        ids,
        d_num,
        phi,
        joint,
        mine,
        other,
        back_matrix,
        weight,
        after=after,
        mib=20,
    )


def d_key_kernel(
    ids, h0, h1, h2, h3, joint, phi, d_query, d_normed_q, d_middle, mine, other, back_matrix, weight, gain,
    g0, g1, g2, g3, d_joint, sums, key_sums, matrix, total_ref, hid, *, factor,
):
    step = pl.program_id(0)
    pairs = matrix.shape[0]
    genes, width = h0.shape
    features = phi.shape[1] // pairs // 2
    pair_width = width // pairs
    head_size = pair_width // 2

    @pl.when(step == 0)
    def _():
        block_matrix(matrix, mine, other, ids[3], pairs, head_size, features, False)
        base = pairs * head_size
        for pair in range(pairs):
            half = pair // (pairs // 2)
            at = base + (pair % (pairs // 2)) * 2
            first = (ids[3] ^ half) == 0
            for i in range(2):
                total_ref[pair : pair + 1, i * features : (i + 1) * features] = jnp.where(
                    first, mine[at + i : at + i + 1, :], other[at + i : at + i + 1, :]
                )
        sums[...] = jnp.zeros_like(sums)
        key_sums[...] = jnp.zeros_like(key_sums)

    for k in range(plane // tile):

        @pl.when(step == k)
        def _():
            for i in range(tile):
                hid[i * genes : (i + 1) * genes, :] = (h0, h1, h2, h3)[k * tile + i][...]

    d_joint[:, :width] = d_query[...]
    for pair in range(pairs):
        at = pair * pair_width
        value = joint[:, 2 * width + at : 2 * width + at + pair_width]
        low = phi[:, pair * 2 * features : (pair + 1) * 2 * features]
        grad_feat = nn(value, matrix[pair]) + total_ref[pair : pair + 1, :]
        grad = feature_back(
            grad_feat, low, joint[:, width + at : width + at + pair_width], back_matrix, factor
        )
        d_joint[:, width + at : width + at + pair_width] = grad.astype(bf16)
        d_joint[:, 2 * width + at : 2 * width + at + pair_width] = nt(low, matrix[pair]).astype(bf16)
    low = d_joint[:, width:]
    key_sums[...] += col_sum(low.astype(f32))
    grad_normed = d_normed_q[...] + nt(low, weight[:, width:])
    scaled, inverse = norm_parts(hid[...])
    result = (d_middle[...] + norm_back(grad_normed, scaled, inverse, gain[...])).astype(bf16)
    result = result.astype(f32)
    sums[0:1, :] += col_sum(grad_normed * scaled)
    sums[1:2, :] += col_sum(grad_normed)
    sums[2:3, :] += col_sum(result)
    for k in range(plane // tile):

        @pl.when(step == k)
        def _():
            for i in range(tile):
                (g0, g1, g2, g3)[k * tile + i][...] = result[i * genes : (i + 1) * genes, :]


def d_key_call(ids, hidden, joint, phi, d_query, d_normed_q, d_middle, mine, other, back_matrix, weight, gain, factor, after=()):
    genes, width = hidden[0].shape
    tokens = plane * genes
    step = tile * genes
    pair_width = back_matrix.shape[1] // 2
    pairs = width // pair_width
    features = back_matrix.shape[0] // 2

    def rows(cols):
        return pl.BlockSpec((step, cols), lambda at, ids: (at, 0))

    ins = list(hidden) + [joint, phi, d_query, d_normed_q, d_middle, mine, other, back_matrix, weight, gain]
    in_specs = [whole(a.shape) for a in ins]
    for i in range(5):
        in_specs[plane + i] = rows(ins[plane + i].shape[1])
    outs = [(free((genes, width)), whole((genes, width)))] * plane + [
        (near((tokens, 3 * width), bf16), rows(3 * width)),
        (near((8, width)), whole((8, width))),
        (near((1, 2 * width)), whole((1, 2 * width))),
    ]
    return call(
        functools.partial(d_key_kernel, factor=factor),
        "key_gradient",
        (plane // tile,),
        in_specs,
        [o[0] for o in outs],
        [o[1] for o in outs],
        [
            pltpu.VMEM((pairs, pair_width, 2 * features), bf16),
            pltpu.VMEM((8, 2 * features), f32),
            pltpu.VMEM((step, width), f32),
        ],
        ids,
        *ins,
        after=after,
        mib=28,
    )


def put_shards(out, size, spot, where, first, count, per, rows, at, value):
    if rows % 8:
        out[at * size + first * rows : at * size + (first + count) * rows, :] = value
        return
    for s in range(count):
        to = (where(first + s) ^ spot) * per + at
        to = pl.multiple_of(to, 8)
        out[pl.ds(to, rows), :] = value[s * rows : (s + 1) * rows, :]


def in_slots(bundle, size, me, per, rows, order):
    if rows % 8 == 0:
        return bundle
    body = bundle[: size * per].reshape(per // rows, size, rows, -1).transpose(1, 0, 2, 3)
    place = placed(order, size.bit_length() - 1)
    owner = sorted(range(size), key=place)
    body = body[jnp.array(owner, jnp.int32) ^ me].reshape(size * per, -1)
    return jnp.concatenate([body, bundle[size * per :]], axis=0)


def side_of(sent):
    return (lambda ids: 1 - ids[1]) if sent else (lambda ids: ids[1])


def lower_weights_kernel(ids, a0, a1, c0, c1, out, *, size, where, spot_at):
    step = pl.program_id(0)
    part = size // 4
    rows = out.shape[0] // size
    value = tn(a0[...], c0[...]) + tn(a1[...], c1[...])
    for k in range(4):

        @pl.when(step == k)
        def _():
            put_shards(out, size, ids[spot_at], where, k * part, part, rows, rows, 0, value)


def lower_weights_call(ids, size, sent, where, spot_at, active, cot_low, after=()):
    tokens, wide = active[0].shape
    half = cot_low[0].shape[1] // 2
    side = side_of(sent)
    shape = (wide, half)
    return call(
        functools.partial(lower_weights_kernel, size=size, where=where, spot_at=spot_at),
        "lower_weights",
        (4,),
        [pl.BlockSpec((tokens, wide // 4), lambda at, ids: (0, at))] * 2
        + [pl.BlockSpec((tokens, half), lambda at, ids: (0, side(ids)))] * 2,
        free(shape) if sent else near(shape),
        whole(shape),
        [],
        ids,
        *active,
        *cot_low,
        after=after,
        mib=16,
    )


def upper_weights_kernel(ids, n0, n1, u0, u1, t0, t1, b0, b1, out, *, size, where, spot_at):
    step = pl.program_id(0)
    part = size // 4
    rows = n0.shape[1] // size
    value = tn(n0[...], u0[...]) + tn(n1[...], u1[...])
    last = tn(t0[...], b0[...]) + tn(t1[...], b1[...])
    for k in range(4):

        @pl.when(step == k)
        def _():
            put_shards(out, size, ids[spot_at], where, 0, size, 5 * rows, rows, k * rows, value)
            put_shards(out, size, ids[spot_at], where, k * part, part, 5 * rows, rows, 4 * rows, last)


def upper_weights_call(ids, size, sent, where, spot_at, normed, d_upper, attention, d_branch, after=()):
    tokens, width = normed[0].shape
    half = width // 2
    side = side_of(sent)
    shape = (5 * width, half)
    return call(
        functools.partial(upper_weights_kernel, size=size, where=where, spot_at=spot_at),
        "upper_weights",
        (4,),
        [pl.BlockSpec((tokens, width), lambda at, ids: (0, 0))] * 2
        + [pl.BlockSpec((tokens, half), lambda at, ids: (0, side(ids) * 4 + at))] * 2
        + [pl.BlockSpec((tokens, width // 4), lambda at, ids: (0, at))] * 2
        + [pl.BlockSpec((tokens, half), lambda at, ids: (0, side(ids)))] * 2,
        free(shape) if sent else near(shape),
        whole(shape),
        [],
        ids,
        *normed,
        *d_upper,
        *attention,
        *d_branch,
        after=after,
        mib=16,
    )


def joint_weights_kernel(ids, n0, n1, j0, j1, out, *, size, where, spot_at):
    step = pl.program_id(0)
    rows = n0.shape[1] // size
    value = tn(n0[...], j0[...]) + tn(n1[...], j1[...])
    for k in range(3):

        @pl.when(step == k)
        def _():
            put_shards(out, size, ids[spot_at], where, 0, size, 3 * rows, rows, k * rows, value)


def joint_weights_call(ids, size, sent, where, spot_at, normed, d_joint, after=()):
    tokens, width = normed[0].shape
    half = width // 2
    side = side_of(sent)
    shape = (3 * width, half)
    return call(
        functools.partial(joint_weights_kernel, size=size, where=where, spot_at=spot_at),
        "joint_weights",
        (3,),
        [pl.BlockSpec((tokens, width), lambda at, ids: (0, 0))] * 2
        + [pl.BlockSpec((tokens, half), lambda at, ids: (0, side(ids) * 3 + at))] * 2,
        free(shape) if sent else near(shape),
        whole(shape),
        [],
        ids,
        *normed,
        *d_joint,
        after=after,
        mib=14,
    )


vector_rows = 32


def input_weights_kernel(ids, *refs, size, where, spot_at):
    pieces = refs[:8]
    r0, r1, v0, v1, f0, f1, u0, u1, k0, k1, q0, q1, s0, s1, d_low, sent, kept, zero_hidden = refs[8:]
    genes, width = pieces[0].shape
    half = width // 2
    rows = (sent.shape[0] - vector_rows) // size
    total = None
    for i, piece in enumerate(pieces):
        wide = piece[...]
        d_low[i * genes : (i + 1) * genes, :] = wide.astype(bf16)
        masked = wide * (v0, v1)[i % 2][i // 2][:, :1]
        total = masked if total is None else total + masked
    zero_hidden[...] = total
    parts = [f0[0:4, :] + f1[0:4, :], s0[0:3, :] + s1[0:3, :], q0[...] + q1[...], k0[...] + k1[...], u0[...] + u1[...]]
    for out, side in ((sent, 1 - ids[1]), (kept, ids[1])):
        value = None
        for i in range(8):
            chosen = (r0, r1)[i % 2][i // 2]
            lo = d_low[i * genes : (i + 1) * genes, :half]
            hi = d_low[i * genes : (i + 1) * genes, half:]
            product = tn(chosen, jnp.where(side == 0, lo, hi))
            value = product if value is None else value + product
        put_shards(out, size, ids[spot_at], where, 0, size, rows, rows, 0, value)
        at = size * rows
        for part in parts:
            for row in range(part.shape[0]):
                for c in range(part.shape[1] // half):
                    out[at : at + 1, :] = part[row : row + 1, c * half : (c + 1) * half]
                    at += 1
        out[at:, :] = jnp.zeros((out.shape[0] - at, half), f32)


def input_weights_call(ids, size, where, spot_at, pieces, rows, vacant, sums, after=()):
    genes, width = pieces[0].shape
    width_in = rows[0].shape[2]
    ins = list(pieces) + list(rows) + list(vacant) + list(sums)
    shape = (width_in + vector_rows, width // 2)
    outs = [near((8 * genes, width), bf16), free(shape), near(shape), free((genes, width))]
    return call(
        functools.partial(input_weights_kernel, size=size, where=where, spot_at=spot_at),
        "input_weights",
        (1,),
        [whole(a.shape) for a in ins],
        outs,
        [whole(o.shape) for o in outs],
        [],
        ids,
        *ins,
        after=after,
        mib=28,
    )


def out_kernel(ids, *refs):
    out = refs[-1]
    for i, piece in enumerate(refs[:-1]):
        out[i ^ (2 * ids[2])] = piece[...].astype(bf16)


def out_call(ids, pieces, after=()):
    genes, width = pieces[0].shape
    shape = (len(pieces), genes, width)
    return call(
        out_kernel,
        "block_out",
        (1,),
        [whole(p.shape) for p in pieces],
        far(shape, bf16),
        whole(shape),
        [],
        ids,
        *pieces,
        after=after,
        mib=14,
    )


def token_kernel(ids, d_low, index, weight, token_grad):
    slots, _ = index.shape
    width = d_low.shape[1]
    genes = d_low.shape[0] // 8
    slot = lax.broadcasted_iota(jnp.int32, (slots, 1), 0)
    picked = jnp.zeros((slots, width), f32)
    gene = lax.broadcasted_iota(jnp.int32, (slots, genes), 1)
    match = (index[...] - ids[0] * genes) == gene
    for i in range(8):
        cell = i ^ (2 * ids[2])
        here = (slot >= ids[8 + cell]) & (slot < ids[9 + cell])
        chosen = jnp.where(match & here, 1.0, 0.0).astype(bf16)
        picked = picked + nn(chosen, d_low[i * genes : (i + 1) * genes, :])
    token_grad[0] = nt(picked.astype(bf16), weight[...])


def token_call(ids, d_low, index, weight, after=()):
    ins = [d_low, index, weight]
    shape = (1, index.shape[0], weight.shape[0])
    return call(
        token_kernel,
        "token_gradient",
        (1,),
        [whole(a.shape) for a in ins],
        far(shape),
        whole(shape),
        [],
        ids,
        *ins,
        after=after,
        mib=24,
    )


def zero_kernel(ids, mine, other, weight, out):
    total = mine[...] + other[...]
    high = total.astype(bf16)
    rest = total - high.astype(f32)
    low = rest.astype(bf16)
    out[...] = nt(high, weight[...]) + nt(low, weight[...])


def zero_call(ids, mine, other, weight, after=()):
    genes, width = mine.shape
    ins = [mine, other, weight]
    shape = (genes, weight.shape[0])
    return call(
        zero_kernel,
        "zero_gradient",
        (1,),
        [whole(a.shape) for a in ins],
        far(shape),
        whole(shape),
        [],
        ids,
        *ins,
        after=after,
        mib=12,
    )


def local(
    encoder_packed_tokens,
    token_gene_index,
    cell_counts,
    zero_embed,
    random_features,
    input_weight,
    input_bias,
    first_gain,
    first_shift,
    joint_weight,
    joint_bias,
    output_weight,
    output_bias,
    second_gain,
    second_shift,
    upper_weight,
    upper_bias,
    lower_weight,
    lower_bias,
    cotangent,
):
    placed_at.clear()
    size = lax.axis_size("gene")
    me = lax.axis_index("gene")
    core = lax.axis_index("cell")
    cells_here, genes, width = cotangent.shape
    head_size, features = random_features.shape
    heads = width // head_size
    factor = head_size ** (-0.25)
    group = cells_here // plane
    log = size.bit_length() - 1
    rest = list(range(3, log))
    orders = ([0, 1, 2] + rest, [2, 1, 0] + rest, [1, 0, 2] + rest)
    where = [placed(order, log) for order in orders]
    ends = jnp.cumsum(cell_counts[0]).astype(jnp.int32)
    ids = jnp.concatenate(
        [
            jnp.stack([me, core, me % plane, (me // plane) % 2, me * 0]).astype(jnp.int32),
            jnp.stack([placed(order, log)(me) for order in orders]).astype(jnp.int32),
            jnp.zeros((1,), jnp.int32),
            ends,
        ]
    )
    nothing = jnp.zeros((head_size, features), bf16)
    minus = jnp.full((head_size, features), -1.0, bf16)
    feats = jnp.concatenate(
        [
            jnp.concatenate([random_features, nothing], axis=1),
            jnp.concatenate([nothing, random_features], axis=1),
            jnp.concatenate([minus, nothing], axis=1),
            jnp.concatenate([nothing, minus], axis=1),
        ],
        axis=0,
    )
    back_matrix = jnp.concatenate([feats[: 2 * head_size].T, -feats[2 * head_size :].T], axis=1)

    def row(vector):
        return vector.reshape(1, -1)

    high = [1 << b for b in range(2, log)]
    last = ()

    def then(made, token, *more):
        nonlocal last
        last = (token, *more)
        return made

    def gene_swap(value, bit):
        return swap(value, "gene", size, bit)

    def out_and_in(blocks):
        return [block if r == 0 else gene_swap(block, r) for r, block in enumerate(blocks)]

    class Halves:
        def __init__(self, mine, sent):
            self.mine = mine
            self.came = gene_swap(sent, high[0])
            self.left = high[1:]

        def add(self):
            self.mine = add_call(ids, self.mine, self.came, after=last)
            then(None, self.mine)
            if self.left:
                self.came = gene_swap(self.mine, self.left.pop(0))
            else:
                self.other = gene_swap(self.mine, high[0])

        def finish(self):
            while not hasattr(self, "other"):
                self.add()
            return self.mine, self.other

    class Scatter:
        def __init__(self, sent, kept, order, rows, extra=0):
            per = (kept.shape[0] - extra) // size
            self.mine = in_slots(kept, size, me, per, rows, order)
            self.came = swap(in_slots(sent, size, me, per, rows, order), "cell", 2, 1)
            self.order = list(order)
            self.extra = extra

        def add(self):
            if self.order:
                self.mine, send = split_call(ids, self.mine, self.came, self.extra, after=last)
                then(None, self.mine)
                self.came = gene_swap(send, 1 << self.order.pop(0))
            else:
                self.mine = add_call(ids, self.mine, self.came, after=last)
                then(None, self.mine)
                self.done = True

        def finish(self):
            while not hasattr(self, "done"):
                self.add()
            return self.mine

    shard = width // size
    wide_shard = upper_weight.shape[1] // size
    in_shard = input_weight.shape[0] // size
    hidden, rows, vacant = [], [], []
    for j in range(group):
        made = rows_call(
            ids, j, group, encoder_packed_tokens[0], token_gene_index, zero_embed, input_weight, row(input_bias),
            after=last,
        )
        hidden.append(out_and_in(made[:plane]))
        rows.append(made[plane])
        vacant.append(made[plane + 1])
        then(None, made[plane + 1])
    normed, joint, key_phi, sums = [], [], [], []

    def keys_of(j):
        made = key_call(
            ids, hidden[j], joint_weight, row(joint_bias), row(first_gain), row(first_shift), feats, factor,
            after=last,
        )
        normed.append(made[0])
        joint.append(made[1])
        key_phi.append(made[2])
        sums.append(Halves(made[3], made[4]))
        then(None, made[0])

    keys_of(0)
    w_up, w_low, w_out, w_joint = hold_call(
        ids, upper_weight, lower_weight, output_weight, joint_weight, after=last
    )
    then(None, w_out)
    sums[0].add()
    keys_of(1)
    wide = cotangent_call(ids, group, cotangent, after=last)
    then(None, wide[0])
    cots = out_and_in(wide)
    query_phi = []

    def query_of(j):
        query_phi.append(query_call(ids, joint[j], feats, factor, after=last))
        then(None, query_phi[j])

    query_of(0)
    sums[1].add()
    sums[0].finish()
    query_of(1)
    sums[1].finish()
    sums = [s.finish() for s in sums]
    fed, d_sums = [], []
    for j in range(group):
        made = feed_call(
            ids, j, hidden[j], cots, query_phi[j], *sums[j], w_out, row(output_bias), row(second_gain),
            row(second_shift), w_up, row(upper_bias), w_low, row(lower_bias), heads,
            after=last,
        )
        fed.append(made)
        d_sums.append(Halves(made[plane + 8], made[plane + 9]))
        then(None, made[plane + 2])
    active, d_upper, normed_two, attention, d_middle, d_branch, d_num, cot_low, _, _, sums_two, up_sums = list(
        zip(*fed)
    )[plane:]
    back_out = [out_and_in(made[:plane]) for made in fed]
    last = (*last, *back_out[0][1:])
    d_sums[0].add()
    queries = []

    def d_query_of(j):
        queries.append(
            d_query_call(
                ids, d_num[j], query_phi[j], joint[j], *sums[j], back_matrix, w_joint, factor, after=last
            )
        )
        then(None, queries[j][1])

    d_query_of(0)
    d_sums[1].add()
    d_query_of(1)
    d_sums[0].finish()

    def lower_of(sent):
        made = lower_weights_call(ids, size, sent, where[0], 5, active, cot_low, after=last)
        return then(made, made)

    def upper_of(sent):
        made = upper_weights_call(
            ids, size, sent, where[1], 6, normed_two, d_upper, attention, d_branch, after=last
        )
        return then(made, made)

    lower_sent = lower_of(True)
    last = (*last, *back_out[1][1:])
    d_sums[1].finish()
    lower_sum = Scatter(lower_sent, lower_of(False), orders[0], wide_shard)
    keys, backs = [], []

    def d_key_of(j):
        made = d_key_call(
            ids, hidden[j], joint[j], key_phi[j], queries[j][0], queries[j][1], d_middle[j], *d_sums[j].finish(),
            back_matrix, w_joint, row(first_gain), factor,
            after=last,
        )
        keys.append(made)
        backs.append(out_and_in(made[:plane]))
        then(None, made[plane])

    d_key_of(0)
    lower_sum.add()
    d_key_of(1)
    upper_sent = upper_of(True)
    last = (*last, *backs[0][1:])
    upper_sum = Scatter(upper_sent, upper_of(False), orders[1], shard)
    lower_sum.add()
    d_joint = [k[plane] for k in keys]

    def joint_of(sent):
        made = joint_weights_call(ids, size, sent, where[2], 7, normed, d_joint, after=last)
        return then(made, made)

    upper_sum.add()
    joint_sent = joint_of(True)
    joint_sum = Scatter(joint_sent, joint_of(False), orders[2], shard)
    lower_sum.add()
    block_out = out_call(
        ids, [back_out[j][r] for r in range(plane) for j in range(group)], after=last
    )
    then(None, block_out)
    joint_sum.add()
    upper_sum.add()
    sums_one = [k[plane + 1] for k in keys]
    key_sums = [k[plane + 2] for k in keys]
    query_sums = [q[2] for q in queries]
    d_low, input_sent, input_kept, zero_hidden = input_weights_call(
        ids, size, where[0], 5, [backs[j][r] for r in range(plane) for j in range(group)], rows, vacant,
        [*sums_two, *up_sums, *key_sums, *query_sums, *sums_one],
        after=last,
    )
    then(None, zero_hidden)
    input_sum = Scatter(input_sent, input_kept, orders[0], in_shard, vector_rows)
    zero_came = swap(zero_hidden, "cell", 2, 1)
    token_grad = token_call(ids, d_low, token_gene_index.reshape(-1, 1), input_weight, after=last)
    then(None, token_grad)
    input_sum.add()
    joint_sum.add()
    zero_grad = zero_call(ids, zero_hidden, zero_came, input_weight, after=last)
    then(None, zero_grad)
    lower_sum.add()
    input_sum.add()
    upper_sum.add()
    joint_sum.add()
    lower_sum.finish()
    input_sum.add()
    upper_sum.finish()
    joint_sum.finish()
    input_sum.finish()

    def both_halves(mine):
        other = swap(mine, "cell", 2, 1)
        return jnp.where(core == 0, mine, other), jnp.where(core == 0, other, mine)

    def opened(pair, at, count, groups):
        parts = [b[at + g * count : at + (g + 1) * count] for b in pair for g in range(groups)]
        return jnp.concatenate(parts, axis=1)

    lower_pair = both_halves(lower_sum.mine)
    upper_pair = both_halves(upper_sum.mine)
    g_lower = opened(lower_pair, 0, wide_shard, 1)
    g_upper = opened(upper_pair, 0, shard, 4)
    g_output = opened(upper_pair, 4 * shard, shard, 1)
    g_joint = opened(both_halves(joint_sum.mine), 0, shard, 3)
    g_input = opened(both_halves(input_sum.mine[:in_shard]), 0, in_shard, 1)
    flat = input_sum.mine[in_shard:].reshape(-1)
    lengths = [width] * 7 + [3 * width, upper_weight.shape[1]]
    found = []
    at = 0
    for length in lengths:
        part = length // size
        found.append(lax.dynamic_slice(flat, (at + me * part,), (part,)))
        at += length
    small_out = [found[i] for i in (6, 4, 5, 7, 2, 0, 1, 8, 3)]
    return (
        block_out,
        token_grad,
        zero_grad,
        g_input,
        small_out[0],
        small_out[1],
        small_out[2],
        g_joint,
        small_out[3],
        g_output,
        small_out[4],
        small_out[5],
        small_out[6],
        g_upper,
        small_out[7],
        g_lower,
        small_out[8],
    )


def solution(mesh):
    return jax.shard_map(
        local,
        mesh=mesh,
        in_specs=(
            P("cell", "gene", None),
            P("cell", "gene"),
            P("cell", "gene"),
            P("gene", None),
            P(),
            P(),
            P(),
            P(),
            P(),
            P(),
            P(),
            P(),
            P(),
            P(),
            P(),
            P(),
            P(),
            P(),
            P(),
            P("cell", "gene", None),
        ),
        out_specs=(
            P("cell", "gene", None),
            P("cell", "gene", None),
            P("gene", None),
            P("gene", None),
            P("gene"),
            P("gene"),
            P("gene"),
            P("gene", None),
            P("gene"),
            P("gene", None),
            P("gene"),
            P("gene"),
            P("gene"),
            P("gene", None),
            P("gene"),
            P("gene", None),
            P("gene"),
        ),
        check_vma=False,
    )
```

```python
import functools
import math

import jax
import jax.numpy as jnp
from jax import lax
from jax.experimental import pallas as pl
from jax.experimental.pallas import tpu as pltpu
from jax.sharding import PartitionSpec as P

epsilon = 1e-05
f32 = jnp.float32
bf16 = jnp.bfloat16
plane = 4
tile = 2


def nn(left, right):
    return jnp.dot(left, right, preferred_element_type=f32)


def nt(left, right):
    return lax.dot_general(left, right, (((1,), (1,)), ((), ())), preferred_element_type=f32)


def tn(left, right):
    return lax.dot_general(left, right, (((0,), (0,)), ((), ())), preferred_element_type=f32)


def col_sum(values):
    return jnp.sum(values, axis=0, keepdims=True)


def norm_parts(values):
    centred = values - jnp.mean(values, axis=-1, keepdims=True)
    inverse = lax.rsqrt(jnp.mean(centred * centred, axis=-1, keepdims=True) + epsilon)
    return centred * inverse, inverse


def norm_back(grad_in, scaled, inverse, gain):
    weighted = grad_in * gain
    return inverse * (
        weighted
        - jnp.mean(weighted, axis=-1, keepdims=True)
        - scaled * jnp.mean(weighted * scaled, axis=-1, keepdims=True)
    )


def whole(shape):
    return pl.BlockSpec(shape, lambda *at: (0,) * len(shape))


placed_at = []


def near(shape, dtype=f32):
    return pltpu.VMEM(shape, dtype)


def far(shape, dtype=f32):
    return pltpu.HBM(shape, dtype)


def free(shape, dtype=f32):
    return jax.ShapeDtypeStruct(shape, dtype)


def placed(order, log):
    return lambda number: sum(((number >> bit) & 1) << (log - 1 - i) for i, bit in enumerate(order))


def call(kernel, name, grid, in_specs, outs, out_specs, scratch, *args, after=(), mib=60):
    first = 1 + len(in_specs)

    def body(*refs):
        kernel(*refs[:first], *refs[first + len(after) :])

    def held(array):
        for other, space in placed_at:
            if array is other:
                return pltpu.with_memory_space_constraint(array, space)
        return array

    made = pl.pallas_call(
        body,
        name=name,
        grid_spec=pltpu.PrefetchScalarGridSpec(
            num_scalar_prefetch=1,
            grid=grid,
            in_specs=list(in_specs) + [pl.BlockSpec(memory_space=pl.ANY)] * len(after),
            out_specs=out_specs,
            scratch_shapes=scratch,
        ),
        out_shape=outs,
        compiler_params=pltpu.CompilerParams(
            vmem_limit_bytes=mib << 20, dimension_semantics=("arbitrary",) * len(grid)
        ),
        cost_estimate=pl.CostEstimate(flops=1000, bytes_accessed=1000, transcendentals=0),
    )(args[0], *(held(a) for a in args[1:]), *(held(a) for a in after))
    several = isinstance(outs, (list, tuple))
    for out, array in zip(outs if several else [outs], made if several else [made]):
        if getattr(out, "memory_space", None) in (pltpu.VMEM, pltpu.HBM):
            placed_at.append((array, out.memory_space))
    return made


def swap(value, axis, size, bit):
    return lax.ppermute(value, axis, [(i, i ^ bit) for i in range(size)])


def rows_kernel(ids, tokens, index, zero, weight, bias, h0, h1, h2, h3, rows_out, vacant_out, *, group, j):
    genes = zero.shape[0]
    first_gene = ids[0] * genes
    slots = index.shape[1]
    slot = lax.broadcasted_iota(jnp.int32, (genes, slots), 1)
    gene = lax.broadcasted_iota(jnp.int32, (genes, slots), 0)
    match = (index[...] - first_gene) == gene
    for r in (3, 1, 2, 0):
        cell = (ids[2] ^ r) * group + j
        here = match & (slot >= ids[8 + cell]) & (slot < ids[9 + cell])
        chosen = jnp.where(here, 1.0, 0.0)
        vacant = 1.0 - jnp.sum(chosen, axis=1, keepdims=True)
        rows = nn(chosen.astype(bf16), tokens[...]) + vacant * zero[...].astype(f32)
        rows = rows.astype(bf16)
        rows_out[r] = rows
        vacant_out[r] = jnp.broadcast_to(vacant, (genes, 128))
        (h0, h1, h2, h3)[r][...] = nn(rows, weight[...]) + bias[...]


def rows_call(ids, j, group, tokens, index, zero, weight, bias, after=()):
    genes, width_in = zero.shape
    width = weight.shape[1]
    outs = [free((genes, width))] * plane + [
        far((plane, genes, width_in), bf16),
        far((plane, genes, 128)),
    ]
    ins = [tokens, index, zero, weight, bias]
    return call(
        functools.partial(rows_kernel, group=group, j=j),
        "gene_rows",
        (1,),
        [whole(a.shape) for a in ins],
        outs,
        [whole(o.shape) for o in outs],
        [],
        ids,
        *ins,
        after=after,
        mib=20,
    )


def cotangent_kernel(ids, cot, c0, c1, c2, c3):
    for r, out in enumerate((c0, c1, c2, c3)):
        for j in range(out.shape[0]):
            out[j] = cot[(ids[2] ^ r) * out.shape[0] + j].astype(f32)


def cotangent_call(ids, group, cot, after=()):
    _, genes, width = cot.shape
    outs = [free((group, genes, width))] * plane
    return call(
        cotangent_kernel,
        "wide_cotangent",
        (1,),
        [whole(cot.shape)],
        outs,
        [whole(o.shape) for o in outs],
        [],
        ids,
        cot,
        after=after,
        mib=14,
    )


def pass_kernel(ids, *refs):
    count = len(refs) // 2
    for given, out in zip(refs[:count], refs[count:]):
        out[...] = given[...]


def pass_call(ids, *arrays, after=()):
    return call(
        pass_kernel,
        "pass_on",
        (1,),
        [whole(a.shape) for a in arrays],
        [free(a.shape, a.dtype) for a in arrays],
        [whole(a.shape) for a in arrays],
        [],
        ids,
        *arrays,
        after=after,
        mib=16,
    )


def release_kernel(ids, *refs):
    outs = refs[-(plane - 1) :]
    for i, piece in enumerate(refs[: -(plane - 1)]):
        outs[i % (plane - 1)][i // (plane - 1)] = piece[...]


def release_call(ids, pieces, after=()):
    genes, width = pieces[0].shape
    outs = [free((len(pieces) // (plane - 1), genes, width))] * (plane - 1)
    return call(
        release_kernel,
        "release",
        (1,),
        [whole(p.shape) for p in pieces],
        outs,
        [whole(o.shape) for o in outs],
        [],
        ids,
        *pieces,
        after=after,
        mib=14,
    )


def hold_kernel(ids, *refs):
    count = len(refs) // 2
    for given, held in zip(refs[:count], refs[count:]):
        held[...] = given[...]


def hold_call(ids, *arrays, after=()):
    outs = [near(a.shape, a.dtype) for a in arrays]
    return call(
        hold_kernel,
        "hold",
        (1,),
        [whole(a.shape) for a in arrays],
        outs,
        [whole(a.shape) for a in arrays],
        [],
        ids,
        *arrays,
        after=after,
        mib=12,
    )


def add_kernel(ids, mine, came, out):
    out[...] = mine[...] + came[...]


def add_call(ids, mine, came, out=free, after=()):
    return call(
        add_kernel,
        "add",
        (1,),
        [whole(mine.shape)] * 2,
        out(mine.shape),
        whole(mine.shape),
        [],
        ids,
        mine,
        came,
        after=after,
        mib=8,
    )


def split_kernel(ids, mine, came, keep, send, *, extra):
    half = keep.shape[0] - extra
    keep[:half, :] = mine[:half, :] + came[:half, :]
    send[:half, :] = mine[half : 2 * half, :] + came[half : 2 * half, :]
    if extra:
        both = mine[2 * half :, :] + came[2 * half :, :]
        keep[half:, :] = both
        send[half:, :] = both


def split_call(ids, mine, came, extra=0, after=()):
    rows, cols = mine.shape
    shape = ((rows - extra) // 2 + extra, cols)
    return call(
        functools.partial(split_kernel, extra=extra),
        "add_halves",
        (1,),
        [whole(mine.shape)] * 2,
        [near(shape), free(shape)],
        [whole(shape)] * 2,
        [],
        ids,
        mine,
        came,
        after=after,
        mib=16,
    )


def phi_of(u, feature_matrix, factor):
    features = feature_matrix.shape[1] // 2
    wide = u.astype(f32)
    square = (wide * wide * (0.5 * factor)).astype(bf16)
    power = nn(jnp.concatenate([u, square], axis=1), feature_matrix[...])
    scale = factor * math.log2(math.e)
    return jnp.exp2(power * scale - 0.5 * math.log2(features)).astype(bf16)


def put_summary(out, pair, pairs, both, totals, head_size, features):
    half = pair // (pairs // 2)
    at = (pair % (pairs // 2)) * 2
    base = pairs * head_size
    for i in range(2):
        cols = slice(i * features, (i + 1) * features)
        out[half, (at + i) * head_size : (at + i + 1) * head_size, :] = both[
            i * head_size : (i + 1) * head_size, cols
        ]
        out[half, base + at + i : base + at + i + 1, :] = totals[i][:, cols]


def block_matrix(matrix, mine, other, flip, pairs, head_size, features, with_totals):
    base = pairs * head_size
    for pair in range(pairs):
        half = pair // (pairs // 2)
        at = (pair % (pairs // 2)) * 2
        first = (flip ^ half) == 0

        def take(lo, hi):
            return jnp.where(first, mine[lo:hi, :], other[lo:hi, :])

        nothing = jnp.zeros((head_size, features), bf16)
        for i in range(2):
            rows = slice(i * head_size, (i + 1) * head_size)
            part = take((at + i) * head_size, (at + i + 1) * head_size).astype(bf16)
            matrix[pair, rows, i * features : (i + 1) * features] = part
            matrix[pair, rows, (1 - i) * features : (2 - i) * features] = nothing
            if with_totals:
                rows = slice((2 + i) * head_size, (3 + i) * head_size)
                total = take(base + at + i, base + at + i + 1)
                spread = jnp.broadcast_to(total, (head_size, features)).astype(bf16)
                matrix[pair, rows, i * features : (i + 1) * features] = spread
                matrix[pair, rows, (1 - i) * features : (2 - i) * features] = nothing


def payload_shape(heads, head_size, features):
    rows = heads // 2 * head_size + heads // 2
    return (rows + (-rows) % 8, features)


def key_kernel(
    ids, h0, h1, h2, h3, weight, bias, gain, shift, feats, normed, joint, phi, mine, sent, out, *, factor
):
    genes, width = h0.shape
    features = feats.shape[1] // 2
    pair_width = feats.shape[0] // 2
    pairs = width // pair_width
    for r, block in enumerate((h0, h1, h2, h3)):
        scaled, _ = norm_parts(block[...])
        normed[r * genes : (r + 1) * genes, :] = (scaled * gain[...] + shift[...]).astype(bf16)
    for part in (1, 2, 0):
        cols = slice(part * width, (part + 1) * width)
        joint[:, cols] = (nn(normed[...], weight[:, cols]) + bias[:, cols]).astype(bf16)
    rows_used = pairs * (pair_width // 2) + pairs
    spare = out.shape[1] - rows_used
    if spare:
        for i in range(2):
            out[i, rows_used:, :] = jnp.zeros((spare, features), f32)
    for pair in range(pairs):
        at = width + pair * pair_width
        low = phi_of(joint[:, at : at + pair_width], feats, factor)
        phi[:, pair * 2 * features : (pair + 1) * 2 * features] = low
        value = joint[:, width + at : width + at + pair_width]
        total = col_sum(low.astype(f32))
        put_summary(out, pair, pairs, tn(value, low), (total, total), pair_width // 2, features)
    mine[...] = out[ids[3]]
    sent[...] = out[1 - ids[3]]


def key_call(ids, hidden, weight, bias, gain, shift, feats, factor, after=()):
    genes, width = hidden[0].shape
    tokens = plane * genes
    features = feats.shape[1] // 2
    heads = 2 * width // (feats.shape[0] // 2)
    pay = payload_shape(heads, width // heads, features)
    outs = [
        far((tokens, width), bf16),
        near((tokens, 3 * width), bf16),
        far((tokens, heads * features), bf16),
        near(pay),
        free(pay),
    ]
    ins = list(hidden) + [weight, bias, gain, shift, feats]
    return call(
        functools.partial(key_kernel, factor=factor),
        "key_summary",
        (1,),
        [whole(a.shape) for a in ins],
        outs,
        [whole(o.shape) for o in outs],
        [pltpu.VMEM((2, *pay), f32)],
        ids,
        *ins,
        after=after,
        mib=24,
    )


def query_kernel(ids, joint, feats, phi, *, factor):
    features = feats.shape[1] // 2
    pair_width = feats.shape[0] // 2
    for pair in range(joint.shape[1] // pair_width):
        u = joint[:, pair * pair_width : (pair + 1) * pair_width]
        phi[:, pair * 2 * features : (pair + 1) * 2 * features] = phi_of(u, feats, factor)


def query_call(ids, joint, feats, factor, after=()):
    tokens, wide = joint.shape
    width = wide // 3
    features = feats.shape[1] // 2
    heads = 2 * width // (feats.shape[0] // 2)
    step = tokens // tile
    return call(
        functools.partial(query_kernel, factor=factor),
        "query_features",
        (tile,),
        [pl.BlockSpec((step, width), lambda at, ids: (at, 0)), whole(feats.shape)],
        near((tokens, heads * features), bf16),
        pl.BlockSpec((step, heads * features), lambda at, ids: (at, 0)),
        [],
        ids,
        joint,
        feats,
        after=after,
        mib=16,
    )


def gelu_parts(x):
    expo = jnp.exp2(x * x * (-0.5 * math.log2(math.e)))
    t = 1.0 / (1.0 + (0.3275911 * math.sqrt(0.5)) * jnp.abs(x))
    poly = t * (
        0.5 * 0.254829592
        + t
        * (
            0.5 * -0.284496736
            + t * (0.5 * 1.421413741 + t * (0.5 * -1.453152027 + t * (0.5 * 1.061405429)))
        )
    )
    tail = poly * expo
    return jnp.where(x > 0, 1.0 - tail, tail), expo * 0.3989422804014327


def feed_kernel(
    ids, h0, h1, h2, h3, c0, c1, c2, c3, phi, mine, other, w_out, b_out, gain, shift, w_up, b_up, w_low, b_low,
    g0, g1, g2, g3, active, d_upper, normed, attention, d_middle, d_branch, d_num, cot_low, mine_out, sent_out, sums, up_sums,
    pay, matrix, acc, hid, cot, att_wide, recip, scaled_ref, back, result,
):
    step = pl.program_id(0)
    genes, width = h0.shape
    features = phi.shape[1] // matrix.shape[0] // 2
    pairs = matrix.shape[0]
    pair_width = width // pairs
    head_size = pair_width // 2
    chunk = 512

    @pl.when(step == 0)
    def _():
        block_matrix(matrix, mine, other, ids[3], pairs, head_size, features, True)
        acc[...] = jnp.zeros_like(acc)
        sums[...] = jnp.zeros_like(sums)
        up_sums[...] = jnp.zeros_like(up_sums)

    for k in range(plane // tile):

        @pl.when(step == k)
        def _():
            for i in range(tile):
                rows = slice(i * genes, (i + 1) * genes)
                hid[rows, :] = (h0, h1, h2, h3)[k * tile + i][...]
                cot[rows, :] = (c0, c1, c2, c3)[k * tile + i][...]

    cot_low[...] = cot[...].astype(bf16)
    for pair in range(pairs):
        cols = slice(pair * pair_width, (pair + 1) * pair_width)
        both = nt(phi[:, pair * 2 * features : (pair + 1) * 2 * features], matrix[pair])
        inverse = 1.0 / both[:, pair_width:]
        quotient = both[:, :pair_width] * inverse
        att_wide[:, cols] = quotient
        recip[:, cols] = inverse
        attention[:, cols] = quotient.astype(bf16)
    mid = hid[...] + nn(attention[...], w_out[...]) + b_out[...]
    result[...] = mid + b_low[...]
    scaled, inverse = norm_parts(mid)
    scaled_ref[...] = scaled
    normed[...] = (scaled * gain[...] + shift[...]).astype(bf16)
    back[...] = jnp.zeros_like(back)

    for at in range(w_up.shape[1] // chunk):
        cols = slice(at * chunk, (at + 1) * chunk)
        upper = nn(normed[...], w_up[:, cols]) + b_up[:, cols]
        grad_active = nt(cot_low[...], w_low[cols, :])
        cumulative, density = gelu_parts(upper)
        active[:, cols] = (upper * cumulative).astype(bf16)
        low = (grad_active * (cumulative + upper * density)).astype(bf16)
        d_upper[:, cols] = low
        up_sums[:, cols] += col_sum(low.astype(f32))
        back[...] += nt(low, w_up[:, cols])
        result[...] += nn(active[:, cols], w_low[cols, :])
    for k in range(plane // tile):

        @pl.when(step == k)
        def _():
            for i in range(tile):
                (g0, g1, g2, g3)[k * tile + i][...] = result[i * genes : (i + 1) * genes, :]

    grad_normed = back[...]
    scaled = scaled_ref[...]
    grad_mid = cot[...] + norm_back(grad_normed, scaled, inverse, gain[...])
    d_middle[...] = grad_mid
    branch = grad_mid.astype(bf16)
    d_branch[...] = branch
    sums[0:1, :] += col_sum(grad_normed * scaled)
    sums[1:2, :] += col_sum(grad_normed)
    sums[2:3, :] += col_sum(branch.astype(f32))
    sums[3:4, :] += col_sum(cot[...])
    back[...] = nt(branch, w_out[...])
    row = lax.broadcasted_iota(jnp.int32, (2 * pair_width, pair_width), 0) // head_size % 2
    col = lax.broadcasted_iota(jnp.int32, (2 * pair_width, pair_width), 1) // head_size
    ones = jnp.where(row == col, 1.0, 0.0).astype(bf16)
    for pair in range(pairs):
        cols = slice(pair * pair_width, (pair + 1) * pair_width)
        grad = back[:, cols]
        inverse = recip[:, cols]
        product = grad * att_wide[:, cols]
        high = product.astype(bf16)
        low = (product - high.astype(f32)).astype(bf16)
        total = nn(jnp.concatenate([high, low], axis=1), ones)
        at = pair * 2 * pair_width
        d_num[:, at : at + pair_width] = (grad * inverse).astype(bf16)
        d_num[:, at + pair_width : at + 2 * pair_width] = (
            total * inverse * (-1.0 / head_size)
        ).astype(bf16)
        acc[pair] += tn(
            d_num[:, at : at + 2 * pair_width],
            phi[:, pair * 2 * features : (pair + 1) * 2 * features],
        )

    @pl.when(step == plane // tile - 1)
    def _():
        rows_used = pairs * head_size + pairs
        spare = pay.shape[1] - rows_used
        if spare:
            for i in range(2):
                pay[i, rows_used:, :] = jnp.zeros((spare, features), f32)
        for pair in range(pairs):
            totals = [
                acc[pair, pair_width + i * head_size : pair_width + i * head_size + 1, :]
                * float(head_size)
                for i in range(2)
            ]
            put_summary(pay, pair, pairs, acc[pair], totals, head_size, features)
        mine_out[...] = pay[ids[3]]
        sent_out[...] = pay[1 - ids[3]]


def feed_call(
    ids, j, hidden, cots, phi, mine, other, w_out, b_out, gain, shift, w_up, b_up, w_low, b_low, heads, after=()
):
    genes, width = hidden[0].shape
    tokens = plane * genes
    step = tile * genes
    features = phi.shape[1] // heads
    wide = w_up.shape[1]
    pairs = heads // 2
    pay = payload_shape(heads, width // heads, features)

    def rows(cols):
        return pl.BlockSpec((step, cols), lambda at, ids: (at, 0))

    ins = list(hidden) + list(cots) + [phi, mine, other, w_out, b_out, gain, shift, w_up, b_up, w_low, b_low]
    in_specs = [whole(a.shape) for a in ins]
    in_specs[2 * plane] = rows(phi.shape[1])
    for r in range(plane):
        in_specs[plane + r] = pl.BlockSpec((None, genes, width), lambda at, ids: (j, 0, 0))
    outs = [(near((genes, width)), whole((genes, width)))] * plane + [
        (near((tokens, wide), bf16), rows(wide)),
        (near((tokens, wide), bf16), rows(wide)),
        (near((tokens, width), bf16), rows(width)),
        (near((tokens, width), bf16), rows(width)),
        (far((tokens, width)), rows(width)),
        (far((tokens, width), bf16), rows(width)),
        (near((tokens, 2 * width), bf16), rows(2 * width)),
        (far((tokens, width), bf16), rows(width)),
        (near(pay), whole(pay)),
        (free(pay), whole(pay)),
        (near((8, width)), whole((8, width))),
        (near((1, wide)), whole((1, wide))),
    ]
    return call(
        feed_kernel,
        "feed_forward",
        (plane // tile,),
        in_specs,
        [o[0] for o in outs],
        [o[1] for o in outs],
        [
            pltpu.VMEM((2, *pay), f32),
            pltpu.VMEM((pairs, 2 * width // pairs, 2 * features), bf16),
            pltpu.VMEM((pairs, 2 * width // pairs, 2 * features), f32),
        ]
        + [pltpu.VMEM((step, width), f32)] * 7,
        ids,
        *ins,
        after=after,
        mib=22,
    )


def feature_back(grad_feat, phi, u, back_matrix, factor):
    pair_width = u.shape[1]
    low = (grad_feat * phi.astype(f32) * factor).astype(bf16)
    both = nn(low, back_matrix[...])
    return both[:, :pair_width] - factor * u.astype(f32) * both[:, pair_width:]


def d_query_kernel(ids, d_num, phi, query, mine, other, back_matrix, weight, d_query, d_normed, sums, matrix, *, factor):
    step = pl.program_id(0)
    pairs = matrix.shape[0]
    features = phi.shape[1] // pairs // 2
    width = query.shape[1]
    pair_width = width // pairs

    @pl.when(step == 0)
    def _():
        block_matrix(matrix, mine, other, ids[3], pairs, pair_width // 2, features, True)
        sums[...] = jnp.zeros_like(sums)

    for pair in range(pairs):
        cols = slice(pair * pair_width, (pair + 1) * pair_width)
        grad_feat = nn(d_num[:, pair * 2 * pair_width : (pair + 1) * 2 * pair_width], matrix[pair])
        grad = feature_back(
            grad_feat,
            phi[:, pair * 2 * features : (pair + 1) * 2 * features],
            query[:, cols],
            back_matrix,
            factor,
        )
        d_query[:, cols] = grad.astype(bf16)
    low = d_query[...]
    d_normed[...] = nt(low, weight[...])
    sums[...] += col_sum(low.astype(f32))


def d_query_call(ids, d_num, phi, joint, mine, other, back_matrix, weight, factor, after=()):
    tokens = joint.shape[0]
    width = joint.shape[1] // 3
    pair_width = back_matrix.shape[1] // 2
    pairs = width // pair_width
    step = tokens // plane * tile
    features = back_matrix.shape[0] // 2

    def rows(cols):
        return pl.BlockSpec((step, cols), lambda at, ids: (at, 0))

    return call(
        functools.partial(d_query_kernel, factor=factor),
        "query_gradient",
        (plane // tile,),
        [
            rows(2 * width),
            rows(phi.shape[1]),
            rows(width),
            whole(mine.shape),
            whole(other.shape),
            whole(back_matrix.shape),
            whole((width, width)),
        ],
        [near((tokens, width), bf16), near((tokens, width)), near((1, width))],
        [rows(width), rows(width), whole((1, width))],
        [pltpu.VMEM((pairs, 2 * pair_width, 2 * features), bf16)],
        ids,
        d_num,
        phi,
        joint,
        mine,
        other,
        back_matrix,
        weight,
        after=after,
        mib=20,
    )


def d_key_kernel(
    ids, h0, h1, h2, h3, joint, phi, d_query, d_normed_q, d_middle, mine, other, back_matrix, weight, gain,
    g0, g1, g2, g3, d_joint, sums, key_sums, matrix, total_ref, hid, *, factor,
):
    step = pl.program_id(0)
    pairs = matrix.shape[0]
    genes, width = h0.shape
    features = phi.shape[1] // pairs // 2
    pair_width = width // pairs
    head_size = pair_width // 2

    @pl.when(step == 0)
    def _():
        block_matrix(matrix, mine, other, ids[3], pairs, head_size, features, False)
        base = pairs * head_size
        for pair in range(pairs):
            half = pair // (pairs // 2)
            at = base + (pair % (pairs // 2)) * 2
            first = (ids[3] ^ half) == 0
            for i in range(2):
                total_ref[pair : pair + 1, i * features : (i + 1) * features] = jnp.where(
                    first, mine[at + i : at + i + 1, :], other[at + i : at + i + 1, :]
                )
        sums[...] = jnp.zeros_like(sums)
        key_sums[...] = jnp.zeros_like(key_sums)

    for k in range(plane // tile):

        @pl.when(step == k)
        def _():
            for i in range(tile):
                hid[i * genes : (i + 1) * genes, :] = (h0, h1, h2, h3)[k * tile + i][...]

    d_joint[:, :width] = d_query[...]
    for pair in range(pairs):
        at = pair * pair_width
        value = joint[:, 2 * width + at : 2 * width + at + pair_width]
        low = phi[:, pair * 2 * features : (pair + 1) * 2 * features]
        grad_feat = nn(value, matrix[pair]) + total_ref[pair : pair + 1, :]
        grad = feature_back(
            grad_feat, low, joint[:, width + at : width + at + pair_width], back_matrix, factor
        )
        d_joint[:, width + at : width + at + pair_width] = grad.astype(bf16)
        d_joint[:, 2 * width + at : 2 * width + at + pair_width] = nt(low, matrix[pair]).astype(bf16)
    low = d_joint[:, width:]
    key_sums[...] += col_sum(low.astype(f32))
    grad_normed = d_normed_q[...] + nt(low, weight[:, width:])
    scaled, inverse = norm_parts(hid[...])
    result = (d_middle[...] + norm_back(grad_normed, scaled, inverse, gain[...])).astype(bf16)
    result = result.astype(f32)
    sums[0:1, :] += col_sum(grad_normed * scaled)
    sums[1:2, :] += col_sum(grad_normed)
    sums[2:3, :] += col_sum(result)
    for k in range(plane // tile):

        @pl.when(step == k)
        def _():
            for i in range(tile):
                (g0, g1, g2, g3)[k * tile + i][...] = result[i * genes : (i + 1) * genes, :]


def d_key_call(ids, hidden, joint, phi, d_query, d_normed_q, d_middle, mine, other, back_matrix, weight, gain, factor, after=()):
    genes, width = hidden[0].shape
    tokens = plane * genes
    step = tile * genes
    pair_width = back_matrix.shape[1] // 2
    pairs = width // pair_width
    features = back_matrix.shape[0] // 2

    def rows(cols):
        return pl.BlockSpec((step, cols), lambda at, ids: (at, 0))

    ins = list(hidden) + [joint, phi, d_query, d_normed_q, d_middle, mine, other, back_matrix, weight, gain]
    in_specs = [whole(a.shape) for a in ins]
    for i in range(5):
        in_specs[plane + i] = rows(ins[plane + i].shape[1])
    outs = [(near((genes, width)), whole((genes, width)))] * plane + [
        (near((tokens, 3 * width), bf16), rows(3 * width)),
        (near((8, width)), whole((8, width))),
        (near((1, 2 * width)), whole((1, 2 * width))),
    ]
    return call(
        functools.partial(d_key_kernel, factor=factor),
        "key_gradient",
        (plane // tile,),
        in_specs,
        [o[0] for o in outs],
        [o[1] for o in outs],
        [
            pltpu.VMEM((pairs, pair_width, 2 * features), bf16),
            pltpu.VMEM((8, 2 * features), f32),
            pltpu.VMEM((step, width), f32),
        ],
        ids,
        *ins,
        after=after,
        mib=28,
    )


def put_shards(out, size, spot, where, first, count, per, rows, at, value):
    if rows % 8:
        out[at * size + first * rows : at * size + (first + count) * rows, :] = value
        return
    for s in range(count):
        to = (where(first + s) ^ spot) * per + at
        to = pl.multiple_of(to, 8)
        out[pl.ds(to, rows), :] = value[s * rows : (s + 1) * rows, :]


def in_slots(bundle, size, me, per, rows, order):
    if rows % 8 == 0:
        return bundle
    body = bundle[: size * per].reshape(per // rows, size, rows, -1).transpose(1, 0, 2, 3)
    place = placed(order, size.bit_length() - 1)
    owner = sorted(range(size), key=place)
    body = body[jnp.array(owner, jnp.int32) ^ me].reshape(size * per, -1)
    return jnp.concatenate([body, bundle[size * per :]], axis=0)


def side_of(sent):
    return (lambda ids: 1 - ids[1]) if sent else (lambda ids: ids[1])


def lower_weights_kernel(ids, a0, a1, c0, c1, out, *, size, where, spot_at):
    step = pl.program_id(0)
    part = size // 4
    rows = out.shape[0] // size
    value = tn(a0[...], c0[...]) + tn(a1[...], c1[...])
    for k in range(4):

        @pl.when(step == k)
        def _():
            put_shards(out, size, ids[spot_at], where, k * part, part, rows, rows, 0, value)


def lower_weights_call(ids, size, sent, where, spot_at, active, cot_low, after=()):
    tokens, wide = active[0].shape
    half = cot_low[0].shape[1] // 2
    side = side_of(sent)
    shape = (wide, half)
    return call(
        functools.partial(lower_weights_kernel, size=size, where=where, spot_at=spot_at),
        "lower_weights",
        (4,),
        [pl.BlockSpec((tokens, wide // 4), lambda at, ids: (0, at))] * 2
        + [pl.BlockSpec((tokens, half), lambda at, ids: (0, side(ids)))] * 2,
        near(shape),
        whole(shape),
        [],
        ids,
        *active,
        *cot_low,
        after=after,
        mib=16,
    )


def upper_weights_kernel(ids, n0, n1, u0, u1, t0, t1, b0, b1, out, *, size, where, spot_at):
    step = pl.program_id(0)
    part = size // 4
    rows = n0.shape[1] // size
    value = tn(n0[...], u0[...]) + tn(n1[...], u1[...])
    last = tn(t0[...], b0[...]) + tn(t1[...], b1[...])
    for k in range(4):

        @pl.when(step == k)
        def _():
            put_shards(out, size, ids[spot_at], where, 0, size, 5 * rows, rows, k * rows, value)
            put_shards(out, size, ids[spot_at], where, k * part, part, 5 * rows, rows, 4 * rows, last)


def upper_weights_call(ids, size, sent, where, spot_at, normed, d_upper, attention, d_branch, after=()):
    tokens, width = normed[0].shape
    half = width // 2
    side = side_of(sent)
    shape = (5 * width, half)
    return call(
        functools.partial(upper_weights_kernel, size=size, where=where, spot_at=spot_at),
        "upper_weights",
        (4,),
        [pl.BlockSpec((tokens, width), lambda at, ids: (0, 0))] * 2
        + [pl.BlockSpec((tokens, half), lambda at, ids: (0, side(ids) * 4 + at))] * 2
        + [pl.BlockSpec((tokens, width // 4), lambda at, ids: (0, at))] * 2
        + [pl.BlockSpec((tokens, half), lambda at, ids: (0, side(ids)))] * 2,
        near(shape),
        whole(shape),
        [],
        ids,
        *normed,
        *d_upper,
        *attention,
        *d_branch,
        after=after,
        mib=16,
    )


def joint_weights_kernel(ids, n0, n1, j0, j1, out, *, size, where, spot_at):
    step = pl.program_id(0)
    rows = n0.shape[1] // size
    value = tn(n0[...], j0[...]) + tn(n1[...], j1[...])
    for k in range(3):

        @pl.when(step == k)
        def _():
            put_shards(out, size, ids[spot_at], where, 0, size, 3 * rows, rows, k * rows, value)


def joint_weights_call(ids, size, sent, where, spot_at, normed, d_joint, after=()):
    tokens, width = normed[0].shape
    half = width // 2
    side = side_of(sent)
    shape = (3 * width, half)
    return call(
        functools.partial(joint_weights_kernel, size=size, where=where, spot_at=spot_at),
        "joint_weights",
        (3,),
        [pl.BlockSpec((tokens, width), lambda at, ids: (0, 0))] * 2
        + [pl.BlockSpec((tokens, half), lambda at, ids: (0, side(ids) * 3 + at))] * 2,
        near(shape),
        whole(shape),
        [],
        ids,
        *normed,
        *d_joint,
        after=after,
        mib=14,
    )


vector_rows = 32


def input_weights_kernel(ids, *refs, size, where, spot_at):
    own = refs[:2]
    merged = refs[2:5]
    r0, r1, v0, v1, f0, f1, u0, u1, k0, k1, q0, q1, s0, s1, d_low, sent, kept, zero_hidden = refs[5:]
    pieces = [own[j] if r == 0 else merged[r - 1].at[j] for r in range(plane) for j in range(2)]
    genes, width = own[0].shape
    half = width // 2
    rows = (sent.shape[0] - vector_rows) // size
    total = None
    for i, piece in enumerate(pieces):
        wide = piece[...]
        d_low[i * genes : (i + 1) * genes, :] = wide.astype(bf16)
        masked = wide * (v0, v1)[i % 2][i // 2][:, :1]
        total = masked if total is None else total + masked
    zero_hidden[...] = total
    parts = [f0[0:4, :] + f1[0:4, :], s0[0:3, :] + s1[0:3, :], q0[...] + q1[...], k0[...] + k1[...], u0[...] + u1[...]]
    for out, side in ((sent, 1 - ids[1]), (kept, ids[1])):
        value = None
        for i in range(8):
            chosen = (r0, r1)[i % 2][i // 2]
            lo = d_low[i * genes : (i + 1) * genes, :half]
            hi = d_low[i * genes : (i + 1) * genes, half:]
            product = tn(chosen, jnp.where(side == 0, lo, hi))
            value = product if value is None else value + product
        put_shards(out, size, ids[spot_at], where, 0, size, rows, rows, 0, value)
        at = size * rows
        for part in parts:
            for row in range(part.shape[0]):
                for c in range(part.shape[1] // half):
                    out[at : at + 1, :] = part[row : row + 1, c * half : (c + 1) * half]
                    at += 1
        out[at:, :] = jnp.zeros((out.shape[0] - at, half), f32)


def input_weights_call(ids, size, where, spot_at, own, came, rows, vacant, sums, after=()):
    genes, width = own[0].shape
    width_in = rows[0].shape[2]
    ins = [*own, *came, *rows, *vacant, *sums]
    shape = (width_in + vector_rows, width // 2)
    outs = [near((8 * genes, width), bf16), free(shape), near(shape), free((genes, width))]
    return call(
        functools.partial(input_weights_kernel, size=size, where=where, spot_at=spot_at),
        "input_weights",
        (1,),
        [whole(a.shape) for a in ins],
        outs,
        [whole(o.shape) for o in outs],
        [],
        ids,
        *ins,
        after=after,
        mib=28,
    )


def out_kernel(ids, *refs):
    out = refs[-1]
    merged = refs[-plane:-1]
    group = len(refs) - plane
    for j in range(group):
        out[ids[2] * group + j] = refs[j][...].astype(bf16)
        for r in range(1, plane):
            out[(ids[2] ^ r) * group + j] = merged[r - 1][j].astype(bf16)


def out_call(ids, own, came, after=()):
    genes, width = own[0].shape
    shape = (plane * len(own), genes, width)
    ins = [*own, *came]
    return call(
        out_kernel,
        "block_out",
        (1,),
        [whole(p.shape) for p in ins],
        far(shape, bf16),
        whole(shape),
        [],
        ids,
        *ins,
        after=after,
        mib=14,
    )


def token_kernel(ids, d_low, index, weight, token_grad):
    slots, _ = index.shape
    width = d_low.shape[1]
    genes = d_low.shape[0] // 8
    slot = lax.broadcasted_iota(jnp.int32, (slots, 1), 0)
    picked = jnp.zeros((slots, width), f32)
    gene = lax.broadcasted_iota(jnp.int32, (slots, genes), 1)
    match = (index[...] - ids[0] * genes) == gene
    for i in range(8):
        cell = i ^ (2 * ids[2])
        here = (slot >= ids[8 + cell]) & (slot < ids[9 + cell])
        chosen = jnp.where(match & here, 1.0, 0.0).astype(bf16)
        picked = picked + nn(chosen, d_low[i * genes : (i + 1) * genes, :])
    token_grad[0] = nt(picked.astype(bf16), weight[...])


def token_call(ids, d_low, index, weight, after=()):
    ins = [d_low, index, weight]
    shape = (1, index.shape[0], weight.shape[0])
    return call(
        token_kernel,
        "token_gradient",
        (1,),
        [whole(a.shape) for a in ins],
        far(shape),
        whole(shape),
        [],
        ids,
        *ins,
        after=after,
        mib=24,
    )


def zero_kernel(ids, mine, other, weight, out):
    total = mine[...] + other[...]
    high = total.astype(bf16)
    rest = total - high.astype(f32)
    low = rest.astype(bf16)
    out[...] = nt(high, weight[...]) + nt(low, weight[...])


def zero_call(ids, mine, other, weight, after=()):
    genes, width = mine.shape
    ins = [mine, other, weight]
    shape = (genes, weight.shape[0])
    return call(
        zero_kernel,
        "zero_gradient",
        (1,),
        [whole(a.shape) for a in ins],
        far(shape),
        whole(shape),
        [],
        ids,
        *ins,
        after=after,
        mib=12,
    )


def local(
    encoder_packed_tokens,
    token_gene_index,
    cell_counts,
    zero_embed,
    random_features,
    input_weight,
    input_bias,
    first_gain,
    first_shift,
    joint_weight,
    joint_bias,
    output_weight,
    output_bias,
    second_gain,
    second_shift,
    upper_weight,
    upper_bias,
    lower_weight,
    lower_bias,
    cotangent,
):
    placed_at.clear()
    size = lax.axis_size("gene")
    me = lax.axis_index("gene")
    core = lax.axis_index("cell")
    cells_here, genes, width = cotangent.shape
    head_size, features = random_features.shape
    heads = width // head_size
    factor = head_size ** (-0.25)
    group = cells_here // plane
    log = size.bit_length() - 1
    rest = list(range(3, log))
    orders = ([2, 1, 0] + rest, [2, 0, 1] + rest, [1, 0, 2] + rest, [0, 1, 2] + rest)
    where = [placed(order, log) for order in orders]
    ends = jnp.cumsum(cell_counts[0]).astype(jnp.int32)
    ids = jnp.concatenate(
        [
            jnp.stack([me, core, me % plane, (me // plane) % 2]).astype(jnp.int32),
            jnp.stack([placed(order, log)(me) for order in orders]).astype(jnp.int32),
            jnp.zeros((1,), jnp.int32),
            ends,
        ]
    )
    nothing = jnp.zeros((head_size, features), bf16)
    minus = jnp.full((head_size, features), -1.0, bf16)
    feats = jnp.concatenate(
        [
            jnp.concatenate([random_features, nothing], axis=1),
            jnp.concatenate([nothing, random_features], axis=1),
            jnp.concatenate([minus, nothing], axis=1),
            jnp.concatenate([nothing, minus], axis=1),
        ],
        axis=0,
    )
    back_matrix = jnp.concatenate([feats[: 2 * head_size].T, -feats[2 * head_size :].T], axis=1)

    def row(vector):
        return vector.reshape(1, -1)

    high = [1 << b for b in range(2, log)]
    last = ()

    def then(made, token, *more):
        nonlocal last
        last = (token, *more)
        return made

    def gene_swap(value, bit):
        return swap(value, "gene", size, bit)

    def out_and_in(blocks):
        return [block if r == 0 else gene_swap(block, r) for r, block in enumerate(blocks)]

    class Halves:
        def __init__(self, mine, sent):
            self.mine = mine
            self.came = gene_swap(sent, high[0])
            self.left = high[1:]

        def add(self):
            self.mine = add_call(ids, self.mine, self.came, after=last)
            then(None, self.mine)
            if self.left:
                self.came = gene_swap(self.mine, self.left.pop(0))
            else:
                self.other = gene_swap(self.mine, high[0])

        def finish(self):
            while not hasattr(self, "other"):
                self.add()
            return self.mine, self.other

    class Scatter:
        def __init__(self, sent, kept, order, rows, extra=0):
            per = (kept.shape[0] - extra) // size
            self.mine = in_slots(kept, size, me, per, rows, order)
            self.came = swap(in_slots(sent, size, me, per, rows, order), "cell", 2, 1)
            self.order = list(order)
            self.extra = extra

        def add(self):
            if self.order:
                self.mine, send = split_call(ids, self.mine, self.came, self.extra, after=last)
                then(None, self.mine)
                self.came = gene_swap(send, 1 << self.order.pop(0))
            else:
                self.mine = add_call(ids, self.mine, self.came, after=last)
                then(None, self.mine)
                self.done = True

        def finish(self):
            while not hasattr(self, "done"):
                self.add()
            return self.mine

    shard = width // size
    wide_shard = upper_weight.shape[1] // size
    in_shard = input_weight.shape[0] // size
    hidden, rows, vacant = [], [], []
    for j in range(group):
        made = rows_call(
            ids, j, group, encoder_packed_tokens[0], token_gene_index, zero_embed, input_weight, row(input_bias),
            after=last,
        )
        hidden.append(out_and_in(made[:plane]))
        rows.append(made[plane])
        vacant.append(made[plane + 1])
        then(None, made[plane + 1])
    normed, joint, key_phi, sums = [], [], [], []

    def keys_of(j):
        made = key_call(
            ids, hidden[j], joint_weight, row(joint_bias), row(first_gain), row(first_shift), feats, factor,
            after=last,
        )
        normed.append(made[0])
        joint.append(made[1])
        key_phi.append(made[2])
        sums.append(Halves(made[3], made[4]))
        then(None, made[0])

    keys_of(0)
    w_up, w_low, w_out, w_joint = hold_call(
        ids, upper_weight, lower_weight, output_weight, joint_weight, after=last
    )
    then(None, w_out)
    sums[0].add()
    keys_of(1)
    wide = cotangent_call(ids, group, cotangent, after=last)
    then(None, wide[0])
    cots = out_and_in(wide)
    query_phi = []

    def query_of(j):
        query_phi.append(query_call(ids, joint[j], feats, factor, after=last))
        then(None, query_phi[j])

    query_of(0)
    sums[1].add()
    sums[0].finish()
    query_of(1)
    sums[1].finish()
    sums = [s.finish() for s in sums]
    fed, d_sums = [], []
    for j in range(group):
        made = feed_call(
            ids, j, hidden[j], cots, query_phi[j], *sums[j], w_out, row(output_bias), row(second_gain),
            row(second_shift), w_up, row(upper_bias), w_low, row(lower_bias), heads,
            after=last,
        )
        fed.append(made)
        d_sums.append(Halves(made[plane + 8], made[plane + 9]))
        then(None, made[plane + 2])
    active, d_upper, normed_two, attention, d_middle, d_branch, d_num, cot_low, _, _, sums_two, up_sums = list(
        zip(*fed)
    )[plane:]
    queries = []

    def d_query_of(j):
        queries.append(
            d_query_call(
                ids, d_num[j], query_phi[j], joint[j], *sums[j], back_matrix, w_joint, factor, after=last
            )
        )
        then(None, queries[j][1])

    def lower_of(sent):
        made = lower_weights_call(ids, size, sent, where[0], 4, active, cot_low, after=last)
        return then(made, made)

    def upper_of(sent):
        made = upper_weights_call(
            ids, size, sent, where[1], 5, normed_two, d_upper, attention, d_branch, after=last
        )
        return then(made, made)

    def joint_of(sent):
        made = joint_weights_call(ids, size, sent, where[2], 6, normed, d_joint, after=last)
        return then(made, made)

    def pass_on(*arrays):
        made = pass_call(ids, *arrays, after=last)
        then(None, made[0])
        return made

    def release(blocks):
        sent = release_call(ids, [block[r] for block in blocks for r in range(1, plane)], after=last)
        then(None, sent[0])
        return [gene_swap(block, r) for r, block in enumerate(sent, 1)]

    keys = []

    def d_key_of(j):
        made = d_key_call(
            ids, hidden[j], joint[j], key_phi[j], queries[j][0], queries[j][1], d_middle[j], *d_sums[j].finish(),
            back_matrix, w_joint, row(first_gain), factor,
            after=last,
        )
        keys.append(made)
        then(None, made[plane])

    back_out = release([made[:plane] for made in fed])
    d_sums[0].add()
    d_query_of(0)
    d_sums[1].add()
    d_query_of(1)
    lower_sent = lower_of(True)
    d_sums[0].add()
    lower_kept = lower_of(False)
    d_sums[1].add()
    upper_sent = upper_of(True)
    then(None, *last, *back_out)
    d_key_of(0)
    upper_kept = upper_of(False)
    d_key_of(1)
    lower_sent, upper_sent = pass_on(lower_sent, upper_sent)
    lower_sum = Scatter(lower_sent, lower_kept, orders[0], wide_shard)
    upper_sum = Scatter(upper_sent, upper_kept, orders[1], shard)
    backs = release([k[:plane] for k in keys])
    upper_sum.add()
    d_joint = [k[plane] for k in keys]
    joint_sent = joint_of(True)
    joint_kept = joint_of(False)
    block_out = out_call(ids, [made[0] for made in fed], back_out, after=last)
    then(None, block_out)
    sums_one = [k[plane + 1] for k in keys]
    key_sums = [k[plane + 2] for k in keys]
    query_sums = [q[2] for q in queries]
    then(None, *last, upper_sum.came)
    d_low, input_sent, input_kept, zero_hidden = input_weights_call(
        ids, size, where[3], 7, [k[0] for k in keys], backs, rows, vacant,
        [*sums_two, *up_sums, *key_sums, *query_sums, *sums_one],
        after=last,
    )
    then(None, zero_hidden)
    input_sum = Scatter(input_sent, input_kept, orders[3], in_shard, vector_rows)
    lower_sum.add()
    upper_sum.add()
    (joint_sent,) = pass_on(joint_sent)
    joint_sum = Scatter(joint_sent, joint_kept, orders[2], shard)
    zero_came = swap(zero_hidden, "cell", 2, 1)
    input_sum.add()
    joint_sum.add()
    token_grad = token_call(ids, d_low, token_gene_index.reshape(-1, 1), input_weight, after=last)
    then(None, token_grad)
    zero_grad = zero_call(ids, zero_hidden, zero_came, input_weight, after=last)
    then(None, zero_grad)
    input_sum.add()
    upper_sum.add()
    lower_sum.add()
    joint_sum.add()
    input_sum.add()
    upper_sum.add()
    lower_sum.add()
    input_sum.add()
    joint_sum.add()
    upper_sum.finish()
    lower_sum.add()
    joint_sum.add()
    input_sum.finish()
    lower_sum.finish()
    joint_sum.finish()

    def both_halves(mine):
        other = swap(mine, "cell", 2, 1)
        return jnp.where(core == 0, mine, other), jnp.where(core == 0, other, mine)

    def opened(pair, at, count, groups):
        parts = [b[at + g * count : at + (g + 1) * count] for b in pair for g in range(groups)]
        return jnp.concatenate(parts, axis=1)

    lower_pair = both_halves(lower_sum.mine)
    upper_pair = both_halves(upper_sum.mine)
    g_lower = opened(lower_pair, 0, wide_shard, 1)
    g_upper = opened(upper_pair, 0, shard, 4)
    g_output = opened(upper_pair, 4 * shard, shard, 1)
    g_joint = opened(both_halves(joint_sum.mine), 0, shard, 3)
    g_input = opened(both_halves(input_sum.mine[:in_shard]), 0, in_shard, 1)
    flat = input_sum.mine[in_shard:].reshape(-1)
    lengths = [width] * 7 + [3 * width, upper_weight.shape[1]]
    found = []
    at = 0
    for length in lengths:
        part = length // size
        found.append(lax.dynamic_slice(flat, (at + me * part,), (part,)))
        at += length
    small_out = [found[i] for i in (6, 4, 5, 7, 2, 0, 1, 8, 3)]
    return (
        block_out,
        token_grad,
        zero_grad,
        g_input,
        small_out[0],
        small_out[1],
        small_out[2],
        g_joint,
        small_out[3],
        g_output,
        small_out[4],
        small_out[5],
        small_out[6],
        g_upper,
        small_out[7],
        g_lower,
        small_out[8],
    )


def solution(mesh):
    return jax.shard_map(
        local,
        mesh=mesh,
        in_specs=(
            P("cell", "gene", None),
            P("cell", "gene"),
            P("cell", "gene"),
            P("gene", None),
            P(),
            P(),
            P(),
            P(),
            P(),
            P(),
            P(),
            P(),
            P(),
            P(),
            P(),
            P(),
            P(),
            P(),
            P(),
            P("cell", "gene", None),
        ),
        out_specs=(
            P("cell", "gene", None),
            P("cell", "gene", None),
            P("gene", None),
            P("gene", None),
            P("gene"),
            P("gene"),
            P("gene"),
            P("gene", None),
            P("gene"),
            P("gene", None),
            P("gene"),
            P("gene"),
            P("gene"),
            P("gene", None),
            P("gene"),
            P("gene", None),
            P("gene"),
        ),
        check_vma=False,
    )
```

```python
import functools
import math

import jax
import jax.numpy as jnp
from jax import lax
from jax.experimental import pallas as pl
from jax.experimental.pallas import tpu as pltpu
from jax.sharding import PartitionSpec as P

epsilon = 1e-05
f32 = jnp.float32
bf16 = jnp.bfloat16
plane = 4
tile = 4


def nn(left, right):
    return jnp.dot(left, right, preferred_element_type=f32)


def nt(left, right):
    return lax.dot_general(left, right, (((1,), (1,)), ((), ())), preferred_element_type=f32)


def tn(left, right):
    return lax.dot_general(left, right, (((0,), (0,)), ((), ())), preferred_element_type=f32)


def col_sum(values):
    return jnp.sum(values, axis=0, keepdims=True)


def norm_parts(values):
    centred = values - jnp.mean(values, axis=-1, keepdims=True)
    inverse = lax.rsqrt(jnp.mean(centred * centred, axis=-1, keepdims=True) + epsilon)
    return centred * inverse, inverse


def norm_back(grad_in, scaled, inverse, gain):
    weighted = grad_in * gain
    return inverse * (
        weighted
        - jnp.mean(weighted, axis=-1, keepdims=True)
        - scaled * jnp.mean(weighted * scaled, axis=-1, keepdims=True)
    )


def whole(shape):
    return pl.BlockSpec(shape, lambda *at: (0,) * len(shape))


placed_at = []


def near(shape, dtype=f32):
    return pltpu.VMEM(shape, dtype)


def far(shape, dtype=f32):
    return pltpu.HBM(shape, dtype)


def free(shape, dtype=f32):
    return jax.ShapeDtypeStruct(shape, dtype)


def placed(order, log):
    return lambda number: sum(((number >> bit) & 1) << (log - 1 - i) for i, bit in enumerate(order))


def call(kernel, name, grid, in_specs, outs, out_specs, scratch, *args, after=(), mib=60):
    first = 1 + len(in_specs)

    def body(*refs):
        kernel(*refs[:first], *refs[first + len(after) :])

    def held(array):
        for other, space in placed_at:
            if array is other:
                return pltpu.with_memory_space_constraint(array, space)
        return array

    made = pl.pallas_call(
        body,
        name=name,
        grid_spec=pltpu.PrefetchScalarGridSpec(
            num_scalar_prefetch=1,
            grid=grid,
            in_specs=list(in_specs) + [pl.BlockSpec(memory_space=pl.ANY)] * len(after),
            out_specs=out_specs,
            scratch_shapes=scratch,
        ),
        out_shape=outs,
        compiler_params=pltpu.CompilerParams(
            vmem_limit_bytes=mib << 20, dimension_semantics=("arbitrary",) * len(grid)
        ),
        cost_estimate=pl.CostEstimate(flops=1000, bytes_accessed=1000, transcendentals=0),
    )(args[0], *(held(a) for a in args[1:]), *(held(a) for a in after))
    several = isinstance(outs, (list, tuple))
    for out, array in zip(outs if several else [outs], made if several else [made]):
        if getattr(out, "memory_space", None) in (pltpu.VMEM, pltpu.HBM):
            placed_at.append((array, out.memory_space))
    return made


def swap(value, axis, size, bit):
    return lax.ppermute(value, axis, [(i, i ^ bit) for i in range(size)])


def rows_kernel(ids, tokens, index, zero, weight, bias, h0, h1, h2, h3, rows_out, vacant_out, *, group, j):
    genes = zero.shape[0]
    first_gene = ids[0] * genes
    slots = index.shape[1]
    slot = lax.broadcasted_iota(jnp.int32, (genes, slots), 1)
    gene = lax.broadcasted_iota(jnp.int32, (genes, slots), 0)
    match = (index[...] - first_gene) == gene
    for r in (3, 1, 2, 0):
        cell = (ids[2] ^ r) * group + j
        here = match & (slot >= ids[8 + cell]) & (slot < ids[9 + cell])
        chosen = jnp.where(here, 1.0, 0.0)
        vacant = 1.0 - jnp.sum(chosen, axis=1, keepdims=True)
        rows = nn(chosen.astype(bf16), tokens[...]) + vacant * zero[...].astype(f32)
        rows = rows.astype(bf16)
        rows_out[r] = rows
        vacant_out[r] = jnp.broadcast_to(vacant, (genes, 128))
        (h0, h1, h2, h3)[r][...] = nn(rows, weight[...]) + bias[...]


def rows_call(ids, j, group, tokens, index, zero, weight, bias, after=()):
    tokens, weight = (pltpu.with_memory_space_constraint(a, pltpu.HBM) for a in (tokens, weight))
    genes, width_in = zero.shape
    width = weight.shape[1]
    outs = [free((genes, width))] * plane + [
        far((plane, genes, width_in), bf16),
        far((plane, genes, 128)),
    ]
    ins = [tokens, index, zero, weight, bias]
    return call(
        functools.partial(rows_kernel, group=group, j=j),
        "gene_rows",
        (1,),
        [whole(a.shape) for a in ins],
        outs,
        [whole(o.shape) for o in outs],
        [],
        ids,
        *ins,
        after=after,
        mib=20,
    )


def cotangent_kernel(ids, cot, c0, c1, c2, c3):
    for r, out in enumerate((c0, c1, c2, c3)):
        for j in range(out.shape[0]):
            out[j] = cot[(ids[2] ^ r) * out.shape[0] + j].astype(f32)


def cotangent_call(ids, group, cot, after=()):
    _, genes, width = cot.shape
    outs = [free((group, genes, width))] * plane
    return call(
        cotangent_kernel,
        "wide_cotangent",
        (1,),
        [whole(cot.shape)],
        outs,
        [whole(o.shape) for o in outs],
        [],
        ids,
        cot,
        after=after,
        mib=14,
    )


def pass_kernel(ids, *refs):
    count = len(refs) // 2
    for given, out in zip(refs[:count], refs[count:]):
        out[...] = given[...]


def pass_call(ids, *arrays, after=()):
    return call(
        pass_kernel,
        "pass_on",
        (1,),
        [whole(a.shape) for a in arrays],
        [free(a.shape, a.dtype) for a in arrays],
        [whole(a.shape) for a in arrays],
        [],
        ids,
        *arrays,
        after=after,
        mib=16,
    )


def release_kernel(ids, *refs):
    outs = refs[-(plane - 1) :]
    for i, piece in enumerate(refs[: -(plane - 1)]):
        outs[i % (plane - 1)][i // (plane - 1)] = piece[...]


def release_call(ids, pieces, after=()):
    genes, width = pieces[0].shape
    outs = [free((len(pieces) // (plane - 1), genes, width))] * (plane - 1)
    return call(
        release_kernel,
        "release",
        (1,),
        [whole(p.shape) for p in pieces],
        outs,
        [whole(o.shape) for o in outs],
        [],
        ids,
        *pieces,
        after=after,
        mib=14,
    )


def hold_kernel(ids, *refs):
    count = len(refs) // 2
    for given, held in zip(refs[:count], refs[count:]):
        held[...] = given[...]


def hold_call(ids, *arrays, after=()):
    outs = [near(a.shape, a.dtype) for a in arrays]
    return call(
        hold_kernel,
        "hold",
        (1,),
        [whole(a.shape) for a in arrays],
        outs,
        [whole(a.shape) for a in arrays],
        [],
        ids,
        *arrays,
        after=after,
        mib=12,
    )


def add_kernel(ids, mine, came, out):
    out[...] = mine[...] + came[...]


def add_call(ids, mine, came, out=free, after=()):
    return call(
        add_kernel,
        "add",
        (1,),
        [whole(mine.shape)] * 2,
        out(mine.shape),
        whole(mine.shape),
        [],
        ids,
        mine,
        came,
        after=after,
        mib=8,
    )


def split_kernel(ids, mine, came, keep, send, *, extra):
    half = keep.shape[0] - extra
    keep[:half, :] = mine[:half, :] + came[:half, :]
    send[:half, :] = mine[half : 2 * half, :] + came[half : 2 * half, :]
    if extra:
        both = mine[2 * half :, :] + came[2 * half :, :]
        keep[half:, :] = both
        send[half:, :] = both


def split_call(ids, mine, came, extra=0, after=()):
    rows, cols = mine.shape
    shape = ((rows - extra) // 2 + extra, cols)
    return call(
        functools.partial(split_kernel, extra=extra),
        "add_halves",
        (1,),
        [whole(mine.shape)] * 2,
        [near(shape), free(shape)],
        [whole(shape)] * 2,
        [],
        ids,
        mine,
        came,
        after=after,
        mib=16,
    )


def phi_of(u, feature_matrix, factor):
    features = feature_matrix.shape[1] // 2
    wide = u.astype(f32)
    square = (wide * wide * (0.5 * factor)).astype(bf16)
    power = nn(jnp.concatenate([u, square], axis=1), feature_matrix[...])
    scale = factor * math.log2(math.e)
    return jnp.exp2(power * scale - 0.5 * math.log2(features)).astype(bf16)


def put_summary(out, pair, pairs, both, totals, head_size, features):
    half = pair // (pairs // 2)
    at = (pair % (pairs // 2)) * 2
    base = pairs * head_size
    for i in range(2):
        cols = slice(i * features, (i + 1) * features)
        out[half, (at + i) * head_size : (at + i + 1) * head_size, :] = both[
            i * head_size : (i + 1) * head_size, cols
        ]
        out[half, base + at + i : base + at + i + 1, :] = totals[i][:, cols]


def block_matrix(matrix, mine, other, flip, pairs, head_size, features, with_totals):
    base = pairs * head_size
    for pair in range(pairs):
        half = pair // (pairs // 2)
        at = (pair % (pairs // 2)) * 2
        first = (flip ^ half) == 0

        def take(lo, hi):
            return jnp.where(first, mine[lo:hi, :], other[lo:hi, :])

        nothing = jnp.zeros((head_size, features), bf16)
        for i in range(2):
            rows = slice(i * head_size, (i + 1) * head_size)
            part = take((at + i) * head_size, (at + i + 1) * head_size).astype(bf16)
            matrix[pair, rows, i * features : (i + 1) * features] = part
            matrix[pair, rows, (1 - i) * features : (2 - i) * features] = nothing
            if with_totals:
                rows = slice((2 + i) * head_size, (3 + i) * head_size)
                total = take(base + at + i, base + at + i + 1)
                spread = jnp.broadcast_to(total, (head_size, features)).astype(bf16)
                matrix[pair, rows, i * features : (i + 1) * features] = spread
                matrix[pair, rows, (1 - i) * features : (2 - i) * features] = nothing


def payload_shape(heads, head_size, features):
    rows = heads // 2 * head_size + heads // 2
    return (rows + (-rows) % 8, features)


def key_kernel(
    ids, h0, h1, h2, h3, weight, bias, gain, shift, feats, normed, joint, phi, mine, sent, out, *, factor
):
    genes, width = h0.shape
    features = feats.shape[1] // 2
    pair_width = feats.shape[0] // 2
    pairs = width // pair_width
    for r, block in enumerate((h0, h1, h2, h3)):
        scaled, _ = norm_parts(block[...])
        normed[r * genes : (r + 1) * genes, :] = (scaled * gain[...] + shift[...]).astype(bf16)
    for part in (1, 2, 0):
        cols = slice(part * width, (part + 1) * width)
        joint[:, cols] = (nn(normed[...], weight[:, cols]) + bias[:, cols]).astype(bf16)
    rows_used = pairs * (pair_width // 2) + pairs
    spare = out.shape[1] - rows_used
    if spare:
        for i in range(2):
            out[i, rows_used:, :] = jnp.zeros((spare, features), f32)
    for pair in range(pairs):
        at = width + pair * pair_width
        low = phi_of(joint[:, at : at + pair_width], feats, factor)
        phi[:, pair * 2 * features : (pair + 1) * 2 * features] = low
        value = joint[:, width + at : width + at + pair_width]
        total = col_sum(low.astype(f32))
        put_summary(out, pair, pairs, tn(value, low), (total, total), pair_width // 2, features)
    mine[...] = out[ids[3]]
    sent[...] = out[1 - ids[3]]


def key_call(ids, hidden, weight, bias, gain, shift, feats, factor, after=()):
    genes, width = hidden[0].shape
    tokens = plane * genes
    features = feats.shape[1] // 2
    heads = 2 * width // (feats.shape[0] // 2)
    pay = payload_shape(heads, width // heads, features)
    outs = [
        far((tokens, width), bf16),
        near((tokens, 3 * width), bf16),
        far((tokens, heads * features), bf16),
        near(pay),
        free(pay),
    ]
    ins = list(hidden) + [weight, bias, gain, shift, feats]
    return call(
        functools.partial(key_kernel, factor=factor),
        "key_summary",
        (1,),
        [whole(a.shape) for a in ins],
        outs,
        [whole(o.shape) for o in outs],
        [pltpu.VMEM((2, *pay), f32)],
        ids,
        *ins,
        after=after,
        mib=24,
    )


def query_kernel(ids, joint, feats, phi, *, factor):
    features = feats.shape[1] // 2
    pair_width = feats.shape[0] // 2
    for pair in range(joint.shape[1] // pair_width):
        u = joint[:, pair * pair_width : (pair + 1) * pair_width]
        phi[:, pair * 2 * features : (pair + 1) * 2 * features] = phi_of(u, feats, factor)


def query_call(ids, joint, feats, factor, after=()):
    tokens, wide = joint.shape
    width = wide // 3
    features = feats.shape[1] // 2
    heads = 2 * width // (feats.shape[0] // 2)
    step = tokens // 2
    return call(
        functools.partial(query_kernel, factor=factor),
        "query_features",
        (2,),
        [pl.BlockSpec((step, width), lambda at, ids: (at, 0)), whole(feats.shape)],
        near((tokens, heads * features), bf16),
        pl.BlockSpec((step, heads * features), lambda at, ids: (at, 0)),
        [],
        ids,
        joint,
        feats,
        after=after,
        mib=16,
    )


def gelu_parts(x):
    expo = jnp.exp2(x * x * (-0.5 * math.log2(math.e)))
    t = 1.0 / (1.0 + (0.3275911 * math.sqrt(0.5)) * jnp.abs(x))
    poly = t * (
        0.5 * 0.254829592
        + t
        * (
            0.5 * -0.284496736
            + t * (0.5 * 1.421413741 + t * (0.5 * -1.453152027 + t * (0.5 * 1.061405429)))
        )
    )
    tail = poly * expo
    return jnp.where(x > 0, 1.0 - tail, tail), expo * 0.3989422804014327


def feed_kernel(
    ids, h0, h1, h2, h3, c0, c1, c2, c3, phi, mine, other, w_out, b_out, gain, shift, w_up, b_up, w_low, b_low,
    g0, g1, g2, g3, active, d_upper, normed, attention, d_middle, d_branch, d_num, cot_low, mine_out, sent_out, sums, up_sums,
    pay, matrix, att_wide, recip, scaled_ref, back, result,
):
    genes, width = h0.shape
    pairs = matrix.shape[0]
    features = phi.shape[1] // pairs // 2
    pair_width = width // pairs
    head_size = pair_width // 2
    chunk = 1024
    blocks = [slice(r * genes, (r + 1) * genes) for r in range(plane)]
    block_matrix(matrix, mine, other, ids[3], pairs, head_size, features, True)
    for rows, block in zip(blocks, (c0, c1, c2, c3)):
        cot_low[rows, :] = block[...].astype(bf16)
    for pair in range(pairs):
        cols = slice(pair * pair_width, (pair + 1) * pair_width)
        both = nt(phi[:, pair * 2 * features : (pair + 1) * 2 * features], matrix[pair])
        inverse = 1.0 / both[:, pair_width:]
        quotient = both[:, :pair_width] * inverse
        att_wide[:, cols] = quotient
        recip[:, cols] = inverse
        attention[:, cols] = quotient.astype(bf16)
    result[...] = nn(attention[...], w_out[...]) + b_out[...]
    for rows, block in zip(blocks, (h0, h1, h2, h3)):
        mid = block[...] + result[rows, :]
        result[rows, :] = mid + b_low[...]
        scaled, inverse = norm_parts(mid)
        scaled_ref[rows, :] = scaled
        normed[rows, :] = (scaled * gain[...] + shift[...]).astype(bf16)
        back[rows, :] = jnp.broadcast_to(inverse, scaled.shape)
    d_middle[...] = back[...]
    for at in range(w_up.shape[1] // chunk):
        cols = slice(at * chunk, (at + 1) * chunk)
        upper = nn(normed[...], w_up[:, cols]) + b_up[:, cols]
        grad_active = nt(cot_low[...], w_low[cols, :])
        cumulative, density = gelu_parts(upper)
        active[:, cols] = (upper * cumulative).astype(bf16)
        low = (grad_active * (cumulative + upper * density)).astype(bf16)
        d_upper[:, cols] = low
        up_sums[:, cols] = col_sum(low.astype(f32))
        if at == 0:
            back[...] = nt(low, w_up[:, cols])
        else:
            back[...] += nt(low, w_up[:, cols])
        result[...] += nn(active[:, cols], w_low[cols, :])
    for rows, block in zip(blocks, (g0, g1, g2, g3)):
        block[...] = result[rows, :]
    grad_normed = back[...]
    scaled = scaled_ref[...]
    cot = cot_low[...].astype(f32)
    grad_mid = cot + norm_back(grad_normed, scaled, d_middle[...], gain[...])
    d_middle[...] = grad_mid
    branch = grad_mid.astype(bf16)
    d_branch[...] = branch
    sums[0:1, :] = col_sum(grad_normed * scaled)
    sums[1:2, :] = col_sum(grad_normed)
    sums[2:3, :] = col_sum(branch.astype(f32))
    sums[3:4, :] = col_sum(cot)
    sums[4:, :] = jnp.zeros((sums.shape[0] - 4, width), f32)
    back[...] = nt(branch, w_out[...])
    row = lax.broadcasted_iota(jnp.int32, (2 * pair_width, pair_width), 0) // head_size % 2
    col = lax.broadcasted_iota(jnp.int32, (2 * pair_width, pair_width), 1) // head_size
    ones = jnp.where(row == col, 1.0, 0.0).astype(bf16)
    rows_used = pairs * head_size + pairs
    spare = pay.shape[1] - rows_used
    if spare:
        for i in range(2):
            pay[i, rows_used:, :] = jnp.zeros((spare, features), f32)
    for pair in range(pairs):
        cols = slice(pair * pair_width, (pair + 1) * pair_width)
        grad = back[:, cols]
        inverse = recip[:, cols]
        product = grad * att_wide[:, cols]
        high = product.astype(bf16)
        low = (product - high.astype(f32)).astype(bf16)
        total = nn(jnp.concatenate([high, low], axis=1), ones)
        at = pair * 2 * pair_width
        d_num[:, at : at + pair_width] = (grad * inverse).astype(bf16)
        d_num[:, at + pair_width : at + 2 * pair_width] = (
            total * inverse * (-1.0 / head_size)
        ).astype(bf16)
        both = tn(
            d_num[:, at : at + 2 * pair_width],
            phi[:, pair * 2 * features : (pair + 1) * 2 * features],
        )
        totals = [
            both[pair_width + i * head_size : pair_width + i * head_size + 1, :] * float(head_size)
            for i in range(2)
        ]
        put_summary(pay, pair, pairs, both, totals, head_size, features)
    mine_out[...] = pay[ids[3]]
    sent_out[...] = pay[1 - ids[3]]


def feed_call(
    ids, j, hidden, cots, phi, mine, other, w_out, b_out, gain, shift, w_up, b_up, w_low, b_low, heads, after=()
):
    genes, width = hidden[0].shape
    tokens = plane * genes
    step = tokens
    features = phi.shape[1] // heads
    wide = w_up.shape[1]
    pairs = heads // 2
    pay = payload_shape(heads, width // heads, features)

    def rows(cols):
        return pl.BlockSpec((step, cols), lambda at, ids: (at, 0))

    ins = list(hidden) + list(cots) + [phi, mine, other, w_out, b_out, gain, shift, w_up, b_up, w_low, b_low]
    in_specs = [whole(a.shape) for a in ins]
    in_specs[2 * plane] = rows(phi.shape[1])
    for r in range(plane):
        in_specs[plane + r] = pl.BlockSpec((None, genes, width), lambda at, ids: (j, 0, 0))
    outs = [(near((genes, width)), whole((genes, width)))] * plane + [
        (near((tokens, wide), bf16), rows(wide)),
        (near((tokens, wide), bf16), rows(wide)),
        (near((tokens, width), bf16), rows(width)),
        (near((tokens, width), bf16), rows(width)),
        (far((tokens, width)), rows(width)),
        (far((tokens, width), bf16), rows(width)),
        (near((tokens, 2 * width), bf16), rows(2 * width)),
        (far((tokens, width), bf16), rows(width)),
        (near(pay), whole(pay)),
        (free(pay), whole(pay)),
        (near((8, width)), whole((8, width))),
        (near((1, wide)), whole((1, wide))),
    ]
    return call(
        feed_kernel,
        "feed_forward",
        (1,),
        in_specs,
        [o[0] for o in outs],
        [o[1] for o in outs],
        [
            pltpu.VMEM((2, *pay), f32),
            pltpu.VMEM((pairs, 2 * width // pairs, 2 * features), bf16),
        ]
        + [pltpu.VMEM((step, width), f32)] * 5,
        ids,
        *ins,
        after=after,
        mib=22,
    )


def feature_back(grad_feat, phi, u, back_matrix, factor):
    pair_width = u.shape[1]
    low = (grad_feat * phi.astype(f32) * factor).astype(bf16)
    both = nn(low, back_matrix[...])
    return both[:, :pair_width] - factor * u.astype(f32) * both[:, pair_width:]


def d_query_kernel(ids, d_num, phi, query, mine, other, back_matrix, weight, d_query, d_normed, sums, matrix, *, factor):
    step = pl.program_id(0)
    pairs = matrix.shape[0]
    features = phi.shape[1] // pairs // 2
    width = query.shape[1]
    pair_width = width // pairs

    @pl.when(step == 0)
    def _():
        block_matrix(matrix, mine, other, ids[3], pairs, pair_width // 2, features, True)
        sums[...] = jnp.zeros_like(sums)

    for pair in range(pairs):
        cols = slice(pair * pair_width, (pair + 1) * pair_width)
        grad_feat = nn(d_num[:, pair * 2 * pair_width : (pair + 1) * 2 * pair_width], matrix[pair])
        grad = feature_back(
            grad_feat,
            phi[:, pair * 2 * features : (pair + 1) * 2 * features],
            query[:, cols],
            back_matrix,
            factor,
        )
        d_query[:, cols] = grad.astype(bf16)
    low = d_query[...]
    d_normed[...] = nt(low, weight[...])
    sums[...] += col_sum(low.astype(f32))


def d_query_call(ids, d_num, phi, joint, mine, other, back_matrix, weight, factor, after=()):
    tokens = joint.shape[0]
    width = joint.shape[1] // 3
    pair_width = back_matrix.shape[1] // 2
    pairs = width // pair_width
    step = tokens // plane * tile
    features = back_matrix.shape[0] // 2

    def rows(cols):
        return pl.BlockSpec((step, cols), lambda at, ids: (at, 0))

    return call(
        functools.partial(d_query_kernel, factor=factor),
        "query_gradient",
        (plane // tile,),
        [
            rows(2 * width),
            rows(phi.shape[1]),
            rows(width),
            whole(mine.shape),
            whole(other.shape),
            whole(back_matrix.shape),
            whole((width, width)),
        ],
        [near((tokens, width), bf16), near((tokens, width)), near((1, width))],
        [rows(width), rows(width), whole((1, width))],
        [pltpu.VMEM((pairs, 2 * pair_width, 2 * features), bf16)],
        ids,
        d_num,
        phi,
        joint,
        mine,
        other,
        back_matrix,
        weight,
        after=after,
        mib=20,
    )


def d_key_kernel(
    ids, h0, h1, h2, h3, joint, phi, d_query, d_normed_q, d_middle, mine, other, back_matrix, weight, gain,
    g0, g1, g2, g3, d_joint, sums, key_sums, matrix, total_ref, hid, *, factor,
):
    step = pl.program_id(0)
    pairs = matrix.shape[0]
    genes, width = h0.shape
    features = phi.shape[1] // pairs // 2
    pair_width = width // pairs
    head_size = pair_width // 2

    @pl.when(step == 0)
    def _():
        block_matrix(matrix, mine, other, ids[3], pairs, head_size, features, False)
        base = pairs * head_size
        for pair in range(pairs):
            half = pair // (pairs // 2)
            at = base + (pair % (pairs // 2)) * 2
            first = (ids[3] ^ half) == 0
            for i in range(2):
                total_ref[pair : pair + 1, i * features : (i + 1) * features] = jnp.where(
                    first, mine[at + i : at + i + 1, :], other[at + i : at + i + 1, :]
                )
        sums[...] = jnp.zeros_like(sums)
        key_sums[...] = jnp.zeros_like(key_sums)

    for k in range(plane // tile):

        @pl.when(step == k)
        def _():
            for i in range(tile):
                hid[i * genes : (i + 1) * genes, :] = (h0, h1, h2, h3)[k * tile + i][...]

    d_joint[:, :width] = d_query[...]
    for pair in range(pairs):
        at = pair * pair_width
        value = joint[:, 2 * width + at : 2 * width + at + pair_width]
        low = phi[:, pair * 2 * features : (pair + 1) * 2 * features]
        grad_feat = nn(value, matrix[pair]) + total_ref[pair : pair + 1, :]
        grad = feature_back(
            grad_feat, low, joint[:, width + at : width + at + pair_width], back_matrix, factor
        )
        d_joint[:, width + at : width + at + pair_width] = grad.astype(bf16)
        d_joint[:, 2 * width + at : 2 * width + at + pair_width] = nt(low, matrix[pair]).astype(bf16)
    low = d_joint[:, width:]
    key_sums[...] += col_sum(low.astype(f32))
    grad_normed = d_normed_q[...] + nt(low, weight[:, width:])
    scaled, inverse = norm_parts(hid[...])
    result = (d_middle[...] + norm_back(grad_normed, scaled, inverse, gain[...])).astype(bf16)
    result = result.astype(f32)
    sums[0:1, :] += col_sum(grad_normed * scaled)
    sums[1:2, :] += col_sum(grad_normed)
    sums[2:3, :] += col_sum(result)
    for k in range(plane // tile):

        @pl.when(step == k)
        def _():
            for i in range(tile):
                (g0, g1, g2, g3)[k * tile + i][...] = result[i * genes : (i + 1) * genes, :]


def d_key_call(ids, hidden, joint, phi, d_query, d_normed_q, d_middle, mine, other, back_matrix, weight, gain, factor, after=()):
    genes, width = hidden[0].shape
    tokens = plane * genes
    step = tile * genes
    pair_width = back_matrix.shape[1] // 2
    pairs = width // pair_width
    features = back_matrix.shape[0] // 2

    def rows(cols):
        return pl.BlockSpec((step, cols), lambda at, ids: (at, 0))

    ins = list(hidden) + [joint, phi, d_query, d_normed_q, d_middle, mine, other, back_matrix, weight, gain]
    in_specs = [whole(a.shape) for a in ins]
    for i in range(5):
        in_specs[plane + i] = rows(ins[plane + i].shape[1])
    outs = [(near((genes, width)), whole((genes, width)))] * plane + [
        (near((tokens, 3 * width), bf16), rows(3 * width)),
        (near((8, width)), whole((8, width))),
        (near((1, 2 * width)), whole((1, 2 * width))),
    ]
    return call(
        functools.partial(d_key_kernel, factor=factor),
        "key_gradient",
        (plane // tile,),
        in_specs,
        [o[0] for o in outs],
        [o[1] for o in outs],
        [
            pltpu.VMEM((pairs, pair_width, 2 * features), bf16),
            pltpu.VMEM((8, 2 * features), f32),
            pltpu.VMEM((step, width), f32),
        ],
        ids,
        *ins,
        after=after,
        mib=28,
    )


def put_shards(out, size, spot, where, first, count, per, rows, at, value):
    if rows % 8:
        out[at * size + first * rows : at * size + (first + count) * rows, :] = value
        return
    for s in range(count):
        to = (where(first + s) ^ spot) * per + at
        to = pl.multiple_of(to, 8)
        out[pl.ds(to, rows), :] = value[s * rows : (s + 1) * rows, :]


def in_slots(bundle, size, me, per, rows, order):
    if rows % 8 == 0:
        return bundle
    body = bundle[: size * per].reshape(per // rows, size, rows, -1).transpose(1, 0, 2, 3)
    place = placed(order, size.bit_length() - 1)
    owner = sorted(range(size), key=place)
    body = body[jnp.array(owner, jnp.int32) ^ me].reshape(size * per, -1)
    return jnp.concatenate([body, bundle[size * per :]], axis=0)


def side_of(sent):
    return (lambda ids: 1 - ids[1]) if sent else (lambda ids: ids[1])


def lower_weights_kernel(ids, a0, a1, c0, c1, out, *, size, where, spot_at):
    step = pl.program_id(0)
    part = size // 4
    rows = out.shape[0] // size
    value = tn(a0[...], c0[...]) + tn(a1[...], c1[...])
    for k in range(4):

        @pl.when(step == k)
        def _():
            put_shards(out, size, ids[spot_at], where, k * part, part, rows, rows, 0, value)


def lower_weights_call(ids, size, sent, where, spot_at, active, cot_low, after=()):
    tokens, wide = active[0].shape
    half = cot_low[0].shape[1] // 2
    side = side_of(sent)
    shape = (wide, half)
    return call(
        functools.partial(lower_weights_kernel, size=size, where=where, spot_at=spot_at),
        "lower_weights",
        (4,),
        [pl.BlockSpec((tokens, wide // 4), lambda at, ids: (0, at))] * 2
        + [pl.BlockSpec((tokens, half), lambda at, ids: (0, side(ids)))] * 2,
        near(shape),
        whole(shape),
        [],
        ids,
        *active,
        *cot_low,
        after=after,
        mib=16,
    )


def upper_weights_kernel(ids, n0, n1, u0, u1, t0, t1, b0, b1, out, *, size, where, spot_at):
    step = pl.program_id(0)
    part = size // 4
    rows = n0.shape[1] // size
    value = tn(n0[...], u0[...]) + tn(n1[...], u1[...])
    last = tn(t0[...], b0[...]) + tn(t1[...], b1[...])
    for k in range(4):

        @pl.when(step == k)
        def _():
            put_shards(out, size, ids[spot_at], where, 0, size, 5 * rows, rows, k * rows, value)
            put_shards(out, size, ids[spot_at], where, k * part, part, 5 * rows, rows, 4 * rows, last)


def upper_weights_call(ids, size, sent, where, spot_at, normed, d_upper, attention, d_branch, after=()):
    tokens, width = normed[0].shape
    half = width // 2
    side = side_of(sent)
    shape = (5 * width, half)
    return call(
        functools.partial(upper_weights_kernel, size=size, where=where, spot_at=spot_at),
        "upper_weights",
        (4,),
        [pl.BlockSpec((tokens, width), lambda at, ids: (0, 0))] * 2
        + [pl.BlockSpec((tokens, half), lambda at, ids: (0, side(ids) * 4 + at))] * 2
        + [pl.BlockSpec((tokens, width // 4), lambda at, ids: (0, at))] * 2
        + [pl.BlockSpec((tokens, half), lambda at, ids: (0, side(ids)))] * 2,
        near(shape),
        whole(shape),
        [],
        ids,
        *normed,
        *d_upper,
        *attention,
        *d_branch,
        after=after,
        mib=16,
    )


def joint_weights_kernel(ids, n0, n1, j0, j1, out, *, size, where, spot_at):
    step = pl.program_id(0)
    rows = n0.shape[1] // size
    value = tn(n0[...], j0[...]) + tn(n1[...], j1[...])
    for k in range(3):

        @pl.when(step == k)
        def _():
            put_shards(out, size, ids[spot_at], where, 0, size, 3 * rows, rows, k * rows, value)


def joint_weights_call(ids, size, sent, where, spot_at, normed, d_joint, after=()):
    tokens, width = normed[0].shape
    half = width // 2
    side = side_of(sent)
    shape = (3 * width, half)
    return call(
        functools.partial(joint_weights_kernel, size=size, where=where, spot_at=spot_at),
        "joint_weights",
        (3,),
        [pl.BlockSpec((tokens, width), lambda at, ids: (0, 0))] * 2
        + [pl.BlockSpec((tokens, half), lambda at, ids: (0, side(ids) * 3 + at))] * 2,
        near(shape),
        whole(shape),
        [],
        ids,
        *normed,
        *d_joint,
        after=after,
        mib=14,
    )


vector_rows = 32


def input_weights_kernel(ids, *refs, size, where, spot_at):
    own = refs[:2]
    merged = refs[2:5]
    r0, r1, v0, v1, f0, f1, u0, u1, k0, k1, q0, q1, s0, s1, d_low, sent, kept, zero_hidden = refs[5:]
    pieces = [own[j] if r == 0 else merged[r - 1].at[j] for r in range(plane) for j in range(2)]
    genes, width = own[0].shape
    half = width // 2
    rows = (sent.shape[0] - vector_rows) // size
    total = None
    for i, piece in enumerate(pieces):
        wide = piece[...]
        d_low[i * genes : (i + 1) * genes, :] = wide.astype(bf16)
        masked = wide * (v0, v1)[i % 2][i // 2][:, :1]
        total = masked if total is None else total + masked
    zero_hidden[...] = total
    parts = [f0[0:4, :] + f1[0:4, :], s0[0:3, :] + s1[0:3, :], q0[...] + q1[...], k0[...] + k1[...], u0[...] + u1[...]]
    for out, side in ((sent, 1 - ids[1]), (kept, ids[1])):
        value = None
        for i in range(8):
            chosen = (r0, r1)[i % 2][i // 2]
            lo = d_low[i * genes : (i + 1) * genes, :half]
            hi = d_low[i * genes : (i + 1) * genes, half:]
            product = tn(chosen, jnp.where(side == 0, lo, hi))
            value = product if value is None else value + product
        put_shards(out, size, ids[spot_at], where, 0, size, rows, rows, 0, value)
        at = size * rows
        for part in parts:
            for row in range(part.shape[0]):
                for c in range(part.shape[1] // half):
                    out[at : at + 1, :] = part[row : row + 1, c * half : (c + 1) * half]
                    at += 1
        out[at:, :] = jnp.zeros((out.shape[0] - at, half), f32)


def input_weights_call(ids, size, where, spot_at, own, came, rows, vacant, sums, after=()):
    genes, width = own[0].shape
    width_in = rows[0].shape[2]
    ins = [*own, *came, *rows, *vacant, *sums]
    shape = (width_in + vector_rows, width // 2)
    outs = [near((8 * genes, width), bf16), free(shape), near(shape), free((genes, width))]
    return call(
        functools.partial(input_weights_kernel, size=size, where=where, spot_at=spot_at),
        "input_weights",
        (1,),
        [whole(a.shape) for a in ins],
        outs,
        [whole(o.shape) for o in outs],
        [],
        ids,
        *ins,
        after=after,
        mib=28,
    )


def out_kernel(ids, *refs):
    out = refs[-1]
    merged = refs[-plane:-1]
    group = len(refs) - plane
    for j in range(group):
        out[ids[2] * group + j] = refs[j][...].astype(bf16)
        for r in range(1, plane):
            out[(ids[2] ^ r) * group + j] = merged[r - 1][j].astype(bf16)


def out_call(ids, own, came, after=()):
    genes, width = own[0].shape
    shape = (plane * len(own), genes, width)
    ins = [*own, *came]
    return call(
        out_kernel,
        "block_out",
        (1,),
        [whole(p.shape) for p in ins],
        far(shape, bf16),
        whole(shape),
        [],
        ids,
        *ins,
        after=after,
        mib=14,
    )


def token_kernel(ids, d_low, index, weight, token_grad):
    slots, _ = index.shape
    width = d_low.shape[1]
    genes = d_low.shape[0] // 8
    slot = lax.broadcasted_iota(jnp.int32, (slots, 1), 0)
    picked = jnp.zeros((slots, width), f32)
    gene = lax.broadcasted_iota(jnp.int32, (slots, genes), 1)
    match = (index[...] - ids[0] * genes) == gene
    for i in range(8):
        cell = i ^ (2 * ids[2])
        here = (slot >= ids[8 + cell]) & (slot < ids[9 + cell])
        chosen = jnp.where(match & here, 1.0, 0.0).astype(bf16)
        picked = picked + nn(chosen, d_low[i * genes : (i + 1) * genes, :])
    token_grad[0] = nt(picked.astype(bf16), weight[...])


def token_call(ids, d_low, index, weight, after=()):
    ins = [d_low, index, weight]
    shape = (1, index.shape[0], weight.shape[0])
    return call(
        token_kernel,
        "token_gradient",
        (1,),
        [whole(a.shape) for a in ins],
        far(shape),
        whole(shape),
        [],
        ids,
        *ins,
        after=after,
        mib=24,
    )


def zero_kernel(ids, mine, other, weight, out):
    total = mine[...] + other[...]
    high = total.astype(bf16)
    rest = total - high.astype(f32)
    low = rest.astype(bf16)
    out[...] = nt(high, weight[...]) + nt(low, weight[...])


def zero_call(ids, mine, other, weight, after=()):
    genes, width = mine.shape
    ins = [mine, other, weight]
    shape = (genes, weight.shape[0])
    return call(
        zero_kernel,
        "zero_gradient",
        (1,),
        [whole(a.shape) for a in ins],
        far(shape),
        whole(shape),
        [],
        ids,
        *ins,
        after=after,
        mib=12,
    )


def local(
    encoder_packed_tokens,
    token_gene_index,
    cell_counts,
    zero_embed,
    random_features,
    input_weight,
    input_bias,
    first_gain,
    first_shift,
    joint_weight,
    joint_bias,
    output_weight,
    output_bias,
    second_gain,
    second_shift,
    upper_weight,
    upper_bias,
    lower_weight,
    lower_bias,
    cotangent,
):
    placed_at.clear()
    size = lax.axis_size("gene")
    me = lax.axis_index("gene")
    core = lax.axis_index("cell")
    cells_here, genes, width = cotangent.shape
    head_size, features = random_features.shape
    heads = width // head_size
    factor = head_size ** (-0.25)
    group = cells_here // plane
    log = size.bit_length() - 1
    rest = list(range(3, log))
    orders = ([2, 0, 1] + rest, [2, 0, 1] + rest, [1, 0, 2] + rest, [0, 1, 2] + rest)
    where = [placed(order, log) for order in orders]
    ends = jnp.cumsum(cell_counts[0]).astype(jnp.int32)
    ids = jnp.concatenate(
        [
            jnp.stack([me, core, me % plane, (me // plane) % 2]).astype(jnp.int32),
            jnp.stack([placed(order, log)(me) for order in orders]).astype(jnp.int32),
            jnp.zeros((1,), jnp.int32),
            ends,
        ]
    )
    nothing = jnp.zeros((head_size, features), bf16)
    minus = jnp.full((head_size, features), -1.0, bf16)
    feats = jnp.concatenate(
        [
            jnp.concatenate([random_features, nothing], axis=1),
            jnp.concatenate([nothing, random_features], axis=1),
            jnp.concatenate([minus, nothing], axis=1),
            jnp.concatenate([nothing, minus], axis=1),
        ],
        axis=0,
    )
    back_matrix = jnp.concatenate([feats[: 2 * head_size].T, -feats[2 * head_size :].T], axis=1)

    def row(vector):
        return vector.reshape(1, -1)

    high = [1 << b for b in range(2, log)]
    last = ()

    def then(made, token, *more):
        nonlocal last
        last = (token, *more)
        return made

    def gene_swap(value, bit):
        return swap(value, "gene", size, bit)

    def out_and_in(blocks):
        return [block if r == 0 else gene_swap(block, r) for r, block in enumerate(blocks)]

    class Halves:
        def __init__(self, mine, sent):
            self.mine = mine
            self.came = gene_swap(sent, high[0])
            self.left = high[1:]

        def add(self):
            self.mine = add_call(ids, self.mine, self.came, after=last)
            then(None, self.mine)
            if self.left:
                self.came = gene_swap(self.mine, self.left.pop(0))
            else:
                self.other = gene_swap(self.mine, high[0])

        def coming(self):
            return getattr(self, "other", self.came)

        def finish(self):
            while not hasattr(self, "other"):
                self.add()
            return self.mine, self.other

    class Scatter:
        def __init__(self, sent, kept, order, rows, extra=0):
            per = (kept.shape[0] - extra) // size
            self.mine = in_slots(kept, size, me, per, rows, order)
            self.came = swap(in_slots(sent, size, me, per, rows, order), "cell", 2, 1)
            self.order = list(order)
            self.extra = extra

        def add(self):
            if self.order:
                self.mine, send = split_call(ids, self.mine, self.came, self.extra, after=last)
                then(None, self.mine)
                self.came = gene_swap(send, 1 << self.order.pop(0))
            else:
                self.mine = add_call(ids, self.mine, self.came, after=last)
                then(None, self.mine)
                self.done = True

        def finish(self):
            while not hasattr(self, "done"):
                self.add()
            return self.mine

    shard = width // size
    wide_shard = upper_weight.shape[1] // size
    in_shard = input_weight.shape[0] // size
    hidden, rows, vacant = [], [], []
    for j in range(group):
        made = rows_call(
            ids, j, group, encoder_packed_tokens[0], token_gene_index, zero_embed, input_weight, row(input_bias),
            after=last,
        )
        hidden.append(out_and_in(made[:plane]))
        rows.append(made[plane])
        vacant.append(made[plane + 1])
        then(None, made[plane + 1])
    normed, joint, key_phi, sums = [], [], [], []

    def keys_of(j):
        made = key_call(
            ids, hidden[j], joint_weight, row(joint_bias), row(first_gain), row(first_shift), feats, factor,
            after=last,
        )
        normed.append(made[0])
        joint.append(made[1])
        key_phi.append(made[2])
        sums.append(Halves(made[3], made[4]))
        then(None, made[0])

    query_phi = []

    def query_of(j):
        query_phi.append(query_call(ids, joint[j], feats, factor, after=last))
        then(None, query_phi[j])

    keys_of(0)
    w_up, w_low, w_out, w_joint = hold_call(
        ids, upper_weight, lower_weight, output_weight, joint_weight, after=last
    )
    then(None, w_out)
    sums[0].add()
    then(None, *last, *hidden[1][1:])
    wide = cotangent_call(ids, group, cotangent, after=last)
    then(None, wide[0])
    cots = out_and_in(wide)
    keys_of(1)
    sums[0].add()
    sums[1].add()
    query_of(0)
    query_of(1)
    then(None, *last, *cots[1:])
    sums[1].finish()
    sums = [s.finish() for s in sums]
    fed, d_sums = [], []
    for j in range(group):
        made = feed_call(
            ids, j, hidden[j], cots, query_phi[j], *sums[j], w_out, row(output_bias), row(second_gain),
            row(second_shift), w_up, row(upper_bias), w_low, row(lower_bias), heads,
            after=last,
        )
        fed.append(made)
        d_sums.append(Halves(made[plane + 8], made[plane + 9]))
        then(None, made[plane + 2])
    active, d_upper, normed_two, attention, d_middle, d_branch, d_num, cot_low, _, _, sums_two, up_sums = list(
        zip(*fed)
    )[plane:]
    queries = []

    def d_query_of(j):
        queries.append(
            d_query_call(
                ids, d_num[j], query_phi[j], joint[j], *sums[j], back_matrix, w_joint, factor, after=last
            )
        )
        then(None, queries[j][1])

    def lower_of(sent):
        made = lower_weights_call(ids, size, sent, where[0], 4, active, cot_low, after=last)
        return then(made, made)

    def upper_of(sent):
        made = upper_weights_call(
            ids, size, sent, where[1], 5, normed_two, d_upper, attention, d_branch, after=last
        )
        return then(made, made)

    def joint_of(sent):
        made = joint_weights_call(ids, size, sent, where[2], 6, normed, d_joint, after=last)
        return then(made, made)

    def pass_on(*arrays):
        made = pass_call(ids, *arrays, after=last)
        then(None, made[0])
        return made

    def release(blocks):
        sent = release_call(ids, [block[r] for block in blocks for r in range(1, plane)], after=last)
        then(None, sent[0])
        return [gene_swap(block, r) for r, block in enumerate(sent, 1)]

    keys = []

    def d_key_of(j):
        made = d_key_call(
            ids, hidden[j], joint[j], key_phi[j], queries[j][0], queries[j][1], d_middle[j], *d_sums[j].finish(),
            back_matrix, w_joint, row(first_gain), factor,
            after=last,
        )
        keys.append(made)
        then(None, made[plane])

    back_out = release([made[:plane] for made in fed])
    d_sums[0].add()
    d_query_of(0)
    lower_sent = lower_of(True)
    d_sums[1].add()
    d_query_of(1)
    lower_kept = lower_of(False)
    d_sums[0].add()
    upper_sent = upper_of(True)
    upper_kept = upper_of(False)
    d_sums[1].add()
    then(None, *last, *back_out, d_sums[0].coming())
    lower_sent, upper_sent = pass_on(lower_sent, upper_sent)
    lower_sum = Scatter(lower_sent, lower_kept, orders[0], wide_shard)
    upper_sum = Scatter(upper_sent, upper_kept, orders[1], shard)
    d_key_of(0)
    d_key_of(1)
    backs = release([k[:plane] for k in keys])
    upper_sum.add()
    d_joint = [k[plane] for k in keys]
    joint_sent = joint_of(True)
    joint_kept = joint_of(False)
    block_out = out_call(ids, [made[0] for made in fed], back_out, after=last)
    then(None, block_out)
    sums_one = [k[plane + 1] for k in keys]
    key_sums = [k[plane + 2] for k in keys]
    query_sums = [q[2] for q in queries]
    then(None, *last, upper_sum.came, *backs)
    (joint_sent,) = pass_on(joint_sent)
    joint_sum = Scatter(joint_sent, joint_kept, orders[2], shard)
    d_low, input_sent, input_kept, zero_hidden = input_weights_call(
        ids, size, where[3], 7, [k[0] for k in keys], backs, rows, vacant,
        [*sums_two, *up_sums, *key_sums, *query_sums, *sums_one],
        after=last,
    )
    then(None, zero_hidden)
    input_sum = Scatter(input_sent, input_kept, orders[3], in_shard, vector_rows)
    zero_came = swap(zero_hidden, "cell", 2, 1)
    joint_sum.add()
    upper_sum.add()
    lower_sum.add()
    input_sum.add()
    token_grad = token_call(ids, d_low, token_gene_index.reshape(-1, 1), input_weight, after=last)
    then(None, token_grad)
    zero_grad = zero_call(ids, zero_hidden, zero_came, input_weight, after=last)
    then(None, zero_grad)
    upper_sum.add()
    input_sum.add()
    joint_sum.add()
    lower_sum.add()
    input_sum.add()
    upper_sum.add()
    joint_sum.add()
    lower_sum.add()
    input_sum.add()
    upper_sum.finish()
    joint_sum.add()
    lower_sum.add()
    input_sum.finish()
    joint_sum.finish()
    lower_sum.finish()

    def both_halves(mine):
        other = swap(mine, "cell", 2, 1)
        return jnp.where(core == 0, mine, other), jnp.where(core == 0, other, mine)

    def opened(pair, at, count, groups):
        parts = [b[at + g * count : at + (g + 1) * count] for b in pair for g in range(groups)]
        return jnp.concatenate(parts, axis=1)

    lower_pair = both_halves(lower_sum.mine)
    upper_pair = both_halves(upper_sum.mine)
    g_lower = opened(lower_pair, 0, wide_shard, 1)
    g_upper = opened(upper_pair, 0, shard, 4)
    g_output = opened(upper_pair, 4 * shard, shard, 1)
    g_joint = opened(both_halves(joint_sum.mine), 0, shard, 3)
    g_input = opened(both_halves(input_sum.mine[:in_shard]), 0, in_shard, 1)
    flat = input_sum.mine[in_shard:].reshape(-1)
    lengths = [width] * 7 + [3 * width, upper_weight.shape[1]]
    found = []
    at = 0
    for length in lengths:
        part = length // size
        found.append(lax.dynamic_slice(flat, (at + me * part,), (part,)))
        at += length
    small_out = [found[i] for i in (6, 4, 5, 7, 2, 0, 1, 8, 3)]
    return (
        block_out,
        token_grad,
        zero_grad,
        g_input,
        small_out[0],
        small_out[1],
        small_out[2],
        g_joint,
        small_out[3],
        g_output,
        small_out[4],
        small_out[5],
        small_out[6],
        g_upper,
        small_out[7],
        g_lower,
        small_out[8],
    )


def solution(mesh):
    return jax.shard_map(
        local,
        mesh=mesh,
        in_specs=(
            P("cell", "gene", None),
            P("cell", "gene"),
            P("cell", "gene"),
            P("gene", None),
            P(),
            P(),
            P(),
            P(),
            P(),
            P(),
            P(),
            P(),
            P(),
            P(),
            P(),
            P(),
            P(),
            P(),
            P(),
            P("cell", "gene", None),
        ),
        out_specs=(
            P("cell", "gene", None),
            P("cell", "gene", None),
            P("gene", None),
            P("gene", None),
            P("gene"),
            P("gene"),
            P("gene"),
            P("gene", None),
            P("gene"),
            P("gene", None),
            P("gene"),
            P("gene"),
            P("gene"),
            P("gene", None),
            P("gene"),
            P("gene", None),
            P("gene"),
        ),
        check_vma=False,
    )
```

```python
import functools
import math

import jax
import jax.numpy as jnp
from jax import lax
from jax.experimental import pallas as pl
from jax.experimental.pallas import tpu as pltpu
from jax.sharding import PartitionSpec as P

epsilon = 1e-05
f32 = jnp.float32
bf16 = jnp.bfloat16
plane = 4
tile = 4


def nn(left, right):
    return jnp.dot(left, right, preferred_element_type=f32)


def nt(left, right):
    return lax.dot_general(left, right, (((1,), (1,)), ((), ())), preferred_element_type=f32)


def tn(left, right):
    return lax.dot_general(left, right, (((0,), (0,)), ((), ())), preferred_element_type=f32)


def col_sum(values):
    return jnp.sum(values, axis=0, keepdims=True)


def norm_parts(values):
    centred = values - jnp.mean(values, axis=-1, keepdims=True)
    inverse = lax.rsqrt(jnp.mean(centred * centred, axis=-1, keepdims=True) + epsilon)
    return centred * inverse, inverse


def norm_back(grad_in, scaled, inverse, gain):
    weighted = grad_in * gain
    return inverse * (
        weighted
        - jnp.mean(weighted, axis=-1, keepdims=True)
        - scaled * jnp.mean(weighted * scaled, axis=-1, keepdims=True)
    )


def whole(shape):
    return pl.BlockSpec(shape, lambda *at: (0,) * len(shape))


placed_at = []


def near(shape, dtype=f32):
    return pltpu.VMEM(shape, dtype)


def far(shape, dtype=f32):
    return pltpu.HBM(shape, dtype)


def free(shape, dtype=f32):
    return jax.ShapeDtypeStruct(shape, dtype)


def placed(order, log):
    return lambda number: sum(((number >> bit) & 1) << (log - 1 - i) for i, bit in enumerate(order))


def call(kernel, name, grid, in_specs, outs, out_specs, scratch, *args, after=(), mib=60):
    first = 1 + len(in_specs)

    def body(*refs):
        kernel(*refs[:first], *refs[first + len(after) :])

    def held(array):
        for other, space in placed_at:
            if array is other:
                return pltpu.with_memory_space_constraint(array, space)
        return array

    made = pl.pallas_call(
        body,
        name=name,
        grid_spec=pltpu.PrefetchScalarGridSpec(
            num_scalar_prefetch=1,
            grid=grid,
            in_specs=list(in_specs) + [pl.BlockSpec(memory_space=pl.ANY)] * len(after),
            out_specs=out_specs,
            scratch_shapes=scratch,
        ),
        out_shape=outs,
        compiler_params=pltpu.CompilerParams(
            vmem_limit_bytes=mib << 20, dimension_semantics=("arbitrary",) * len(grid)
        ),
        cost_estimate=pl.CostEstimate(flops=1000, bytes_accessed=1000, transcendentals=0),
    )(args[0], *(held(a) for a in args[1:]), *(held(a) for a in after))
    several = isinstance(outs, (list, tuple))
    for out, array in zip(outs if several else [outs], made if several else [made]):
        if getattr(out, "memory_space", None) in (pltpu.VMEM, pltpu.HBM):
            placed_at.append((array, out.memory_space))
    return made


def swap(value, axis, size, bit):
    return lax.ppermute(value, axis, [(i, i ^ bit) for i in range(size)])


def rows_kernel(ids, tokens, index, zero, weight, bias, h0, h1, h2, h3, rows_out, vacant_out, *, group, j):
    genes = zero.shape[0]
    first_gene = ids[0] * genes
    slots = index.shape[1]
    slot = lax.broadcasted_iota(jnp.int32, (genes, slots), 1)
    gene = lax.broadcasted_iota(jnp.int32, (genes, slots), 0)
    match = (index[...] - first_gene) == gene
    for r in (3, 1, 2, 0):
        cell = (ids[2] ^ r) * group + j
        here = match & (slot >= ids[8 + cell]) & (slot < ids[9 + cell])
        chosen = jnp.where(here, 1.0, 0.0)
        vacant = 1.0 - jnp.sum(chosen, axis=1, keepdims=True)
        rows = nn(chosen.astype(bf16), tokens[...]) + vacant * zero[...].astype(f32)
        rows = rows.astype(bf16)
        rows_out[r] = rows
        vacant_out[r] = jnp.broadcast_to(vacant, (genes, 128))
        (h0, h1, h2, h3)[r][...] = nn(rows, weight[...]) + bias[...]


def rows_call(ids, j, group, tokens, index, zero, weight, bias, after=()):
    tokens, index, zero, weight = (
        pltpu.with_memory_space_constraint(a, pltpu.HBM) for a in (tokens, index, zero, weight)
    )
    genes, width_in = zero.shape
    width = weight.shape[1]
    outs = [free((genes, width))] * plane + [
        far((plane, genes, width_in), bf16),
        far((plane, genes, 128)),
    ]
    ins = [tokens, index, zero, weight, bias]
    return call(
        functools.partial(rows_kernel, group=group, j=j),
        "gene_rows",
        (1,),
        [whole(a.shape) for a in ins],
        outs,
        [whole(o.shape) for o in outs],
        [],
        ids,
        *ins,
        after=after,
        mib=20,
    )


def cotangent_kernel(ids, cot, c0, c1, c2, c3):
    for r, out in enumerate((c0, c1, c2, c3)):
        for j in range(out.shape[0]):
            out[j] = cot[(ids[2] ^ r) * out.shape[0] + j].astype(f32)


def cotangent_call(ids, group, cot, after=()):
    _, genes, width = cot.shape
    outs = [free((group, genes, width))] * plane
    return call(
        cotangent_kernel,
        "wide_cotangent",
        (1,),
        [whole(cot.shape)],
        outs,
        [whole(o.shape) for o in outs],
        [],
        ids,
        cot,
        after=after,
        mib=14,
    )


def pass_kernel(ids, *refs):
    count = len(refs) // 2
    for given, out in zip(refs[:count], refs[count:]):
        out[...] = given[...]


def pass_call(ids, *arrays, after=()):
    return call(
        pass_kernel,
        "pass_on",
        (1,),
        [whole(a.shape) for a in arrays],
        [free(a.shape, a.dtype) for a in arrays],
        [whole(a.shape) for a in arrays],
        [],
        ids,
        *arrays,
        after=after,
        mib=16,
    )


def release_kernel(ids, *refs):
    outs = refs[-(plane - 1) :]
    for i, piece in enumerate(refs[: -(plane - 1)]):
        outs[i % (plane - 1)][i // (plane - 1)] = piece[...]


def release_call(ids, pieces, after=()):
    genes, width = pieces[0].shape
    outs = [free((len(pieces) // (plane - 1), genes, width))] * (plane - 1)
    return call(
        release_kernel,
        "release",
        (1,),
        [whole(p.shape) for p in pieces],
        outs,
        [whole(o.shape) for o in outs],
        [],
        ids,
        *pieces,
        after=after,
        mib=14,
    )


def hold_kernel(ids, *refs):
    count = len(refs) // 2
    for given, held in zip(refs[:count], refs[count:]):
        held[...] = given[...]


def hold_call(ids, *arrays, after=()):
    outs = [near(a.shape, a.dtype) for a in arrays]
    return call(
        hold_kernel,
        "hold",
        (1,),
        [whole(a.shape) for a in arrays],
        outs,
        [whole(a.shape) for a in arrays],
        [],
        ids,
        *arrays,
        after=after,
        mib=12,
    )


def add_kernel(ids, mine, came, out):
    out[...] = mine[...] + came[...]


def add_call(ids, mine, came, out=free, after=()):
    return call(
        add_kernel,
        "add",
        (1,),
        [whole(mine.shape)] * 2,
        out(mine.shape),
        whole(mine.shape),
        [],
        ids,
        mine,
        came,
        after=after,
        mib=8,
    )


def split_kernel(ids, mine, came, keep, send, *, extra):
    half = keep.shape[0] - extra
    keep[:half, :] = mine[:half, :] + came[:half, :]
    send[:half, :] = mine[half : 2 * half, :] + came[half : 2 * half, :]
    if extra:
        both = mine[2 * half :, :] + came[2 * half :, :]
        keep[half:, :] = both
        send[half:, :] = both


def split_call(ids, mine, came, extra=0, after=()):
    rows, cols = mine.shape
    shape = ((rows - extra) // 2 + extra, cols)
    return call(
        functools.partial(split_kernel, extra=extra),
        "add_halves",
        (1,),
        [whole(mine.shape)] * 2,
        [near(shape), free(shape)],
        [whole(shape)] * 2,
        [],
        ids,
        mine,
        came,
        after=after,
        mib=16,
    )


def phi_of(u, feature_matrix, factor):
    features = feature_matrix.shape[1] // 2
    wide = u.astype(f32)
    square = (wide * wide * (0.5 * factor)).astype(bf16)
    power = nn(jnp.concatenate([u, square], axis=1), feature_matrix[...])
    scale = factor * math.log2(math.e)
    return jnp.exp2(power * scale - 0.5 * math.log2(features)).astype(bf16)


def put_summary(out, pair, pairs, both, totals, head_size, features):
    half = pair // (pairs // 2)
    at = (pair % (pairs // 2)) * 2
    base = pairs * head_size
    for i in range(2):
        cols = slice(i * features, (i + 1) * features)
        out[half, (at + i) * head_size : (at + i + 1) * head_size, :] = both[
            i * head_size : (i + 1) * head_size, cols
        ]
        out[half, base + at + i : base + at + i + 1, :] = totals[i][:, cols]


def block_matrix(matrix, mine, other, flip, pairs, head_size, features, with_totals):
    base = pairs * head_size
    for pair in range(pairs):
        half = pair // (pairs // 2)
        at = (pair % (pairs // 2)) * 2
        first = (flip ^ half) == 0

        def take(lo, hi):
            return jnp.where(first, mine[lo:hi, :], other[lo:hi, :])

        nothing = jnp.zeros((head_size, features), bf16)
        for i in range(2):
            rows = slice(i * head_size, (i + 1) * head_size)
            part = take((at + i) * head_size, (at + i + 1) * head_size).astype(bf16)
            matrix[pair, rows, i * features : (i + 1) * features] = part
            matrix[pair, rows, (1 - i) * features : (2 - i) * features] = nothing
            if with_totals:
                rows = slice((2 + i) * head_size, (3 + i) * head_size)
                total = take(base + at + i, base + at + i + 1)
                spread = jnp.broadcast_to(total, (head_size, features)).astype(bf16)
                matrix[pair, rows, i * features : (i + 1) * features] = spread
                matrix[pair, rows, (1 - i) * features : (2 - i) * features] = nothing


def payload_shape(heads, head_size, features):
    rows = heads // 2 * head_size + heads // 2
    return (rows + (-rows) % 8, features)


def key_kernel(
    ids, h0, h1, h2, h3, weight, bias, gain, shift, feats, normed, joint, phi, mine, sent, out, *, factor
):
    genes, width = h0.shape
    features = feats.shape[1] // 2
    pair_width = feats.shape[0] // 2
    pairs = width // pair_width
    for r, block in enumerate((h0, h1, h2, h3)):
        scaled, _ = norm_parts(block[...])
        normed[r * genes : (r + 1) * genes, :] = (scaled * gain[...] + shift[...]).astype(bf16)
    for part in (1, 2, 0):
        cols = slice(part * width, (part + 1) * width)
        joint[:, cols] = (nn(normed[...], weight[:, cols]) + bias[:, cols]).astype(bf16)
    rows_used = pairs * (pair_width // 2) + pairs
    spare = out.shape[1] - rows_used
    if spare:
        for i in range(2):
            out[i, rows_used:, :] = jnp.zeros((spare, features), f32)
    for pair in range(pairs):
        at = width + pair * pair_width
        low = phi_of(joint[:, at : at + pair_width], feats, factor)
        phi[:, pair * 2 * features : (pair + 1) * 2 * features] = low
        value = joint[:, width + at : width + at + pair_width]
        total = col_sum(low.astype(f32))
        put_summary(out, pair, pairs, tn(value, low), (total, total), pair_width // 2, features)
    mine[...] = out[ids[3]]
    sent[...] = out[1 - ids[3]]


def key_call(ids, hidden, weight, bias, gain, shift, feats, factor, after=()):
    genes, width = hidden[0].shape
    tokens = plane * genes
    features = feats.shape[1] // 2
    heads = 2 * width // (feats.shape[0] // 2)
    pay = payload_shape(heads, width // heads, features)
    outs = [
        far((tokens, width), bf16),
        near((tokens, 3 * width), bf16),
        far((tokens, heads * features), bf16),
        near(pay),
        free(pay),
    ]
    ins = list(hidden) + [weight, bias, gain, shift, feats]
    return call(
        functools.partial(key_kernel, factor=factor),
        "key_summary",
        (1,),
        [whole(a.shape) for a in ins],
        outs,
        [whole(o.shape) for o in outs],
        [pltpu.VMEM((2, *pay), f32)],
        ids,
        *ins,
        after=after,
        mib=24,
    )


def query_kernel(ids, joint, feats, phi, *, factor):
    features = feats.shape[1] // 2
    pair_width = feats.shape[0] // 2
    for pair in range(joint.shape[1] // pair_width):
        u = joint[:, pair * pair_width : (pair + 1) * pair_width]
        phi[:, pair * 2 * features : (pair + 1) * 2 * features] = phi_of(u, feats, factor)


def query_call(ids, joint, feats, factor, after=()):
    tokens, wide = joint.shape
    width = wide // 3
    features = feats.shape[1] // 2
    heads = 2 * width // (feats.shape[0] // 2)
    step = tokens // 2
    return call(
        functools.partial(query_kernel, factor=factor),
        "query_features",
        (2,),
        [pl.BlockSpec((step, width), lambda at, ids: (at, 0)), whole(feats.shape)],
        near((tokens, heads * features), bf16),
        pl.BlockSpec((step, heads * features), lambda at, ids: (at, 0)),
        [],
        ids,
        joint,
        feats,
        after=after,
        mib=16,
    )


def gelu_parts(x):
    expo = jnp.exp2(x * x * (-0.5 * math.log2(math.e)))
    t = 1.0 / (1.0 + (0.3275911 * math.sqrt(0.5)) * jnp.abs(x))
    poly = t * (
        0.5 * 0.254829592
        + t
        * (
            0.5 * -0.284496736
            + t * (0.5 * 1.421413741 + t * (0.5 * -1.453152027 + t * (0.5 * 1.061405429)))
        )
    )
    tail = poly * expo
    return jnp.where(x > 0, 1.0 - tail, tail), expo * 0.3989422804014327


def feed_kernel(
    ids, h0, h1, h2, h3, c0, c1, c2, c3, phi, mine, other, w_out, b_out, gain, shift, w_up, b_up, w_low, b_low,
    g0, g1, g2, g3, active, d_upper, normed, attention, d_middle, d_branch, d_num, cot_low, mine_out, sent_out, sums, up_sums,
    pay, matrix, att_wide, recip, scaled_ref, back, result,
):
    genes, width = h0.shape
    pairs = matrix.shape[0]
    features = phi.shape[1] // pairs // 2
    pair_width = width // pairs
    head_size = pair_width // 2
    chunk = 1024
    blocks = [slice(r * genes, (r + 1) * genes) for r in range(plane)]
    block_matrix(matrix, mine, other, ids[3], pairs, head_size, features, True)
    for rows, block in zip(blocks, (c0, c1, c2, c3)):
        cot_low[rows, :] = block[...].astype(bf16)
    for pair in range(pairs):
        cols = slice(pair * pair_width, (pair + 1) * pair_width)
        both = nt(phi[:, pair * 2 * features : (pair + 1) * 2 * features], matrix[pair])
        inverse = 1.0 / both[:, pair_width:]
        quotient = both[:, :pair_width] * inverse
        att_wide[:, cols] = quotient
        recip[:, cols] = inverse
        attention[:, cols] = quotient.astype(bf16)
    result[...] = nn(attention[...], w_out[...]) + b_out[...]
    for rows, block in zip(blocks, (h0, h1, h2, h3)):
        mid = block[...] + result[rows, :]
        result[rows, :] = mid + b_low[...]
        scaled, inverse = norm_parts(mid)
        scaled_ref[rows, :] = scaled
        normed[rows, :] = (scaled * gain[...] + shift[...]).astype(bf16)
        back[rows, :] = jnp.broadcast_to(inverse, scaled.shape)
    d_middle[...] = back[...]
    for at in range(w_up.shape[1] // chunk):
        cols = slice(at * chunk, (at + 1) * chunk)
        upper = nn(normed[...], w_up[:, cols]) + b_up[:, cols]
        grad_active = nt(cot_low[...], w_low[cols, :])
        cumulative, density = gelu_parts(upper)
        active[:, cols] = (upper * cumulative).astype(bf16)
        low = (grad_active * (cumulative + upper * density)).astype(bf16)
        d_upper[:, cols] = low
        up_sums[:, cols] = col_sum(low.astype(f32))
        if at == 0:
            back[...] = nt(low, w_up[:, cols])
        else:
            back[...] += nt(low, w_up[:, cols])
        result[...] += nn(active[:, cols], w_low[cols, :])
    for rows, block in zip(blocks, (g0, g1, g2, g3)):
        block[...] = result[rows, :]
    grad_normed = back[...]
    scaled = scaled_ref[...]
    cot = cot_low[...].astype(f32)
    grad_mid = cot + norm_back(grad_normed, scaled, d_middle[...], gain[...])
    d_middle[...] = grad_mid
    branch = grad_mid.astype(bf16)
    d_branch[...] = branch
    sums[0:1, :] = col_sum(grad_normed * scaled)
    sums[1:2, :] = col_sum(grad_normed)
    sums[2:3, :] = col_sum(branch.astype(f32))
    sums[3:4, :] = col_sum(cot)
    sums[4:, :] = jnp.zeros((sums.shape[0] - 4, width), f32)
    back[...] = nt(branch, w_out[...])
    row = lax.broadcasted_iota(jnp.int32, (2 * pair_width, pair_width), 0) // head_size % 2
    col = lax.broadcasted_iota(jnp.int32, (2 * pair_width, pair_width), 1) // head_size
    ones = jnp.where(row == col, 1.0, 0.0).astype(bf16)
    rows_used = pairs * head_size + pairs
    spare = pay.shape[1] - rows_used
    if spare:
        for i in range(2):
            pay[i, rows_used:, :] = jnp.zeros((spare, features), f32)
    for pair in range(pairs):
        cols = slice(pair * pair_width, (pair + 1) * pair_width)
        grad = back[:, cols]
        inverse = recip[:, cols]
        product = grad * att_wide[:, cols]
        high = product.astype(bf16)
        low = (product - high.astype(f32)).astype(bf16)
        total = nn(jnp.concatenate([high, low], axis=1), ones)
        at = pair * 2 * pair_width
        d_num[:, at : at + pair_width] = (grad * inverse).astype(bf16)
        d_num[:, at + pair_width : at + 2 * pair_width] = (
            total * inverse * (-1.0 / head_size)
        ).astype(bf16)
        both = tn(
            d_num[:, at : at + 2 * pair_width],
            phi[:, pair * 2 * features : (pair + 1) * 2 * features],
        )
        totals = [
            both[pair_width + i * head_size : pair_width + i * head_size + 1, :] * float(head_size)
            for i in range(2)
        ]
        put_summary(pay, pair, pairs, both, totals, head_size, features)
    mine_out[...] = pay[ids[3]]
    sent_out[...] = pay[1 - ids[3]]


def feed_call(
    ids, j, hidden, cots, phi, mine, other, w_out, b_out, gain, shift, w_up, b_up, w_low, b_low, heads, after=()
):
    genes, width = hidden[0].shape
    tokens = plane * genes
    step = tokens
    features = phi.shape[1] // heads
    wide = w_up.shape[1]
    pairs = heads // 2
    pay = payload_shape(heads, width // heads, features)

    def rows(cols):
        return pl.BlockSpec((step, cols), lambda at, ids: (at, 0))

    ins = list(hidden) + list(cots) + [phi, mine, other, w_out, b_out, gain, shift, w_up, b_up, w_low, b_low]
    in_specs = [whole(a.shape) for a in ins]
    in_specs[2 * plane] = rows(phi.shape[1])
    for r in range(plane):
        in_specs[plane + r] = pl.BlockSpec((None, genes, width), lambda at, ids: (j, 0, 0))
    outs = [(near((genes, width)), whole((genes, width)))] * plane + [
        (near((tokens, wide), bf16), rows(wide)),
        (near((tokens, wide), bf16), rows(wide)),
        (near((tokens, width), bf16), rows(width)),
        (near((tokens, width), bf16), rows(width)),
        (far((tokens, width)), rows(width)),
        (far((tokens, width), bf16), rows(width)),
        (near((tokens, 2 * width), bf16), rows(2 * width)),
        (far((tokens, width), bf16), rows(width)),
        (near(pay), whole(pay)),
        (free(pay), whole(pay)),
        (near((8, width)), whole((8, width))),
        (near((1, wide)), whole((1, wide))),
    ]
    return call(
        feed_kernel,
        "feed_forward",
        (1,),
        in_specs,
        [o[0] for o in outs],
        [o[1] for o in outs],
        [
            pltpu.VMEM((2, *pay), f32),
            pltpu.VMEM((pairs, 2 * width // pairs, 2 * features), bf16),
        ]
        + [pltpu.VMEM((step, width), f32)] * 5,
        ids,
        *ins,
        after=after,
        mib=22,
    )


def feature_back(grad_feat, phi, u, back_matrix, factor):
    pair_width = u.shape[1]
    low = (grad_feat * phi.astype(f32) * factor).astype(bf16)
    both = nn(low, back_matrix[...])
    return both[:, :pair_width] - factor * u.astype(f32) * both[:, pair_width:]


def d_query_kernel(ids, d_num, phi, query, mine, other, back_matrix, weight, d_query, d_normed, sums, matrix, *, factor):
    step = pl.program_id(0)
    pairs = matrix.shape[0]
    features = phi.shape[1] // pairs // 2
    width = query.shape[1]
    pair_width = width // pairs

    @pl.when(step == 0)
    def _():
        block_matrix(matrix, mine, other, ids[3], pairs, pair_width // 2, features, True)
        sums[...] = jnp.zeros_like(sums)

    for pair in range(pairs):
        cols = slice(pair * pair_width, (pair + 1) * pair_width)
        grad_feat = nn(d_num[:, pair * 2 * pair_width : (pair + 1) * 2 * pair_width], matrix[pair])
        grad = feature_back(
            grad_feat,
            phi[:, pair * 2 * features : (pair + 1) * 2 * features],
            query[:, cols],
            back_matrix,
            factor,
        )
        d_query[:, cols] = grad.astype(bf16)
    low = d_query[...]
    d_normed[...] = nt(low, weight[...])
    sums[...] += col_sum(low.astype(f32))


def d_query_call(ids, d_num, phi, joint, mine, other, back_matrix, weight, factor, after=()):
    tokens = joint.shape[0]
    width = joint.shape[1] // 3
    pair_width = back_matrix.shape[1] // 2
    pairs = width // pair_width
    step = tokens // plane * tile
    features = back_matrix.shape[0] // 2

    def rows(cols):
        return pl.BlockSpec((step, cols), lambda at, ids: (at, 0))

    return call(
        functools.partial(d_query_kernel, factor=factor),
        "query_gradient",
        (plane // tile,),
        [
            rows(2 * width),
            rows(phi.shape[1]),
            rows(width),
            whole(mine.shape),
            whole(other.shape),
            whole(back_matrix.shape),
            whole((width, width)),
        ],
        [near((tokens, width), bf16), near((tokens, width)), near((1, width))],
        [rows(width), rows(width), whole((1, width))],
        [pltpu.VMEM((pairs, 2 * pair_width, 2 * features), bf16)],
        ids,
        d_num,
        phi,
        joint,
        mine,
        other,
        back_matrix,
        weight,
        after=after,
        mib=20,
    )


def d_key_kernel(
    ids, h0, h1, h2, h3, joint, phi, d_query, d_normed_q, d_middle, mine, other, back_matrix, weight, gain,
    g0, g1, g2, g3, d_joint, sums, key_sums, matrix, total_ref, hid, *, factor,
):
    step = pl.program_id(0)
    pairs = matrix.shape[0]
    genes, width = h0.shape
    features = phi.shape[1] // pairs // 2
    pair_width = width // pairs
    head_size = pair_width // 2

    @pl.when(step == 0)
    def _():
        block_matrix(matrix, mine, other, ids[3], pairs, head_size, features, False)
        base = pairs * head_size
        for pair in range(pairs):
            half = pair // (pairs // 2)
            at = base + (pair % (pairs // 2)) * 2
            first = (ids[3] ^ half) == 0
            for i in range(2):
                total_ref[pair : pair + 1, i * features : (i + 1) * features] = jnp.where(
                    first, mine[at + i : at + i + 1, :], other[at + i : at + i + 1, :]
                )
        sums[...] = jnp.zeros_like(sums)
        key_sums[...] = jnp.zeros_like(key_sums)

    for k in range(plane // tile):

        @pl.when(step == k)
        def _():
            for i in range(tile):
                hid[i * genes : (i + 1) * genes, :] = (h0, h1, h2, h3)[k * tile + i][...]

    d_joint[:, :width] = d_query[...]
    for pair in range(pairs):
        at = pair * pair_width
        value = joint[:, 2 * width + at : 2 * width + at + pair_width]
        low = phi[:, pair * 2 * features : (pair + 1) * 2 * features]
        grad_feat = nn(value, matrix[pair]) + total_ref[pair : pair + 1, :]
        grad = feature_back(
            grad_feat, low, joint[:, width + at : width + at + pair_width], back_matrix, factor
        )
        d_joint[:, width + at : width + at + pair_width] = grad.astype(bf16)
        d_joint[:, 2 * width + at : 2 * width + at + pair_width] = nt(low, matrix[pair]).astype(bf16)
    low = d_joint[:, width:]
    key_sums[...] += col_sum(low.astype(f32))
    grad_normed = d_normed_q[...] + nt(low, weight[:, width:])
    scaled, inverse = norm_parts(hid[...])
    result = (d_middle[...] + norm_back(grad_normed, scaled, inverse, gain[...])).astype(bf16)
    result = result.astype(f32)
    sums[0:1, :] += col_sum(grad_normed * scaled)
    sums[1:2, :] += col_sum(grad_normed)
    sums[2:3, :] += col_sum(result)
    for k in range(plane // tile):

        @pl.when(step == k)
        def _():
            for i in range(tile):
                (g0, g1, g2, g3)[k * tile + i][...] = result[i * genes : (i + 1) * genes, :]


def d_key_call(ids, hidden, joint, phi, d_query, d_normed_q, d_middle, mine, other, back_matrix, weight, gain, factor, after=()):
    genes, width = hidden[0].shape
    tokens = plane * genes
    step = tile * genes
    pair_width = back_matrix.shape[1] // 2
    pairs = width // pair_width
    features = back_matrix.shape[0] // 2

    def rows(cols):
        return pl.BlockSpec((step, cols), lambda at, ids: (at, 0))

    ins = list(hidden) + [joint, phi, d_query, d_normed_q, d_middle, mine, other, back_matrix, weight, gain]
    in_specs = [whole(a.shape) for a in ins]
    for i in range(5):
        in_specs[plane + i] = rows(ins[plane + i].shape[1])
    outs = [(near((genes, width)), whole((genes, width)))] * plane + [
        (near((tokens, 3 * width), bf16), rows(3 * width)),
        (near((8, width)), whole((8, width))),
        (near((1, 2 * width)), whole((1, 2 * width))),
    ]
    return call(
        functools.partial(d_key_kernel, factor=factor),
        "key_gradient",
        (plane // tile,),
        in_specs,
        [o[0] for o in outs],
        [o[1] for o in outs],
        [
            pltpu.VMEM((pairs, pair_width, 2 * features), bf16),
            pltpu.VMEM((8, 2 * features), f32),
            pltpu.VMEM((step, width), f32),
        ],
        ids,
        *ins,
        after=after,
        mib=28,
    )


def put_shards(out, size, spot, where, first, count, per, rows, at, value):
    if rows % 8:
        out[at * size + first * rows : at * size + (first + count) * rows, :] = value
        return
    for s in range(count):
        to = (where(first + s) ^ spot) * per + at
        to = pl.multiple_of(to, 8)
        out[pl.ds(to, rows), :] = value[s * rows : (s + 1) * rows, :]


def in_slots(bundle, size, me, per, rows, order):
    if rows % 8 == 0:
        return bundle
    body = bundle[: size * per].reshape(per // rows, size, rows, -1).transpose(1, 0, 2, 3)
    place = placed(order, size.bit_length() - 1)
    owner = sorted(range(size), key=place)
    body = body[jnp.array(owner, jnp.int32) ^ me].reshape(size * per, -1)
    return jnp.concatenate([body, bundle[size * per :]], axis=0)


def side_of(sent):
    return (lambda ids: 1 - ids[1]) if sent else (lambda ids: ids[1])


def lower_weights_kernel(ids, a0, a1, c0, c1, out, *, size, where, spot_at):
    step = pl.program_id(0)
    part = size // 4
    rows = out.shape[0] // size
    value = tn(a0[...], c0[...]) + tn(a1[...], c1[...])
    for k in range(4):

        @pl.when(step == k)
        def _():
            put_shards(out, size, ids[spot_at], where, k * part, part, rows, rows, 0, value)


def lower_weights_call(ids, size, sent, where, spot_at, active, cot_low, after=()):
    tokens, wide = active[0].shape
    half = cot_low[0].shape[1] // 2
    side = side_of(sent)
    shape = (wide, half)
    return call(
        functools.partial(lower_weights_kernel, size=size, where=where, spot_at=spot_at),
        "lower_weights",
        (4,),
        [pl.BlockSpec((tokens, wide // 4), lambda at, ids: (0, at))] * 2
        + [pl.BlockSpec((tokens, half), lambda at, ids: (0, side(ids)))] * 2,
        near(shape),
        whole(shape),
        [],
        ids,
        *active,
        *cot_low,
        after=after,
        mib=16,
    )


def upper_weights_kernel(ids, n0, n1, u0, u1, t0, t1, b0, b1, out, *, size, where, spot_at):
    step = pl.program_id(0)
    part = size // 4
    rows = n0.shape[1] // size
    value = tn(n0[...], u0[...]) + tn(n1[...], u1[...])
    last = tn(t0[...], b0[...]) + tn(t1[...], b1[...])
    for k in range(4):

        @pl.when(step == k)
        def _():
            put_shards(out, size, ids[spot_at], where, 0, size, 5 * rows, rows, k * rows, value)
            put_shards(out, size, ids[spot_at], where, k * part, part, 5 * rows, rows, 4 * rows, last)


def upper_weights_call(ids, size, sent, where, spot_at, normed, d_upper, attention, d_branch, after=()):
    tokens, width = normed[0].shape
    half = width // 2
    side = side_of(sent)
    shape = (5 * width, half)
    return call(
        functools.partial(upper_weights_kernel, size=size, where=where, spot_at=spot_at),
        "upper_weights",
        (4,),
        [pl.BlockSpec((tokens, width), lambda at, ids: (0, 0))] * 2
        + [pl.BlockSpec((tokens, half), lambda at, ids: (0, side(ids) * 4 + at))] * 2
        + [pl.BlockSpec((tokens, width // 4), lambda at, ids: (0, at))] * 2
        + [pl.BlockSpec((tokens, half), lambda at, ids: (0, side(ids)))] * 2,
        near(shape),
        whole(shape),
        [],
        ids,
        *normed,
        *d_upper,
        *attention,
        *d_branch,
        after=after,
        mib=16,
    )


def joint_weights_kernel(ids, n0, n1, j0, j1, out, *, size, where, spot_at):
    step = pl.program_id(0)
    rows = n0.shape[1] // size
    value = tn(n0[...], j0[...]) + tn(n1[...], j1[...])
    for k in range(3):

        @pl.when(step == k)
        def _():
            put_shards(out, size, ids[spot_at], where, 0, size, 3 * rows, rows, k * rows, value)


def joint_weights_call(ids, size, sent, where, spot_at, normed, d_joint, after=()):
    tokens, width = normed[0].shape
    half = width // 2
    side = side_of(sent)
    shape = (3 * width, half)
    return call(
        functools.partial(joint_weights_kernel, size=size, where=where, spot_at=spot_at),
        "joint_weights",
        (3,),
        [pl.BlockSpec((tokens, width), lambda at, ids: (0, 0))] * 2
        + [pl.BlockSpec((tokens, half), lambda at, ids: (0, side(ids) * 3 + at))] * 2,
        near(shape),
        whole(shape),
        [],
        ids,
        *normed,
        *d_joint,
        after=after,
        mib=14,
    )


vector_rows = 32


def input_weights_kernel(ids, *refs, size, where, spot_at):
    own = refs[:2]
    merged = refs[2:5]
    r0, r1, v0, v1, f0, f1, u0, u1, k0, k1, q0, q1, s0, s1, d_low, sent, kept, zero_hidden = refs[5:]
    pieces = [own[j] if r == 0 else merged[r - 1].at[j] for r in range(plane) for j in range(2)]
    genes, width = own[0].shape
    half = width // 2
    rows = (sent.shape[0] - vector_rows) // size
    total = None
    for i, piece in enumerate(pieces):
        wide = piece[...]
        d_low[i * genes : (i + 1) * genes, :] = wide.astype(bf16)
        masked = wide * (v0, v1)[i % 2][i // 2][:, :1]
        total = masked if total is None else total + masked
    zero_hidden[...] = total
    parts = [f0[0:4, :] + f1[0:4, :], s0[0:3, :] + s1[0:3, :], q0[...] + q1[...], k0[...] + k1[...], u0[...] + u1[...]]
    for out, side in ((sent, 1 - ids[1]), (kept, ids[1])):
        value = None
        for i in range(8):
            chosen = (r0, r1)[i % 2][i // 2]
            lo = d_low[i * genes : (i + 1) * genes, :half]
            hi = d_low[i * genes : (i + 1) * genes, half:]
            product = tn(chosen, jnp.where(side == 0, lo, hi))
            value = product if value is None else value + product
        put_shards(out, size, ids[spot_at], where, 0, size, rows, rows, 0, value)
        at = size * rows
        for part in parts:
            for row in range(part.shape[0]):
                for c in range(part.shape[1] // half):
                    out[at : at + 1, :] = part[row : row + 1, c * half : (c + 1) * half]
                    at += 1
        out[at:, :] = jnp.zeros((out.shape[0] - at, half), f32)


def input_weights_call(ids, size, where, spot_at, own, came, rows, vacant, sums, after=()):
    genes, width = own[0].shape
    width_in = rows[0].shape[2]
    ins = [*own, *came, *rows, *vacant, *sums]
    shape = (width_in + vector_rows, width // 2)
    outs = [near((8 * genes, width), bf16), free(shape), near(shape), free((genes, width))]
    return call(
        functools.partial(input_weights_kernel, size=size, where=where, spot_at=spot_at),
        "input_weights",
        (1,),
        [whole(a.shape) for a in ins],
        outs,
        [whole(o.shape) for o in outs],
        [],
        ids,
        *ins,
        after=after,
        mib=28,
    )


def finish_kernel(ids, *refs, parts):
    first_core = ids[1] == 0
    outs = refs[-len(parts) :]
    for out, (bundle, rows, groups, at) in zip(outs, parts):
        mine, came = refs[2 * bundle : 2 * bundle + 2]
        half = mine.shape[1]
        for g in range(groups):
            one = mine[at + g * rows : at + (g + 1) * rows, :]
            two = came[at + g * rows : at + (g + 1) * rows, :]
            out[:, g * half : (g + 1) * half] = jnp.where(first_core, one, two)
            out[:, (groups + g) * half : (groups + g + 1) * half] = jnp.where(first_core, two, one)


def finish_call(ids, bundles, parts, after=()):
    ins = [array for pair in bundles for array in pair]
    half = ins[0].shape[1]
    outs = [far((rows, 2 * groups * half)) for _, rows, groups, _ in parts]
    return call(
        functools.partial(finish_kernel, parts=parts),
        "weight_results",
        (1,),
        [whole(a.shape) for a in ins],
        outs,
        [whole(o.shape) for o in outs],
        [],
        ids,
        *ins,
        after=after,
        mib=12,
    )


def out_kernel(ids, *refs):
    out = refs[-1]
    merged = refs[-plane:-1]
    group = len(refs) - plane
    for j in range(group):
        out[ids[2] * group + j] = refs[j][...].astype(bf16)
        for r in range(1, plane):
            out[(ids[2] ^ r) * group + j] = merged[r - 1][j].astype(bf16)


def out_call(ids, own, came, after=()):
    genes, width = own[0].shape
    shape = (plane * len(own), genes, width)
    ins = [*own, *came]
    return call(
        out_kernel,
        "block_out",
        (1,),
        [whole(p.shape) for p in ins],
        far(shape, bf16),
        whole(shape),
        [],
        ids,
        *ins,
        after=after,
        mib=14,
    )


def token_kernel(ids, d_low, index, weight, token_grad):
    slots, _ = index.shape
    width = d_low.shape[1]
    genes = d_low.shape[0] // 8
    slot = lax.broadcasted_iota(jnp.int32, (slots, 1), 0)
    picked = jnp.zeros((slots, width), f32)
    gene = lax.broadcasted_iota(jnp.int32, (slots, genes), 1)
    match = (index[...] - ids[0] * genes) == gene
    for i in range(8):
        cell = i ^ (2 * ids[2])
        here = (slot >= ids[8 + cell]) & (slot < ids[9 + cell])
        chosen = jnp.where(match & here, 1.0, 0.0).astype(bf16)
        picked = picked + nn(chosen, d_low[i * genes : (i + 1) * genes, :])
    token_grad[0] = nt(picked.astype(bf16), weight[...])


def token_call(ids, d_low, index, weight, after=()):
    ins = [d_low, index, weight]
    shape = (1, index.shape[0], weight.shape[0])
    return call(
        token_kernel,
        "token_gradient",
        (1,),
        [whole(a.shape) for a in ins],
        far(shape),
        whole(shape),
        [],
        ids,
        *ins,
        after=after,
        mib=24,
    )


def zero_kernel(ids, mine, other, weight, out):
    total = mine[...] + other[...]
    high = total.astype(bf16)
    rest = total - high.astype(f32)
    low = rest.astype(bf16)
    out[...] = nt(high, weight[...]) + nt(low, weight[...])


def zero_call(ids, mine, other, weight, after=()):
    genes, width = mine.shape
    ins = [mine, other, weight]
    shape = (genes, weight.shape[0])
    return call(
        zero_kernel,
        "zero_gradient",
        (1,),
        [whole(a.shape) for a in ins],
        far(shape),
        whole(shape),
        [],
        ids,
        *ins,
        after=after,
        mib=12,
    )


def local(
    encoder_packed_tokens,
    token_gene_index,
    cell_counts,
    zero_embed,
    random_features,
    input_weight,
    input_bias,
    first_gain,
    first_shift,
    joint_weight,
    joint_bias,
    output_weight,
    output_bias,
    second_gain,
    second_shift,
    upper_weight,
    upper_bias,
    lower_weight,
    lower_bias,
    cotangent,
):
    placed_at.clear()
    size = lax.axis_size("gene")
    me = lax.axis_index("gene")
    core = lax.axis_index("cell")
    cells_here, genes, width = cotangent.shape
    head_size, features = random_features.shape
    heads = width // head_size
    factor = head_size ** (-0.25)
    group = cells_here // plane
    log = size.bit_length() - 1
    rest = list(range(3, log))
    orders = ([2, 0, 1] + rest, [2, 0, 1] + rest, [1, 0, 2] + rest, [0, 1, 2] + rest)
    where = [placed(order, log) for order in orders]
    ends = jnp.cumsum(cell_counts[0]).astype(jnp.int32)
    ids = jnp.concatenate(
        [
            jnp.stack([me, core, me % plane, (me // plane) % 2]).astype(jnp.int32),
            jnp.stack([placed(order, log)(me) for order in orders]).astype(jnp.int32),
            jnp.zeros((1,), jnp.int32),
            ends,
        ]
    )
    nothing = jnp.zeros((head_size, features), bf16)
    minus = jnp.full((head_size, features), -1.0, bf16)
    feats = jnp.concatenate(
        [
            jnp.concatenate([random_features, nothing], axis=1),
            jnp.concatenate([nothing, random_features], axis=1),
            jnp.concatenate([minus, nothing], axis=1),
            jnp.concatenate([nothing, minus], axis=1),
        ],
        axis=0,
    )
    back_matrix = jnp.concatenate([feats[: 2 * head_size].T, -feats[2 * head_size :].T], axis=1)

    def row(vector):
        return vector.reshape(1, -1)

    high = [1 << b for b in range(2, log)]
    last = ()

    def then(made, token, *more):
        nonlocal last
        last = (token, *more)
        return made

    def gene_swap(value, bit):
        return swap(value, "gene", size, bit)

    def out_and_in(blocks):
        return [block if r == 0 else gene_swap(block, r) for r, block in enumerate(blocks)]

    class Halves:
        def __init__(self, mine, sent):
            self.mine = mine
            self.came = gene_swap(sent, high[0])
            self.left = high[1:]

        def add(self):
            self.mine = add_call(ids, self.mine, self.came, after=last)
            then(None, self.mine)
            if self.left:
                self.came = gene_swap(self.mine, self.left.pop(0))
            else:
                self.other = gene_swap(self.mine, high[0])

        def coming(self):
            return getattr(self, "other", self.came)

        def finish(self):
            while not hasattr(self, "other"):
                self.add()
            return self.mine, self.other

    class Scatter:
        def __init__(self, sent, kept, order, rows, extra=0):
            per = (kept.shape[0] - extra) // size
            self.mine = in_slots(kept, size, me, per, rows, order)
            self.came = swap(in_slots(sent, size, me, per, rows, order), "cell", 2, 1)
            self.order = list(order)
            self.extra = extra

        def add(self):
            if self.order:
                self.mine, send = split_call(ids, self.mine, self.came, self.extra, after=last)
                then(None, self.mine)
                self.came = gene_swap(send, 1 << self.order.pop(0))

        def close(self):
            while self.order:
                self.add()
            self.mine = add_call(ids, self.mine, self.came, after=last)
            then(None, self.mine)
            self.other = swap(self.mine, "cell", 2, 1)

    shard = width // size
    wide_shard = upper_weight.shape[1] // size
    in_shard = input_weight.shape[0] // size
    hidden, rows, vacant = [], [], []
    for j in range(group):
        made = rows_call(
            ids, j, group, encoder_packed_tokens[0], token_gene_index, zero_embed, input_weight, row(input_bias),
            after=last,
        )
        hidden.append(out_and_in(made[:plane]))
        rows.append(made[plane])
        vacant.append(made[plane + 1])
        then(None, made[plane + 1])
    normed, joint, key_phi, sums = [], [], [], []

    def keys_of(j):
        made = key_call(
            ids, hidden[j], joint_weight, row(joint_bias), row(first_gain), row(first_shift), feats, factor,
            after=last,
        )
        normed.append(made[0])
        joint.append(made[1])
        key_phi.append(made[2])
        sums.append(Halves(made[3], made[4]))
        then(None, made[0])

    query_phi = []

    def query_of(j):
        query_phi.append(query_call(ids, joint[j], feats, factor, after=last))
        then(None, query_phi[j])

    keys_of(0)
    w_up, w_low, w_out, w_joint = hold_call(
        ids, upper_weight, lower_weight, output_weight, joint_weight, after=last
    )
    then(None, w_out)
    sums[0].add()
    then(None, *last, *hidden[1][1:])
    wide = cotangent_call(ids, group, cotangent, after=last)
    then(None, wide[0])
    cots = out_and_in(wide)
    keys_of(1)
    sums[0].add()
    sums[1].add()
    query_of(0)
    query_of(1)
    then(None, *last, *cots[1:])
    sums[1].finish()
    sums = [s.finish() for s in sums]
    fed, d_sums = [], []
    for j in range(group):
        made = feed_call(
            ids, j, hidden[j], cots, query_phi[j], *sums[j], w_out, row(output_bias), row(second_gain),
            row(second_shift), w_up, row(upper_bias), w_low, row(lower_bias), heads,
            after=last,
        )
        fed.append(made)
        d_sums.append(Halves(made[plane + 8], made[plane + 9]))
        then(None, made[plane + 2])
    active, d_upper, normed_two, attention, d_middle, d_branch, d_num, cot_low, _, _, sums_two, up_sums = list(
        zip(*fed)
    )[plane:]
    queries = []

    def d_query_of(j):
        queries.append(
            d_query_call(
                ids, d_num[j], query_phi[j], joint[j], *sums[j], back_matrix, w_joint, factor, after=last
            )
        )
        then(None, queries[j][1])

    def lower_of(sent):
        made = lower_weights_call(ids, size, sent, where[0], 4, active, cot_low, after=last)
        return then(made, made)

    def upper_of(sent):
        made = upper_weights_call(
            ids, size, sent, where[1], 5, normed_two, d_upper, attention, d_branch, after=last
        )
        return then(made, made)

    def joint_of(sent):
        made = joint_weights_call(ids, size, sent, where[2], 6, normed, d_joint, after=last)
        return then(made, made)

    def pass_on(*arrays):
        made = pass_call(ids, *arrays, after=last)
        then(None, made[0])
        return made

    def release(blocks):
        sent = release_call(ids, [block[r] for block in blocks for r in range(1, plane)], after=last)
        then(None, sent[0])
        return [gene_swap(block, r) for r, block in enumerate(sent, 1)]

    keys = []

    def d_key_of(j):
        made = d_key_call(
            ids, hidden[j], joint[j], key_phi[j], queries[j][0], queries[j][1], d_middle[j], *d_sums[j].finish(),
            back_matrix, w_joint, row(first_gain), factor,
            after=last,
        )
        keys.append(made)
        then(None, made[plane])

    back_out = release([made[:plane] for made in fed])
    d_sums[0].add()
    d_query_of(0)
    d_sums[1].add()
    d_query_of(1)
    upper_sent = upper_of(True)
    d_sums[0].add()
    upper_kept = upper_of(False)
    d_sums[1].add()
    then(None, *last, *back_out, d_sums[0].coming())
    (upper_sent,) = pass_on(upper_sent)
    upper_sum = Scatter(upper_sent, upper_kept, orders[1], shard)
    d_key_of(0)
    d_key_of(1)
    backs = release([k[:plane] for k in keys])
    upper_sum.add()
    d_joint = [k[plane] for k in keys]
    joint_sent = joint_of(True)
    joint_kept = joint_of(False)
    lower_sent = lower_of(True)
    lower_kept = lower_of(False)
    block_out = out_call(ids, [made[0] for made in fed], back_out, after=last)
    then(None, block_out)
    sums_one = [k[plane + 1] for k in keys]
    key_sums = [k[plane + 2] for k in keys]
    query_sums = [q[2] for q in queries]
    then(None, *last, upper_sum.came, *backs)
    joint_sent, lower_sent = pass_on(joint_sent, lower_sent)
    lower_sum = Scatter(lower_sent, lower_kept, orders[0], wide_shard)
    joint_sum = Scatter(joint_sent, joint_kept, orders[2], shard)
    d_low, input_sent, input_kept, zero_hidden = input_weights_call(
        ids, size, where[3], 7, [k[0] for k in keys], backs, rows, vacant,
        [*sums_two, *up_sums, *key_sums, *query_sums, *sums_one],
        after=last,
    )
    then(None, zero_hidden)
    input_sum = Scatter(input_sent, input_kept, orders[3], in_shard, vector_rows)
    zero_came = swap(zero_hidden, "cell", 2, 1)
    joint_sum.add()
    upper_sum.add()
    lower_sum.add()
    input_sum.add()
    token_grad = token_call(ids, d_low, token_gene_index.reshape(-1, 1), input_weight, after=last)
    then(None, token_grad)
    zero_grad = zero_call(ids, zero_hidden, zero_came, input_weight, after=last)
    then(None, zero_grad)
    upper_sum.add()
    joint_sum.add()
    lower_sum.add()
    input_sum.add()
    upper_sum.add()
    input_sum.add()
    input_sum.add()
    upper_sum.close()
    joint_sum.add()
    lower_sum.add()
    input_sum.close()
    joint_sum.add()
    lower_sum.add()
    joint_sum.close()
    lower_sum.close()
    g_lower, g_upper, g_output, g_joint, g_input = finish_call(
        ids,
        [(b.mine, b.other) for b in (lower_sum, upper_sum, joint_sum, input_sum)],
        [
            (0, wide_shard, 1, 0),
            (1, shard, 4, 0),
            (1, shard, 1, 4 * shard),
            (2, shard, 3, 0),
            (3, in_shard, 1, 0),
        ],
        after=last,
    )
    flat = input_sum.mine[in_shard:].reshape(-1)
    lengths = [width] * 7 + [3 * width, upper_weight.shape[1]]
    found = []
    at = 0
    for length in lengths:
        part = length // size
        found.append(lax.dynamic_slice(flat, (at + me * part,), (part,)))
        at += length
    small_out = [found[i] for i in (6, 4, 5, 7, 2, 0, 1, 8, 3)]
    return (
        block_out,
        token_grad,
        zero_grad,
        g_input,
        small_out[0],
        small_out[1],
        small_out[2],
        g_joint,
        small_out[3],
        g_output,
        small_out[4],
        small_out[5],
        small_out[6],
        g_upper,
        small_out[7],
        g_lower,
        small_out[8],
    )


def solution(mesh):
    return jax.shard_map(
        local,
        mesh=mesh,
        in_specs=(
            P("cell", "gene", None),
            P("cell", "gene"),
            P("cell", "gene"),
            P("gene", None),
            P(),
            P(),
            P(),
            P(),
            P(),
            P(),
            P(),
            P(),
            P(),
            P(),
            P(),
            P(),
            P(),
            P(),
            P(),
            P("cell", "gene", None),
        ),
        out_specs=(
            P("cell", "gene", None),
            P("cell", "gene", None),
            P("gene", None),
            P("gene", None),
            P("gene"),
            P("gene"),
            P("gene"),
            P("gene", None),
            P("gene"),
            P("gene", None),
            P("gene"),
            P("gene"),
            P("gene"),
            P("gene", None),
            P("gene"),
            P("gene", None),
            P("gene"),
        ),
        check_vma=False,
    )
```

```python
import functools
import math

import jax
import jax.numpy as jnp
from jax import lax
from jax.experimental import pallas as pl
from jax.experimental.pallas import tpu as pltpu
from jax.sharding import PartitionSpec as P

epsilon = 1e-05
f32 = jnp.float32
bf16 = jnp.bfloat16
plane = 4
tile = 4


def nn(left, right):
    return jnp.dot(left, right, preferred_element_type=f32)


def nt(left, right):
    return lax.dot_general(left, right, (((1,), (1,)), ((), ())), preferred_element_type=f32)


def tn(left, right):
    return lax.dot_general(left, right, (((0,), (0,)), ((), ())), preferred_element_type=f32)


def col_sum(values):
    return jnp.sum(values, axis=0, keepdims=True)


def norm_parts(values):
    centred = values - jnp.mean(values, axis=-1, keepdims=True)
    inverse = lax.rsqrt(jnp.mean(centred * centred, axis=-1, keepdims=True) + epsilon)
    return centred * inverse, inverse


def norm_back(grad_in, scaled, inverse, gain):
    weighted = grad_in * gain
    return inverse * (
        weighted
        - jnp.mean(weighted, axis=-1, keepdims=True)
        - scaled * jnp.mean(weighted * scaled, axis=-1, keepdims=True)
    )


def whole(shape):
    return pl.BlockSpec(shape, lambda *at: (0,) * len(shape))


placed_at = []


def near(shape, dtype=f32):
    return pltpu.VMEM(shape, dtype)


def far(shape, dtype=f32):
    return pltpu.HBM(shape, dtype)


def free(shape, dtype=f32):
    return jax.ShapeDtypeStruct(shape, dtype)


def placed(order, log):
    return lambda number: sum(((number >> bit) & 1) << (log - 1 - i) for i, bit in enumerate(order))


def call(kernel, name, grid, in_specs, outs, out_specs, scratch, *args, after=(), mib=60):
    first = 1 + len(in_specs)

    def body(*refs):
        kernel(*refs[:first], *refs[first + len(after) :])

    def held(array):
        for other, space in placed_at:
            if array is other:
                return pltpu.with_memory_space_constraint(array, space)
        return array

    made = pl.pallas_call(
        body,
        name=name,
        grid_spec=pltpu.PrefetchScalarGridSpec(
            num_scalar_prefetch=1,
            grid=grid,
            in_specs=list(in_specs) + [pl.BlockSpec(memory_space=pl.ANY)] * len(after),
            out_specs=out_specs,
            scratch_shapes=scratch,
        ),
        out_shape=outs,
        compiler_params=pltpu.CompilerParams(
            vmem_limit_bytes=mib << 20, dimension_semantics=("arbitrary",) * len(grid)
        ),
        cost_estimate=pl.CostEstimate(flops=1000, bytes_accessed=1000, transcendentals=0),
    )(args[0], *(held(a) for a in args[1:]), *(held(a) for a in after))
    several = isinstance(outs, (list, tuple))
    for out, array in zip(outs if several else [outs], made if several else [made]):
        if getattr(out, "memory_space", None) in (pltpu.VMEM, pltpu.HBM):
            placed_at.append((array, out.memory_space))
    return made


def swap(value, axis, size, bit):
    return lax.ppermute(value, axis, [(i, i ^ bit) for i in range(size)])


def rows_kernel(ids, tokens, index, zero, weight, bias, h0, h1, h2, h3, rows_out, vacant_out, *, group, j):
    genes = zero.shape[0]
    first_gene = ids[0] * genes
    slots = index.shape[1]
    slot = lax.broadcasted_iota(jnp.int32, (genes, slots), 1)
    gene = lax.broadcasted_iota(jnp.int32, (genes, slots), 0)
    match = (index[...] - first_gene) == gene
    for r in (3, 1, 2, 0):
        cell = (ids[2] ^ r) * group + j
        here = match & (slot >= ids[8 + cell]) & (slot < ids[9 + cell])
        chosen = jnp.where(here, 1.0, 0.0)
        vacant = 1.0 - jnp.sum(chosen, axis=1, keepdims=True)
        rows = nn(chosen.astype(bf16), tokens[...]) + vacant * zero[...].astype(f32)
        rows = rows.astype(bf16)
        rows_out[r] = rows
        vacant_out[r] = jnp.broadcast_to(vacant, (genes, 128))
        (h0, h1, h2, h3)[r][...] = nn(rows, weight[...]) + bias[...]


def rows_call(ids, j, group, tokens, index, zero, weight, bias, after=()):
    tokens, index, zero, weight = (
        pltpu.with_memory_space_constraint(a, pltpu.HBM) for a in (tokens, index, zero, weight)
    )
    genes, width_in = zero.shape
    width = weight.shape[1]
    outs = [free((genes, width))] * plane + [
        far((plane, genes, width_in), bf16),
        far((plane, genes, 128)),
    ]
    ins = [tokens, index, zero, weight, bias]
    return call(
        functools.partial(rows_kernel, group=group, j=j),
        "gene_rows",
        (1,),
        [whole(a.shape) for a in ins],
        outs,
        [whole(o.shape) for o in outs],
        [],
        ids,
        *ins,
        after=after,
        mib=20,
    )


def cotangent_kernel(ids, cot, c0, c1, c2, c3, *, group, j):
    for r, out in enumerate((c0, c1, c2, c3)):
        out[...] = cot[(ids[2] ^ r) * group + j].astype(f32)


def cotangent_call(ids, j, group, cot, after=()):
    _, genes, width = cot.shape
    outs = [free((genes, width))] * plane
    return call(
        functools.partial(cotangent_kernel, group=group, j=j),
        "wide_cotangent",
        (1,),
        [whole(cot.shape)],
        outs,
        [whole(o.shape) for o in outs],
        [],
        ids,
        cot,
        after=after,
        mib=14,
    )


def pass_kernel(ids, *refs):
    count = len(refs) // 2
    for given, out in zip(refs[:count], refs[count:]):
        out[...] = given[...]


def pass_call(ids, *arrays, after=()):
    return call(
        pass_kernel,
        "pass_on",
        (1,),
        [whole(a.shape) for a in arrays],
        [free(a.shape, a.dtype) for a in arrays],
        [whole(a.shape) for a in arrays],
        [],
        ids,
        *arrays,
        after=after,
        mib=16,
    )


def release_kernel(ids, *refs):
    outs = refs[-(plane - 1) :]
    for i, piece in enumerate(refs[: -(plane - 1)]):
        outs[i % (plane - 1)][i // (plane - 1)] = piece[...]


def release_call(ids, pieces, after=()):
    genes, width = pieces[0].shape
    outs = [free((len(pieces) // (plane - 1), genes, width))] * (plane - 1)
    return call(
        release_kernel,
        "release",
        (1,),
        [whole(p.shape) for p in pieces],
        outs,
        [whole(o.shape) for o in outs],
        [],
        ids,
        *pieces,
        after=after,
        mib=14,
    )


def hold_kernel(ids, *refs):
    count = len(refs) // 2
    for given, held in zip(refs[:count], refs[count:]):
        held[...] = given[...]


def hold_call(ids, *arrays, after=()):
    outs = [near(a.shape, a.dtype) for a in arrays]
    return call(
        hold_kernel,
        "hold",
        (1,),
        [whole(a.shape) for a in arrays],
        outs,
        [whole(a.shape) for a in arrays],
        [],
        ids,
        *arrays,
        after=after,
        mib=12,
    )


def add_kernel(ids, mine, came, out):
    out[...] = mine[...] + came[...]


def add_call(ids, mine, came, out=free, after=()):
    return call(
        add_kernel,
        "add",
        (1,),
        [whole(mine.shape)] * 2,
        out(mine.shape),
        whole(mine.shape),
        [],
        ids,
        mine,
        came,
        after=after,
        mib=8,
    )


def split_kernel(ids, mine, came, keep, send, *, extra):
    half = keep.shape[0] - extra
    keep[:half, :] = mine[:half, :] + came[:half, :]
    send[:half, :] = mine[half : 2 * half, :] + came[half : 2 * half, :]
    if extra:
        both = mine[2 * half :, :] + came[2 * half :, :]
        keep[half:, :] = both
        send[half:, :] = both


def split_call(ids, mine, came, extra=0, after=()):
    rows, cols = mine.shape
    shape = ((rows - extra) // 2 + extra, cols)
    return call(
        functools.partial(split_kernel, extra=extra),
        "add_halves",
        (1,),
        [whole(mine.shape)] * 2,
        [near(shape), free(shape)],
        [whole(shape)] * 2,
        [],
        ids,
        mine,
        came,
        after=after,
        mib=16,
    )


def phi_of(u, feature_matrix, factor):
    features = feature_matrix.shape[1] // 2
    wide = u.astype(f32)
    square = (wide * wide * (0.5 * factor)).astype(bf16)
    power = nn(jnp.concatenate([u, square], axis=1), feature_matrix[...])
    scale = factor * math.log2(math.e)
    return jnp.exp2(power * scale - 0.5 * math.log2(features)).astype(bf16)


def put_summary(out, pair, pairs, both, totals, head_size, features):
    half = pair // (pairs // 2)
    at = (pair % (pairs // 2)) * 2
    base = pairs * head_size
    for i in range(2):
        cols = slice(i * features, (i + 1) * features)
        out[half, (at + i) * head_size : (at + i + 1) * head_size, :] = both[
            i * head_size : (i + 1) * head_size, cols
        ]
        out[half, base + at + i : base + at + i + 1, :] = totals[i][:, cols]


def block_matrix(matrix, mine, other, flip, pairs, head_size, features, with_totals):
    base = pairs * head_size
    for pair in range(pairs):
        half = pair // (pairs // 2)
        at = (pair % (pairs // 2)) * 2
        first = (flip ^ half) == 0

        def take(lo, hi):
            return jnp.where(first, mine[lo:hi, :], other[lo:hi, :])

        nothing = jnp.zeros((head_size, features), bf16)
        for i in range(2):
            rows = slice(i * head_size, (i + 1) * head_size)
            part = take((at + i) * head_size, (at + i + 1) * head_size).astype(bf16)
            matrix[pair, rows, i * features : (i + 1) * features] = part
            matrix[pair, rows, (1 - i) * features : (2 - i) * features] = nothing
            if with_totals:
                rows = slice((2 + i) * head_size, (3 + i) * head_size)
                total = take(base + at + i, base + at + i + 1)
                spread = jnp.broadcast_to(total, (head_size, features)).astype(bf16)
                matrix[pair, rows, i * features : (i + 1) * features] = spread
                matrix[pair, rows, (1 - i) * features : (2 - i) * features] = nothing


def payload_shape(heads, head_size, features):
    rows = heads // 2 * head_size + heads // 2
    return (rows + (-rows) % 8, features)


def key_kernel(
    ids, h0, h1, h2, h3, weight, bias, gain, shift, feats, normed, joint, phi, mine, sent, out, *, factor
):
    genes, width = h0.shape
    features = feats.shape[1] // 2
    pair_width = feats.shape[0] // 2
    pairs = width // pair_width
    for r, block in enumerate((h0, h1, h2, h3)):
        scaled, _ = norm_parts(block[...])
        normed[r * genes : (r + 1) * genes, :] = (scaled * gain[...] + shift[...]).astype(bf16)
    for part in (1, 2, 0):
        cols = slice(part * width, (part + 1) * width)
        joint[:, cols] = (nn(normed[...], weight[:, cols]) + bias[:, cols]).astype(bf16)
    rows_used = pairs * (pair_width // 2) + pairs
    spare = out.shape[1] - rows_used
    if spare:
        for i in range(2):
            out[i, rows_used:, :] = jnp.zeros((spare, features), f32)
    for pair in range(pairs):
        at = width + pair * pair_width
        low = phi_of(joint[:, at : at + pair_width], feats, factor)
        phi[:, pair * 2 * features : (pair + 1) * 2 * features] = low
        value = joint[:, width + at : width + at + pair_width]
        total = col_sum(low.astype(f32))
        put_summary(out, pair, pairs, tn(value, low), (total, total), pair_width // 2, features)
    mine[...] = out[ids[3]]
    sent[...] = out[1 - ids[3]]


def key_call(ids, hidden, weight, bias, gain, shift, feats, factor, after=()):
    genes, width = hidden[0].shape
    tokens = plane * genes
    features = feats.shape[1] // 2
    heads = 2 * width // (feats.shape[0] // 2)
    pay = payload_shape(heads, width // heads, features)
    outs = [
        far((tokens, width), bf16),
        near((tokens, 3 * width), bf16),
        far((tokens, heads * features), bf16),
        near(pay),
        free(pay),
    ]
    ins = list(hidden) + [weight, bias, gain, shift, feats]
    return call(
        functools.partial(key_kernel, factor=factor),
        "key_summary",
        (1,),
        [whole(a.shape) for a in ins],
        outs,
        [whole(o.shape) for o in outs],
        [pltpu.VMEM((2, *pay), f32)],
        ids,
        *ins,
        after=after,
        mib=24,
    )


def query_kernel(ids, joint, feats, phi, *, factor):
    features = feats.shape[1] // 2
    pair_width = feats.shape[0] // 2
    for pair in range(joint.shape[1] // pair_width):
        u = joint[:, pair * pair_width : (pair + 1) * pair_width]
        phi[:, pair * 2 * features : (pair + 1) * 2 * features] = phi_of(u, feats, factor)


def query_call(ids, joint, feats, factor, after=()):
    tokens, wide = joint.shape
    width = wide // 3
    features = feats.shape[1] // 2
    heads = 2 * width // (feats.shape[0] // 2)
    step = tokens // 2
    return call(
        functools.partial(query_kernel, factor=factor),
        "query_features",
        (2,),
        [pl.BlockSpec((step, width), lambda at, ids: (at, 0)), whole(feats.shape)],
        near((tokens, heads * features), bf16),
        pl.BlockSpec((step, heads * features), lambda at, ids: (at, 0)),
        [],
        ids,
        joint,
        feats,
        after=after,
        mib=16,
    )


def gelu_parts(x):
    expo = jnp.exp2(x * x * (-0.5 * math.log2(math.e)))
    t = 1.0 / (1.0 + (0.3275911 * math.sqrt(0.5)) * jnp.abs(x))
    poly = t * (
        0.5 * 0.254829592
        + t
        * (
            0.5 * -0.284496736
            + t * (0.5 * 1.421413741 + t * (0.5 * -1.453152027 + t * (0.5 * 1.061405429)))
        )
    )
    tail = poly * expo
    return jnp.where(x > 0, 1.0 - tail, tail), expo * 0.3989422804014327


def feed_kernel(
    ids, h0, h1, h2, h3, c0, c1, c2, c3, phi, mine, other, w_out, b_out, gain, shift, w_up, b_up, w_low, b_low,
    g0, g1, g2, g3, active, d_upper, normed, attention, d_middle, d_branch, d_num, cot_low, mine_out, sent_out, sums, up_sums,
    pay, matrix, att_wide, recip, scaled_ref, back, result,
):
    genes, width = h0.shape
    pairs = matrix.shape[0]
    features = phi.shape[1] // pairs // 2
    pair_width = width // pairs
    head_size = pair_width // 2
    chunk = 1024
    blocks = [slice(r * genes, (r + 1) * genes) for r in range(plane)]
    block_matrix(matrix, mine, other, ids[3], pairs, head_size, features, True)
    for rows, block in zip(blocks, (c0, c1, c2, c3)):
        cot_low[rows, :] = block[...].astype(bf16)
    for pair in range(pairs):
        cols = slice(pair * pair_width, (pair + 1) * pair_width)
        both = nt(phi[:, pair * 2 * features : (pair + 1) * 2 * features], matrix[pair])
        inverse = 1.0 / both[:, pair_width:]
        quotient = both[:, :pair_width] * inverse
        att_wide[:, cols] = quotient
        recip[:, cols] = inverse
        attention[:, cols] = quotient.astype(bf16)
    result[...] = nn(attention[...], w_out[...]) + b_out[...]
    for rows, block in zip(blocks, (h0, h1, h2, h3)):
        mid = block[...] + result[rows, :]
        result[rows, :] = mid + b_low[...]
        scaled, inverse = norm_parts(mid)
        scaled_ref[rows, :] = scaled
        normed[rows, :] = (scaled * gain[...] + shift[...]).astype(bf16)
        back[rows, :] = jnp.broadcast_to(inverse, scaled.shape)
    d_middle[...] = back[...]
    for at in range(w_up.shape[1] // chunk):
        cols = slice(at * chunk, (at + 1) * chunk)
        upper = nn(normed[...], w_up[:, cols]) + b_up[:, cols]
        grad_active = nt(cot_low[...], w_low[cols, :])
        cumulative, density = gelu_parts(upper)
        active[:, cols] = (upper * cumulative).astype(bf16)
        low = (grad_active * (cumulative + upper * density)).astype(bf16)
        d_upper[:, cols] = low
        up_sums[:, cols] = col_sum(low.astype(f32))
        if at == 0:
            back[...] = nt(low, w_up[:, cols])
        else:
            back[...] += nt(low, w_up[:, cols])
        result[...] += nn(active[:, cols], w_low[cols, :])
    for rows, block in zip(blocks, (g0, g1, g2, g3)):
        block[...] = result[rows, :]
    grad_normed = back[...]
    scaled = scaled_ref[...]
    cot = cot_low[...].astype(f32)
    grad_mid = cot + norm_back(grad_normed, scaled, d_middle[...], gain[...])
    d_middle[...] = grad_mid
    branch = grad_mid.astype(bf16)
    d_branch[...] = branch
    sums[0:1, :] = col_sum(grad_normed * scaled)
    sums[1:2, :] = col_sum(grad_normed)
    sums[2:3, :] = col_sum(branch.astype(f32))
    sums[3:4, :] = col_sum(cot)
    sums[4:, :] = jnp.zeros((sums.shape[0] - 4, width), f32)
    back[...] = nt(branch, w_out[...])
    row = lax.broadcasted_iota(jnp.int32, (2 * pair_width, pair_width), 0) // head_size % 2
    col = lax.broadcasted_iota(jnp.int32, (2 * pair_width, pair_width), 1) // head_size
    ones = jnp.where(row == col, 1.0, 0.0).astype(bf16)
    rows_used = pairs * head_size + pairs
    spare = pay.shape[1] - rows_used
    if spare:
        for i in range(2):
            pay[i, rows_used:, :] = jnp.zeros((spare, features), f32)
    for pair in range(pairs):
        cols = slice(pair * pair_width, (pair + 1) * pair_width)
        grad = back[:, cols]
        inverse = recip[:, cols]
        product = grad * att_wide[:, cols]
        high = product.astype(bf16)
        low = (product - high.astype(f32)).astype(bf16)
        total = nn(jnp.concatenate([high, low], axis=1), ones)
        at = pair * 2 * pair_width
        d_num[:, at : at + pair_width] = (grad * inverse).astype(bf16)
        d_num[:, at + pair_width : at + 2 * pair_width] = (
            total * inverse * (-1.0 / head_size)
        ).astype(bf16)
        both = tn(
            d_num[:, at : at + 2 * pair_width],
            phi[:, pair * 2 * features : (pair + 1) * 2 * features],
        )
        totals = [
            both[pair_width + i * head_size : pair_width + i * head_size + 1, :] * float(head_size)
            for i in range(2)
        ]
        put_summary(pay, pair, pairs, both, totals, head_size, features)
    mine_out[...] = pay[ids[3]]
    sent_out[...] = pay[1 - ids[3]]


def feed_call(
    ids, hidden, cots, phi, mine, other, w_out, b_out, gain, shift, w_up, b_up, w_low, b_low, heads, after=()
):
    genes, width = hidden[0].shape
    tokens = plane * genes
    step = tokens
    features = phi.shape[1] // heads
    wide = w_up.shape[1]
    pairs = heads // 2
    pay = payload_shape(heads, width // heads, features)

    def rows(cols):
        return pl.BlockSpec((step, cols), lambda at, ids: (at, 0))

    ins = list(hidden) + list(cots) + [phi, mine, other, w_out, b_out, gain, shift, w_up, b_up, w_low, b_low]
    in_specs = [whole(a.shape) for a in ins]
    in_specs[2 * plane] = rows(phi.shape[1])
    outs = [(near((genes, width)), whole((genes, width)))] * plane + [
        (near((tokens, wide), bf16), rows(wide)),
        (near((tokens, wide), bf16), rows(wide)),
        (near((tokens, width), bf16), rows(width)),
        (near((tokens, width), bf16), rows(width)),
        (far((tokens, width)), rows(width)),
        (far((tokens, width), bf16), rows(width)),
        (near((tokens, 2 * width), bf16), rows(2 * width)),
        (far((tokens, width), bf16), rows(width)),
        (near(pay), whole(pay)),
        (free(pay), whole(pay)),
        (near((8, width)), whole((8, width))),
        (near((1, wide)), whole((1, wide))),
    ]
    return call(
        feed_kernel,
        "feed_forward",
        (1,),
        in_specs,
        [o[0] for o in outs],
        [o[1] for o in outs],
        [
            pltpu.VMEM((2, *pay), f32),
            pltpu.VMEM((pairs, 2 * width // pairs, 2 * features), bf16),
        ]
        + [pltpu.VMEM((step, width), f32)] * 5,
        ids,
        *ins,
        after=after,
        mib=22,
    )


def feature_back(grad_feat, phi, u, back_matrix, factor):
    pair_width = u.shape[1]
    low = (grad_feat * phi.astype(f32) * factor).astype(bf16)
    both = nn(low, back_matrix[...])
    return both[:, :pair_width] - factor * u.astype(f32) * both[:, pair_width:]


def d_query_kernel(ids, d_num, phi, query, mine, other, back_matrix, weight, d_query, d_normed, sums, matrix, *, factor):
    step = pl.program_id(0)
    pairs = matrix.shape[0]
    features = phi.shape[1] // pairs // 2
    width = query.shape[1]
    pair_width = width // pairs

    @pl.when(step == 0)
    def _():
        block_matrix(matrix, mine, other, ids[3], pairs, pair_width // 2, features, True)
        sums[...] = jnp.zeros_like(sums)

    for pair in range(pairs):
        cols = slice(pair * pair_width, (pair + 1) * pair_width)
        grad_feat = nn(d_num[:, pair * 2 * pair_width : (pair + 1) * 2 * pair_width], matrix[pair])
        grad = feature_back(
            grad_feat,
            phi[:, pair * 2 * features : (pair + 1) * 2 * features],
            query[:, cols],
            back_matrix,
            factor,
        )
        d_query[:, cols] = grad.astype(bf16)
    low = d_query[...]
    d_normed[...] = nt(low, weight[...])
    sums[...] += col_sum(low.astype(f32))


def d_query_call(ids, d_num, phi, joint, mine, other, back_matrix, weight, factor, after=()):
    tokens = joint.shape[0]
    width = joint.shape[1] // 3
    pair_width = back_matrix.shape[1] // 2
    pairs = width // pair_width
    step = tokens // plane * tile
    features = back_matrix.shape[0] // 2

    def rows(cols):
        return pl.BlockSpec((step, cols), lambda at, ids: (at, 0))

    return call(
        functools.partial(d_query_kernel, factor=factor),
        "query_gradient",
        (plane // tile,),
        [
            rows(2 * width),
            rows(phi.shape[1]),
            rows(width),
            whole(mine.shape),
            whole(other.shape),
            whole(back_matrix.shape),
            whole((width, width)),
        ],
        [near((tokens, width), bf16), near((tokens, width)), near((1, width))],
        [rows(width), rows(width), whole((1, width))],
        [pltpu.VMEM((pairs, 2 * pair_width, 2 * features), bf16)],
        ids,
        d_num,
        phi,
        joint,
        mine,
        other,
        back_matrix,
        weight,
        after=after,
        mib=20,
    )


def d_key_kernel(
    ids, h0, h1, h2, h3, joint, phi, d_query, d_normed_q, d_middle, mine, other, back_matrix, weight, gain,
    g0, g1, g2, g3, d_joint, sums, key_sums, matrix, total_ref, hid, *, factor,
):
    step = pl.program_id(0)
    pairs = matrix.shape[0]
    genes, width = h0.shape
    features = phi.shape[1] // pairs // 2
    pair_width = width // pairs
    head_size = pair_width // 2

    @pl.when(step == 0)
    def _():
        block_matrix(matrix, mine, other, ids[3], pairs, head_size, features, False)
        base = pairs * head_size
        for pair in range(pairs):
            half = pair // (pairs // 2)
            at = base + (pair % (pairs // 2)) * 2
            first = (ids[3] ^ half) == 0
            for i in range(2):
                total_ref[pair : pair + 1, i * features : (i + 1) * features] = jnp.where(
                    first, mine[at + i : at + i + 1, :], other[at + i : at + i + 1, :]
                )
        sums[...] = jnp.zeros_like(sums)
        key_sums[...] = jnp.zeros_like(key_sums)

    for k in range(plane // tile):

        @pl.when(step == k)
        def _():
            for i in range(tile):
                hid[i * genes : (i + 1) * genes, :] = (h0, h1, h2, h3)[k * tile + i][...]

    d_joint[:, :width] = d_query[...]
    for pair in range(pairs):
        at = pair * pair_width
        value = joint[:, 2 * width + at : 2 * width + at + pair_width]
        low = phi[:, pair * 2 * features : (pair + 1) * 2 * features]
        grad_feat = nn(value, matrix[pair]) + total_ref[pair : pair + 1, :]
        grad = feature_back(
            grad_feat, low, joint[:, width + at : width + at + pair_width], back_matrix, factor
        )
        d_joint[:, width + at : width + at + pair_width] = grad.astype(bf16)
        d_joint[:, 2 * width + at : 2 * width + at + pair_width] = nt(low, matrix[pair]).astype(bf16)
    low = d_joint[:, width:]
    key_sums[...] += col_sum(low.astype(f32))
    grad_normed = d_normed_q[...] + nt(low, weight[:, width:])
    scaled, inverse = norm_parts(hid[...])
    result = (d_middle[...] + norm_back(grad_normed, scaled, inverse, gain[...])).astype(bf16)
    result = result.astype(f32)
    sums[0:1, :] += col_sum(grad_normed * scaled)
    sums[1:2, :] += col_sum(grad_normed)
    sums[2:3, :] += col_sum(result)
    for k in range(plane // tile):

        @pl.when(step == k)
        def _():
            for i in range(tile):
                (g0, g1, g2, g3)[k * tile + i][...] = result[i * genes : (i + 1) * genes, :]


def d_key_call(ids, hidden, joint, phi, d_query, d_normed_q, d_middle, mine, other, back_matrix, weight, gain, factor, after=()):
    genes, width = hidden[0].shape
    tokens = plane * genes
    step = tile * genes
    pair_width = back_matrix.shape[1] // 2
    pairs = width // pair_width
    features = back_matrix.shape[0] // 2

    def rows(cols):
        return pl.BlockSpec((step, cols), lambda at, ids: (at, 0))

    ins = list(hidden) + [joint, phi, d_query, d_normed_q, d_middle, mine, other, back_matrix, weight, gain]
    in_specs = [whole(a.shape) for a in ins]
    for i in range(5):
        in_specs[plane + i] = rows(ins[plane + i].shape[1])
    outs = [(near((genes, width)), whole((genes, width)))] * plane + [
        (near((tokens, 3 * width), bf16), rows(3 * width)),
        (near((8, width)), whole((8, width))),
        (near((1, 2 * width)), whole((1, 2 * width))),
    ]
    return call(
        functools.partial(d_key_kernel, factor=factor),
        "key_gradient",
        (plane // tile,),
        in_specs,
        [o[0] for o in outs],
        [o[1] for o in outs],
        [
            pltpu.VMEM((pairs, pair_width, 2 * features), bf16),
            pltpu.VMEM((8, 2 * features), f32),
            pltpu.VMEM((step, width), f32),
        ],
        ids,
        *ins,
        after=after,
        mib=28,
    )


def put_shards(out, size, spot, where, first, count, per, rows, at, value):
    if rows % 8:
        out[at * size + first * rows : at * size + (first + count) * rows, :] = value
        return
    for s in range(count):
        to = (where(first + s) ^ spot) * per + at
        to = pl.multiple_of(to, 8)
        out[pl.ds(to, rows), :] = value[s * rows : (s + 1) * rows, :]


def in_slots(bundle, size, me, per, rows, order):
    if rows % 8 == 0:
        return bundle
    body = bundle[: size * per].reshape(per // rows, size, rows, -1).transpose(1, 0, 2, 3)
    place = placed(order, size.bit_length() - 1)
    owner = sorted(range(size), key=place)
    body = body[jnp.array(owner, jnp.int32) ^ me].reshape(size * per, -1)
    return jnp.concatenate([body, bundle[size * per :]], axis=0)


def side_of(sent):
    return (lambda ids: 1 - ids[1]) if sent else (lambda ids: ids[1])


def lower_weights_kernel(ids, a0, a1, c0, c1, out, *, size, where, spot_at):
    step = pl.program_id(0)
    part = size // 4
    rows = out.shape[0] // size
    value = tn(a0[...], c0[...]) + tn(a1[...], c1[...])
    for k in range(4):

        @pl.when(step == k)
        def _():
            put_shards(out, size, ids[spot_at], where, k * part, part, rows, rows, 0, value)


def lower_weights_call(ids, size, sent, where, spot_at, active, cot_low, after=()):
    tokens, wide = active[0].shape
    half = cot_low[0].shape[1] // 2
    side = side_of(sent)
    shape = (wide, half)
    return call(
        functools.partial(lower_weights_kernel, size=size, where=where, spot_at=spot_at),
        "lower_weights",
        (4,),
        [pl.BlockSpec((tokens, wide // 4), lambda at, ids: (0, at))] * 2
        + [pl.BlockSpec((tokens, half), lambda at, ids: (0, side(ids)))] * 2,
        near(shape),
        whole(shape),
        [],
        ids,
        *active,
        *cot_low,
        after=after,
        mib=16,
    )


def upper_weights_kernel(ids, n0, n1, u0, u1, t0, t1, b0, b1, out, *, size, where, spot_at):
    step = pl.program_id(0)
    part = size // 4
    rows = n0.shape[1] // size
    value = tn(n0[...], u0[...]) + tn(n1[...], u1[...])
    last = tn(t0[...], b0[...]) + tn(t1[...], b1[...])
    for k in range(4):

        @pl.when(step == k)
        def _():
            put_shards(out, size, ids[spot_at], where, 0, size, 5 * rows, rows, k * rows, value)
            put_shards(out, size, ids[spot_at], where, k * part, part, 5 * rows, rows, 4 * rows, last)


def upper_weights_call(ids, size, sent, where, spot_at, normed, d_upper, attention, d_branch, after=()):
    tokens, width = normed[0].shape
    half = width // 2
    side = side_of(sent)
    shape = (5 * width, half)
    return call(
        functools.partial(upper_weights_kernel, size=size, where=where, spot_at=spot_at),
        "upper_weights",
        (4,),
        [pl.BlockSpec((tokens, width), lambda at, ids: (0, 0))] * 2
        + [pl.BlockSpec((tokens, half), lambda at, ids: (0, side(ids) * 4 + at))] * 2
        + [pl.BlockSpec((tokens, width // 4), lambda at, ids: (0, at))] * 2
        + [pl.BlockSpec((tokens, half), lambda at, ids: (0, side(ids)))] * 2,
        near(shape),
        whole(shape),
        [],
        ids,
        *normed,
        *d_upper,
        *attention,
        *d_branch,
        after=after,
        mib=16,
    )


def joint_weights_kernel(ids, n0, n1, j0, j1, out, *, size, where, spot_at):
    step = pl.program_id(0)
    rows = n0.shape[1] // size
    value = tn(n0[...], j0[...]) + tn(n1[...], j1[...])
    for k in range(3):

        @pl.when(step == k)
        def _():
            put_shards(out, size, ids[spot_at], where, 0, size, 3 * rows, rows, k * rows, value)


def joint_weights_call(ids, size, sent, where, spot_at, normed, d_joint, after=()):
    tokens, width = normed[0].shape
    half = width // 2
    side = side_of(sent)
    shape = (3 * width, half)
    return call(
        functools.partial(joint_weights_kernel, size=size, where=where, spot_at=spot_at),
        "joint_weights",
        (3,),
        [pl.BlockSpec((tokens, width), lambda at, ids: (0, 0))] * 2
        + [pl.BlockSpec((tokens, half), lambda at, ids: (0, side(ids) * 3 + at))] * 2,
        near(shape),
        whole(shape),
        [],
        ids,
        *normed,
        *d_joint,
        after=after,
        mib=14,
    )


vector_rows = 32


def input_weights_kernel(ids, *refs, size, where, spot_at):
    own = refs[:2]
    merged = refs[2:5]
    r0, r1, v0, v1, f0, f1, u0, u1, k0, k1, q0, q1, s0, s1, d_low, sent, kept, zero_hidden = refs[5:]
    pieces = [own[j] if r == 0 else merged[r - 1].at[j] for r in range(plane) for j in range(2)]
    genes, width = own[0].shape
    half = width // 2
    rows = (sent.shape[0] - vector_rows) // size
    total = None
    for i, piece in enumerate(pieces):
        wide = piece[...]
        d_low[i * genes : (i + 1) * genes, :] = wide.astype(bf16)
        masked = wide * (v0, v1)[i % 2][i // 2][:, :1]
        total = masked if total is None else total + masked
    zero_hidden[...] = total
    parts = [f0[0:4, :] + f1[0:4, :], s0[0:3, :] + s1[0:3, :], q0[...] + q1[...], k0[...] + k1[...], u0[...] + u1[...]]
    for out, side in ((sent, 1 - ids[1]), (kept, ids[1])):
        value = None
        for i in range(8):
            chosen = (r0, r1)[i % 2][i // 2]
            lo = d_low[i * genes : (i + 1) * genes, :half]
            hi = d_low[i * genes : (i + 1) * genes, half:]
            product = tn(chosen, jnp.where(side == 0, lo, hi))
            value = product if value is None else value + product
        put_shards(out, size, ids[spot_at], where, 0, size, rows, rows, 0, value)
        at = size * rows
        for part in parts:
            for row in range(part.shape[0]):
                for c in range(part.shape[1] // half):
                    out[at : at + 1, :] = part[row : row + 1, c * half : (c + 1) * half]
                    at += 1
        out[at:, :] = jnp.zeros((out.shape[0] - at, half), f32)


def input_weights_call(ids, size, where, spot_at, own, came, rows, vacant, sums, after=()):
    genes, width = own[0].shape
    width_in = rows[0].shape[2]
    ins = [*own, *came, *rows, *vacant, *sums]
    shape = (width_in + vector_rows, width // 2)
    outs = [near((8 * genes, width), bf16), free(shape), near(shape), free((genes, width))]
    return call(
        functools.partial(input_weights_kernel, size=size, where=where, spot_at=spot_at),
        "input_weights",
        (1,),
        [whole(a.shape) for a in ins],
        outs,
        [whole(o.shape) for o in outs],
        [],
        ids,
        *ins,
        after=after,
        mib=28,
    )


def finish_kernel(ids, *refs, parts):
    first_core = ids[1] == 0
    outs = refs[-len(parts) :]
    for out, (bundle, rows, groups, at) in zip(outs, parts):
        mine, came = refs[2 * bundle : 2 * bundle + 2]
        half = mine.shape[1]
        for g in range(groups):
            one = mine[at + g * rows : at + (g + 1) * rows, :]
            two = came[at + g * rows : at + (g + 1) * rows, :]
            out[:, g * half : (g + 1) * half] = jnp.where(first_core, one, two)
            out[:, (groups + g) * half : (groups + g + 1) * half] = jnp.where(first_core, two, one)


def finish_call(ids, bundles, parts, after=()):
    ins = [array for pair in bundles for array in pair]
    half = ins[0].shape[1]
    outs = [far((rows, 2 * groups * half)) for _, rows, groups, _ in parts]
    return call(
        functools.partial(finish_kernel, parts=parts),
        "weight_results",
        (1,),
        [whole(a.shape) for a in ins],
        outs,
        [whole(o.shape) for o in outs],
        [],
        ids,
        *ins,
        after=after,
        mib=12,
    )


def out_kernel(ids, *refs):
    out = refs[-1]
    merged = refs[-plane:-1]
    group = len(refs) - plane
    for j in range(group):
        out[ids[2] * group + j] = refs[j][...].astype(bf16)
        for r in range(1, plane):
            out[(ids[2] ^ r) * group + j] = merged[r - 1][j].astype(bf16)


def out_call(ids, own, came, after=()):
    genes, width = own[0].shape
    shape = (plane * len(own), genes, width)
    ins = [*own, *came]
    return call(
        out_kernel,
        "block_out",
        (1,),
        [whole(p.shape) for p in ins],
        far(shape, bf16),
        whole(shape),
        [],
        ids,
        *ins,
        after=after,
        mib=14,
    )


def token_kernel(ids, d_low, index, weight, token_grad):
    slots, _ = index.shape
    width = d_low.shape[1]
    genes = d_low.shape[0] // 8
    slot = lax.broadcasted_iota(jnp.int32, (slots, 1), 0)
    picked = jnp.zeros((slots, width), f32)
    gene = lax.broadcasted_iota(jnp.int32, (slots, genes), 1)
    match = (index[...] - ids[0] * genes) == gene
    for i in range(8):
        cell = i ^ (2 * ids[2])
        here = (slot >= ids[8 + cell]) & (slot < ids[9 + cell])
        chosen = jnp.where(match & here, 1.0, 0.0).astype(bf16)
        picked = picked + nn(chosen, d_low[i * genes : (i + 1) * genes, :])
    token_grad[0] = nt(picked.astype(bf16), weight[...])


def token_call(ids, d_low, index, weight, after=()):
    ins = [d_low, index, weight]
    shape = (1, index.shape[0], weight.shape[0])
    return call(
        token_kernel,
        "token_gradient",
        (1,),
        [whole(a.shape) for a in ins],
        far(shape),
        whole(shape),
        [],
        ids,
        *ins,
        after=after,
        mib=24,
    )


def zero_kernel(ids, mine, other, weight, out):
    total = mine[...] + other[...]
    high = total.astype(bf16)
    rest = total - high.astype(f32)
    low = rest.astype(bf16)
    out[...] = nt(high, weight[...]) + nt(low, weight[...])


def zero_call(ids, mine, other, weight, after=()):
    genes, width = mine.shape
    ins = [mine, other, weight]
    shape = (genes, weight.shape[0])
    return call(
        zero_kernel,
        "zero_gradient",
        (1,),
        [whole(a.shape) for a in ins],
        far(shape),
        whole(shape),
        [],
        ids,
        *ins,
        after=after,
        mib=12,
    )


def local(
    encoder_packed_tokens,
    token_gene_index,
    cell_counts,
    zero_embed,
    random_features,
    input_weight,
    input_bias,
    first_gain,
    first_shift,
    joint_weight,
    joint_bias,
    output_weight,
    output_bias,
    second_gain,
    second_shift,
    upper_weight,
    upper_bias,
    lower_weight,
    lower_bias,
    cotangent,
):
    placed_at.clear()
    size = lax.axis_size("gene")
    me = lax.axis_index("gene")
    core = lax.axis_index("cell")
    cells_here, genes, width = cotangent.shape
    head_size, features = random_features.shape
    heads = width // head_size
    factor = head_size ** (-0.25)
    group = cells_here // plane
    log = size.bit_length() - 1
    rest = list(range(3, log))
    orders = ([2, 0, 1] + rest, [2, 0, 1] + rest, [1, 0, 2] + rest, [0, 1, 2] + rest)
    where = [placed(order, log) for order in orders]
    ends = jnp.cumsum(cell_counts[0]).astype(jnp.int32)
    ids = jnp.concatenate(
        [
            jnp.stack([me, core, me % plane, (me // plane) % 2]).astype(jnp.int32),
            jnp.stack([placed(order, log)(me) for order in orders]).astype(jnp.int32),
            jnp.zeros((1,), jnp.int32),
            ends,
        ]
    )
    nothing = jnp.zeros((head_size, features), bf16)
    minus = jnp.full((head_size, features), -1.0, bf16)
    feats = jnp.concatenate(
        [
            jnp.concatenate([random_features, nothing], axis=1),
            jnp.concatenate([nothing, random_features], axis=1),
            jnp.concatenate([minus, nothing], axis=1),
            jnp.concatenate([nothing, minus], axis=1),
        ],
        axis=0,
    )
    back_matrix = jnp.concatenate([feats[: 2 * head_size].T, -feats[2 * head_size :].T], axis=1)

    def row(vector):
        return vector.reshape(1, -1)

    high = [1 << b for b in range(2, log)]
    last = ()

    def then(made, token, *more):
        nonlocal last
        last = (token, *more)
        return made

    def gene_swap(value, bit):
        return swap(value, "gene", size, bit)

    def out_and_in(blocks):
        return [block if r == 0 else gene_swap(block, r) for r, block in enumerate(blocks)]

    class Halves:
        def __init__(self, mine, sent):
            self.mine = mine
            self.came = gene_swap(sent, high[0])
            self.left = high[1:]

        def add(self):
            self.mine = add_call(ids, self.mine, self.came, after=last)
            then(None, self.mine)
            if self.left:
                self.came = gene_swap(self.mine, self.left.pop(0))
            else:
                self.other = gene_swap(self.mine, high[0])

        def coming(self):
            return getattr(self, "other", self.came)

        def finish(self):
            while not hasattr(self, "other"):
                self.add()
            return self.mine, self.other

    class Scatter:
        def __init__(self, sent, kept, order, rows, extra=0):
            per = (kept.shape[0] - extra) // size
            self.mine = in_slots(kept, size, me, per, rows, order)
            self.came = swap(in_slots(sent, size, me, per, rows, order), "cell", 2, 1)
            self.order = list(order)
            self.extra = extra

        def add(self):
            if self.order:
                self.mine, send = split_call(ids, self.mine, self.came, self.extra, after=last)
                then(None, self.mine)
                self.came = gene_swap(send, 1 << self.order.pop(0))

        def close(self):
            while self.order:
                self.add()
            self.mine = add_call(ids, self.mine, self.came, after=last)
            then(None, self.mine)
            self.other = swap(self.mine, "cell", 2, 1)

    shard = width // size
    wide_shard = upper_weight.shape[1] // size
    in_shard = input_weight.shape[0] // size
    hidden, rows, vacant = [], [], []
    for j in range(group):
        made = rows_call(
            ids, j, group, encoder_packed_tokens[0], token_gene_index, zero_embed, input_weight, row(input_bias),
            after=last,
        )
        hidden.append(out_and_in(made[:plane]))
        rows.append(made[plane])
        vacant.append(made[plane + 1])
        then(None, made[plane + 1])
    normed, joint, key_phi, sums = [], [], [], []

    def keys_of(j):
        made = key_call(
            ids, hidden[j], joint_weight, row(joint_bias), row(first_gain), row(first_shift), feats, factor,
            after=last,
        )
        normed.append(made[0])
        joint.append(made[1])
        key_phi.append(made[2])
        sums.append(Halves(made[3], made[4]))
        then(None, made[0])

    query_phi = []

    def query_of(j):
        query_phi.append(query_call(ids, joint[j], feats, factor, after=last))
        then(None, query_phi[j])

    keys_of(0)
    w_up, w_low, w_out, w_joint = hold_call(
        ids, upper_weight, lower_weight, output_weight, joint_weight, after=last
    )
    then(None, w_out)
    sums[0].add()
    cots = []

    def cotangent_of(j):
        wide = cotangent_call(ids, j, group, cotangent, after=last)
        then(None, wide[0])
        cots.append(out_and_in(wide))

    keys_of(1)
    cotangent_of(0)
    sums[0].add()
    sums[1].add()
    query_of(0)
    query_of(1)
    then(None, *last, *cots[0][1:])
    cotangent_of(1)
    sums[1].finish()
    sums = [s.finish() for s in sums]
    fed, d_sums = [], []
    for j in range(group):
        made = feed_call(
            ids, hidden[j], cots[j], query_phi[j], *sums[j], w_out, row(output_bias), row(second_gain),
            row(second_shift), w_up, row(upper_bias), w_low, row(lower_bias), heads,
            after=last,
        )
        fed.append(made)
        d_sums.append(Halves(made[plane + 8], made[plane + 9]))
        then(None, made[plane + 2])
    active, d_upper, normed_two, attention, d_middle, d_branch, d_num, cot_low, _, _, sums_two, up_sums = list(
        zip(*fed)
    )[plane:]
    queries = []

    def d_query_of(j):
        queries.append(
            d_query_call(
                ids, d_num[j], query_phi[j], joint[j], *sums[j], back_matrix, w_joint, factor, after=last
            )
        )
        then(None, queries[j][1])

    def lower_of(sent):
        made = lower_weights_call(ids, size, sent, where[0], 4, active, cot_low, after=last)
        return then(made, made)

    def upper_of(sent):
        made = upper_weights_call(
            ids, size, sent, where[1], 5, normed_two, d_upper, attention, d_branch, after=last
        )
        return then(made, made)

    def joint_of(sent):
        made = joint_weights_call(ids, size, sent, where[2], 6, normed, d_joint, after=last)
        return then(made, made)

    def pass_on(*arrays):
        made = pass_call(ids, *arrays, after=last)
        then(None, made[0])
        return made

    def release(blocks):
        sent = release_call(ids, [block[r] for block in blocks for r in range(1, plane)], after=last)
        then(None, sent[0])
        return [gene_swap(block, r) for r, block in enumerate(sent, 1)]

    keys = []

    def d_key_of(j):
        made = d_key_call(
            ids, hidden[j], joint[j], key_phi[j], queries[j][0], queries[j][1], d_middle[j], *d_sums[j].finish(),
            back_matrix, w_joint, row(first_gain), factor,
            after=last,
        )
        keys.append(made)
        then(None, made[plane])

    back_out = release([made[:plane] for made in fed])
    d_sums[0].add()
    d_query_of(0)
    d_query_of(1)
    d_sums[1].add()
    upper_sent = upper_of(True)
    d_sums[0].add()
    upper_kept = upper_of(False)
    d_sums[1].add()
    then(None, *last, *back_out, d_sums[0].coming())
    (upper_sent,) = pass_on(upper_sent)
    upper_sum = Scatter(upper_sent, upper_kept, orders[1], shard)
    d_key_of(0)
    d_key_of(1)
    backs = release([k[:plane] for k in keys])
    upper_sum.add()
    d_joint = [k[plane] for k in keys]
    joint_sent = joint_of(True)
    joint_kept = joint_of(False)
    lower_sent = lower_of(True)
    lower_kept = lower_of(False)
    block_out = out_call(ids, [made[0] for made in fed], back_out, after=last)
    then(None, block_out)
    sums_one = [k[plane + 1] for k in keys]
    key_sums = [k[plane + 2] for k in keys]
    query_sums = [q[2] for q in queries]
    then(None, *last, upper_sum.came, *backs)
    joint_sent, lower_sent = pass_on(joint_sent, lower_sent)
    lower_sum = Scatter(lower_sent, lower_kept, orders[0], wide_shard)
    joint_sum = Scatter(joint_sent, joint_kept, orders[2], shard)
    d_low, input_sent, input_kept, zero_hidden = input_weights_call(
        ids, size, where[3], 7, [k[0] for k in keys], backs, rows, vacant,
        [*sums_two, *up_sums, *key_sums, *query_sums, *sums_one],
        after=last,
    )
    then(None, zero_hidden)
    input_sum = Scatter(input_sent, input_kept, orders[3], in_shard, vector_rows)
    zero_came = swap(zero_hidden, "cell", 2, 1)
    joint_sum.add()
    upper_sum.add()
    lower_sum.add()
    input_sum.add()
    token_grad = token_call(ids, d_low, token_gene_index.reshape(-1, 1), input_weight, after=last)
    then(None, token_grad)
    zero_grad = zero_call(ids, zero_hidden, zero_came, input_weight, after=last)
    then(None, zero_grad)
    upper_sum.add()
    joint_sum.add()
    lower_sum.add()
    input_sum.add()
    upper_sum.add()
    input_sum.add()
    input_sum.add()
    upper_sum.close()
    joint_sum.add()
    lower_sum.add()
    input_sum.close()
    joint_sum.add()
    lower_sum.add()
    joint_sum.close()
    lower_sum.close()
    g_lower, g_upper, g_output, g_joint, g_input = finish_call(
        ids,
        [(b.mine, b.other) for b in (lower_sum, upper_sum, joint_sum, input_sum)],
        [
            (0, wide_shard, 1, 0),
            (1, shard, 4, 0),
            (1, shard, 1, 4 * shard),
            (2, shard, 3, 0),
            (3, in_shard, 1, 0),
        ],
        after=last,
    )
    flat = input_sum.mine[in_shard:].reshape(-1)
    lengths = [width] * 7 + [3 * width, upper_weight.shape[1]]
    found = []
    at = 0
    for length in lengths:
        part = length // size
        found.append(lax.dynamic_slice(flat, (at + me * part,), (part,)))
        at += length
    small_out = [found[i] for i in (6, 4, 5, 7, 2, 0, 1, 8, 3)]
    return (
        block_out,
        token_grad,
        zero_grad,
        g_input,
        small_out[0],
        small_out[1],
        small_out[2],
        g_joint,
        small_out[3],
        g_output,
        small_out[4],
        small_out[5],
        small_out[6],
        g_upper,
        small_out[7],
        g_lower,
        small_out[8],
    )


def solution(mesh):
    return jax.shard_map(
        local,
        mesh=mesh,
        in_specs=(
            P("cell", "gene", None),
            P("cell", "gene"),
            P("cell", "gene"),
            P("gene", None),
            P(),
            P(),
            P(),
            P(),
            P(),
            P(),
            P(),
            P(),
            P(),
            P(),
            P(),
            P(),
            P(),
            P(),
            P(),
            P("cell", "gene", None),
        ),
        out_specs=(
            P("cell", "gene", None),
            P("cell", "gene", None),
            P("gene", None),
            P("gene", None),
            P("gene"),
            P("gene"),
            P("gene"),
            P("gene", None),
            P("gene"),
            P("gene", None),
            P("gene"),
            P("gene"),
            P("gene"),
            P("gene", None),
            P("gene"),
            P("gene", None),
            P("gene"),
        ),
        check_vma=False,
    )
```

```python
import functools
import math

import jax
import jax.numpy as jnp
from jax import lax
from jax.experimental import pallas as pl
from jax.experimental.pallas import tpu as pltpu
from jax.sharding import PartitionSpec as P

epsilon = 1e-05
f32 = jnp.float32
bf16 = jnp.bfloat16
plane = 4
tile = 4


def nn(left, right):
    return jnp.dot(left, right, preferred_element_type=f32)


def nt(left, right):
    return lax.dot_general(left, right, (((1,), (1,)), ((), ())), preferred_element_type=f32)


def tn(left, right):
    return lax.dot_general(left, right, (((0,), (0,)), ((), ())), preferred_element_type=f32)


def col_sum(values):
    return jnp.sum(values, axis=0, keepdims=True)


def norm_parts(values):
    centred = values - jnp.mean(values, axis=-1, keepdims=True)
    inverse = lax.rsqrt(jnp.mean(centred * centred, axis=-1, keepdims=True) + epsilon)
    return centred * inverse, inverse


def norm_back(grad_in, scaled, inverse, gain):
    weighted = grad_in * gain
    return inverse * (
        weighted
        - jnp.mean(weighted, axis=-1, keepdims=True)
        - scaled * jnp.mean(weighted * scaled, axis=-1, keepdims=True)
    )


def whole(shape):
    return pl.BlockSpec(shape, lambda *at: (0,) * len(shape))


placed_at = []


def near(shape, dtype=f32):
    return pltpu.VMEM(shape, dtype)


def far(shape, dtype=f32):
    return pltpu.HBM(shape, dtype)


def free(shape, dtype=f32):
    return jax.ShapeDtypeStruct(shape, dtype)


def placed(order, log):
    return lambda number: sum(((number >> bit) & 1) << (log - 1 - i) for i, bit in enumerate(order))


def call(kernel, name, grid, in_specs, outs, out_specs, scratch, *args, after=(), mib=60):
    first = 1 + len(in_specs)

    def body(*refs):
        kernel(*refs[:first], *refs[first + len(after) :])

    def held(array):
        for other, space in placed_at:
            if array is other:
                return pltpu.with_memory_space_constraint(array, space)
        return array

    made = pl.pallas_call(
        body,
        name=name,
        grid_spec=pltpu.PrefetchScalarGridSpec(
            num_scalar_prefetch=1,
            grid=grid,
            in_specs=list(in_specs) + [pl.BlockSpec(memory_space=pl.ANY)] * len(after),
            out_specs=out_specs,
            scratch_shapes=scratch,
        ),
        out_shape=outs,
        compiler_params=pltpu.CompilerParams(
            vmem_limit_bytes=mib << 20, dimension_semantics=("arbitrary",) * len(grid)
        ),
        cost_estimate=pl.CostEstimate(flops=1000, bytes_accessed=1000, transcendentals=0),
    )(args[0], *(held(a) for a in args[1:]), *(held(a) for a in after))
    several = isinstance(outs, (list, tuple))
    for out, array in zip(outs if several else [outs], made if several else [made]):
        if getattr(out, "memory_space", None) in (pltpu.VMEM, pltpu.HBM):
            placed_at.append((array, out.memory_space))
    return made


def swap(value, axis, size, bit):
    return lax.ppermute(value, axis, [(i, i ^ bit) for i in range(size)])


def rows_kernel(ids, tokens, index, zero, weight, bias, h0, h1, h2, h3, rows_out, vacant_out, *, group, j):
    genes = zero.shape[0]
    first_gene = ids[0] * genes
    slots = index.shape[1]
    slot = lax.broadcasted_iota(jnp.int32, (genes, slots), 1)
    gene = lax.broadcasted_iota(jnp.int32, (genes, slots), 0)
    match = (index[...] - first_gene) == gene
    for r in (3, 1, 2, 0):
        cell = (ids[2] ^ r) * group + j
        here = match & (slot >= ids[8 + cell]) & (slot < ids[9 + cell])
        chosen = jnp.where(here, 1.0, 0.0)
        vacant = 1.0 - jnp.sum(chosen, axis=1, keepdims=True)
        rows = nn(chosen.astype(bf16), tokens[...]) + vacant * zero[...].astype(f32)
        rows = rows.astype(bf16)
        rows_out[r] = rows
        vacant_out[r] = jnp.broadcast_to(vacant, (genes, 128))
        (h0, h1, h2, h3)[r][...] = nn(rows, weight[...]) + bias[...]


def rows_call(ids, j, group, tokens, index, zero, weight, bias, after=()):
    tokens, index, zero, weight = (
        pltpu.with_memory_space_constraint(a, pltpu.HBM) for a in (tokens, index, zero, weight)
    )
    genes, width_in = zero.shape
    width = weight.shape[1]
    outs = [free((genes, width))] * plane + [
        far((plane, genes, width_in), bf16),
        far((plane, genes, 128)),
    ]
    ins = [tokens, index, zero, weight, bias]
    return call(
        functools.partial(rows_kernel, group=group, j=j),
        "gene_rows",
        (1,),
        [whole(a.shape) for a in ins],
        outs,
        [whole(o.shape) for o in outs],
        [],
        ids,
        *ins,
        after=after,
        mib=20,
    )


def cotangent_kernel(ids, cot, c0, c1, c2, c3, *, group, j):
    for r, out in enumerate((c0, c1, c2, c3)):
        out[...] = cot[(ids[2] ^ r) * group + j].astype(f32)


def cotangent_call(ids, j, group, cot, after=()):
    _, genes, width = cot.shape
    outs = [free((genes, width))] * plane
    return call(
        functools.partial(cotangent_kernel, group=group, j=j),
        "wide_cotangent",
        (1,),
        [whole(cot.shape)],
        outs,
        [whole(o.shape) for o in outs],
        [],
        ids,
        cot,
        after=after,
        mib=14,
    )


def pass_kernel(ids, *refs):
    count = len(refs) // 2
    for given, out in zip(refs[:count], refs[count:]):
        out[...] = given[...]


def pass_call(ids, *arrays, after=()):
    return call(
        pass_kernel,
        "pass_on",
        (1,),
        [whole(a.shape) for a in arrays],
        [free(a.shape, a.dtype) for a in arrays],
        [whole(a.shape) for a in arrays],
        [],
        ids,
        *arrays,
        after=after,
        mib=16,
    )


def release_kernel(ids, *refs):
    outs = refs[-(plane - 1) :]
    for i, piece in enumerate(refs[: -(plane - 1)]):
        outs[i % (plane - 1)][i // (plane - 1)] = piece[...]


def release_call(ids, pieces, after=()):
    genes, width = pieces[0].shape
    outs = [free((len(pieces) // (plane - 1), genes, width))] * (plane - 1)
    return call(
        release_kernel,
        "release",
        (1,),
        [whole(p.shape) for p in pieces],
        outs,
        [whole(o.shape) for o in outs],
        [],
        ids,
        *pieces,
        after=after,
        mib=14,
    )


def hold_kernel(ids, *refs):
    count = len(refs) // 2
    for given, held in zip(refs[:count], refs[count:]):
        held[...] = given[...]


def hold_call(ids, *arrays, after=()):
    outs = [near(a.shape, a.dtype) for a in arrays]
    return call(
        hold_kernel,
        "hold",
        (1,),
        [whole(a.shape) for a in arrays],
        outs,
        [whole(a.shape) for a in arrays],
        [],
        ids,
        *arrays,
        after=after,
        mib=12,
    )


def add_kernel(ids, mine, came, out):
    out[...] = mine[...] + came[...]


def add_call(ids, mine, came, out=free, after=()):
    return call(
        add_kernel,
        "add",
        (1,),
        [whole(mine.shape)] * 2,
        out(mine.shape),
        whole(mine.shape),
        [],
        ids,
        mine,
        came,
        after=after,
        mib=8,
    )


def split_kernel(ids, mine, came, keep, send, *, extra):
    half = keep.shape[0] - extra
    keep[:half, :] = mine[:half, :] + came[:half, :]
    send[:half, :] = mine[half : 2 * half, :] + came[half : 2 * half, :]
    if extra:
        both = mine[2 * half :, :] + came[2 * half :, :]
        keep[half:, :] = both
        send[half:, :] = both


def split_call(ids, mine, came, extra=0, after=()):
    rows, cols = mine.shape
    shape = ((rows - extra) // 2 + extra, cols)
    return call(
        functools.partial(split_kernel, extra=extra),
        "add_halves",
        (1,),
        [whole(mine.shape)] * 2,
        [near(shape), free(shape)],
        [whole(shape)] * 2,
        [],
        ids,
        mine,
        came,
        after=after,
        mib=16,
    )


def phi_of(u, feature_matrix, factor):
    features = feature_matrix.shape[1] // 2
    wide = u.astype(f32)
    square = (wide * wide * (0.5 * factor)).astype(bf16)
    power = nn(jnp.concatenate([u, square], axis=1), feature_matrix[...])
    scale = factor * math.log2(math.e)
    return jnp.exp2(power * scale - 0.5 * math.log2(features)).astype(bf16)


def put_summary(out, pair, pairs, both, totals, head_size, features):
    half = pair // (pairs // 2)
    at = (pair % (pairs // 2)) * 2
    base = pairs * head_size
    for i in range(2):
        cols = slice(i * features, (i + 1) * features)
        out[half, (at + i) * head_size : (at + i + 1) * head_size, :] = both[
            i * head_size : (i + 1) * head_size, cols
        ]
        out[half, base + at + i : base + at + i + 1, :] = totals[i][:, cols]


def block_matrix(matrix, mine, other, flip, pairs, head_size, features, with_totals):
    base = pairs * head_size
    for pair in range(pairs):
        half = pair // (pairs // 2)
        at = (pair % (pairs // 2)) * 2
        first = (flip ^ half) == 0

        def take(lo, hi):
            return jnp.where(first, mine[lo:hi, :], other[lo:hi, :])

        nothing = jnp.zeros((head_size, features), bf16)
        for i in range(2):
            rows = slice(i * head_size, (i + 1) * head_size)
            part = take((at + i) * head_size, (at + i + 1) * head_size).astype(bf16)
            matrix[pair, rows, i * features : (i + 1) * features] = part
            matrix[pair, rows, (1 - i) * features : (2 - i) * features] = nothing
            if with_totals:
                rows = slice((2 + i) * head_size, (3 + i) * head_size)
                total = take(base + at + i, base + at + i + 1)
                spread = jnp.broadcast_to(total, (head_size, features)).astype(bf16)
                matrix[pair, rows, i * features : (i + 1) * features] = spread
                matrix[pair, rows, (1 - i) * features : (2 - i) * features] = nothing


def payload_shape(heads, head_size, features):
    rows = heads // 2 * head_size + heads // 2
    return (rows + (-rows) % 8, features)


def key_kernel(
    ids, h0, h1, h2, h3, weight, bias, gain, shift, feats, normed, joint, phi, mine, sent, out, *, factor
):
    genes, width = h0.shape
    features = feats.shape[1] // 2
    pair_width = feats.shape[0] // 2
    pairs = width // pair_width
    for r, block in enumerate((h0, h1, h2, h3)):
        scaled, _ = norm_parts(block[...])
        normed[r * genes : (r + 1) * genes, :] = (scaled * gain[...] + shift[...]).astype(bf16)
    for part in (1, 2, 0):
        cols = slice(part * width, (part + 1) * width)
        joint[:, cols] = (nn(normed[...], weight[:, cols]) + bias[:, cols]).astype(bf16)
    rows_used = pairs * (pair_width // 2) + pairs
    spare = out.shape[1] - rows_used
    if spare:
        for i in range(2):
            out[i, rows_used:, :] = jnp.zeros((spare, features), f32)
    for pair in range(pairs):
        at = width + pair * pair_width
        low = phi_of(joint[:, at : at + pair_width], feats, factor)
        phi[:, pair * 2 * features : (pair + 1) * 2 * features] = low
        value = joint[:, width + at : width + at + pair_width]
        total = col_sum(low.astype(f32))
        put_summary(out, pair, pairs, tn(value, low), (total, total), pair_width // 2, features)
    mine[...] = out[ids[3]]
    sent[...] = out[1 - ids[3]]


def key_call(ids, hidden, weight, bias, gain, shift, feats, factor, after=()):
    genes, width = hidden[0].shape
    tokens = plane * genes
    features = feats.shape[1] // 2
    heads = 2 * width // (feats.shape[0] // 2)
    pay = payload_shape(heads, width // heads, features)
    outs = [
        far((tokens, width), bf16),
        near((tokens, 3 * width), bf16),
        far((tokens, heads * features), bf16),
        near(pay),
        free(pay),
    ]
    ins = list(hidden) + [weight, bias, gain, shift, feats]
    return call(
        functools.partial(key_kernel, factor=factor),
        "key_summary",
        (1,),
        [whole(a.shape) for a in ins],
        outs,
        [whole(o.shape) for o in outs],
        [pltpu.VMEM((2, *pay), f32)],
        ids,
        *ins,
        after=after,
        mib=24,
    )


def query_kernel(ids, joint, feats, phi, *, factor):
    features = feats.shape[1] // 2
    pair_width = feats.shape[0] // 2
    for pair in range(joint.shape[1] // pair_width):
        u = joint[:, pair * pair_width : (pair + 1) * pair_width]
        phi[:, pair * 2 * features : (pair + 1) * 2 * features] = phi_of(u, feats, factor)


def query_call(ids, joint, feats, factor, after=()):
    tokens, wide = joint.shape
    width = wide // 3
    features = feats.shape[1] // 2
    heads = 2 * width // (feats.shape[0] // 2)
    step = tokens // 2
    return call(
        functools.partial(query_kernel, factor=factor),
        "query_features",
        (2,),
        [pl.BlockSpec((step, width), lambda at, ids: (at, 0)), whole(feats.shape)],
        near((tokens, heads * features), bf16),
        pl.BlockSpec((step, heads * features), lambda at, ids: (at, 0)),
        [],
        ids,
        joint,
        feats,
        after=after,
        mib=16,
    )


def gelu_parts(x):
    expo = jnp.exp2(x * x * (-0.5 * math.log2(math.e)))
    t = 1.0 / (1.0 + (0.3275911 * math.sqrt(0.5)) * jnp.abs(x))
    poly = t * (
        0.5 * 0.254829592
        + t
        * (
            0.5 * -0.284496736
            + t * (0.5 * 1.421413741 + t * (0.5 * -1.453152027 + t * (0.5 * 1.061405429)))
        )
    )
    tail = poly * expo
    return jnp.where(x > 0, 1.0 - tail, tail), expo * 0.3989422804014327


def feed_kernel(
    ids, h0, h1, h2, h3, c0, c1, c2, c3, phi, mine, other, w_out, b_out, gain, shift, w_up, b_up, w_low, b_low,
    g0, g1, g2, g3, active, d_upper, normed, attention, d_middle, d_branch, d_num, cot_low, mine_out, sent_out, sums, up_sums,
    pay, matrix, att_wide, recip, scaled_ref, back, result,
):
    genes, width = h0.shape
    pairs = matrix.shape[0]
    features = phi.shape[1] // pairs // 2
    pair_width = width // pairs
    head_size = pair_width // 2
    chunk = 1024
    blocks = [slice(r * genes, (r + 1) * genes) for r in range(plane)]
    block_matrix(matrix, mine, other, ids[3], pairs, head_size, features, True)
    for rows, block in zip(blocks, (c0, c1, c2, c3)):
        cot_low[rows, :] = block[...].astype(bf16)
    for pair in range(pairs):
        cols = slice(pair * pair_width, (pair + 1) * pair_width)
        both = nt(phi[:, pair * 2 * features : (pair + 1) * 2 * features], matrix[pair])
        inverse = 1.0 / both[:, pair_width:]
        quotient = both[:, :pair_width] * inverse
        att_wide[:, cols] = quotient
        recip[:, cols] = inverse
        attention[:, cols] = quotient.astype(bf16)
    result[...] = nn(attention[...], w_out[...]) + b_out[...]
    for rows, block in zip(blocks, (h0, h1, h2, h3)):
        mid = block[...] + result[rows, :]
        result[rows, :] = mid + b_low[...]
        scaled, inverse = norm_parts(mid)
        scaled_ref[rows, :] = scaled
        normed[rows, :] = (scaled * gain[...] + shift[...]).astype(bf16)
        back[rows, :] = jnp.broadcast_to(inverse, scaled.shape)
    d_middle[...] = back[...]
    for at in range(w_up.shape[1] // chunk):
        cols = slice(at * chunk, (at + 1) * chunk)
        upper = nn(normed[...], w_up[:, cols]) + b_up[:, cols]
        grad_active = nt(cot_low[...], w_low[cols, :])
        cumulative, density = gelu_parts(upper)
        active[:, cols] = (upper * cumulative).astype(bf16)
        low = (grad_active * (cumulative + upper * density)).astype(bf16)
        d_upper[:, cols] = low
        up_sums[:, cols] = col_sum(low.astype(f32))
        if at == 0:
            back[...] = nt(low, w_up[:, cols])
        else:
            back[...] += nt(low, w_up[:, cols])
        result[...] += nn(active[:, cols], w_low[cols, :])
    for rows, block in zip(blocks, (g0, g1, g2, g3)):
        block[...] = result[rows, :]
    grad_normed = back[...]
    scaled = scaled_ref[...]
    cot = cot_low[...].astype(f32)
    grad_mid = cot + norm_back(grad_normed, scaled, d_middle[...], gain[...])
    d_middle[...] = grad_mid
    branch = grad_mid.astype(bf16)
    d_branch[...] = branch
    sums[0:1, :] = col_sum(grad_normed * scaled)
    sums[1:2, :] = col_sum(grad_normed)
    sums[2:3, :] = col_sum(branch.astype(f32))
    sums[3:4, :] = col_sum(cot)
    sums[4:, :] = jnp.zeros((sums.shape[0] - 4, width), f32)
    back[...] = nt(branch, w_out[...])
    row = lax.broadcasted_iota(jnp.int32, (2 * pair_width, pair_width), 0) // head_size % 2
    col = lax.broadcasted_iota(jnp.int32, (2 * pair_width, pair_width), 1) // head_size
    ones = jnp.where(row == col, 1.0, 0.0).astype(bf16)
    rows_used = pairs * head_size + pairs
    spare = pay.shape[1] - rows_used
    if spare:
        for i in range(2):
            pay[i, rows_used:, :] = jnp.zeros((spare, features), f32)
    for pair in range(pairs):
        cols = slice(pair * pair_width, (pair + 1) * pair_width)
        grad = back[:, cols]
        inverse = recip[:, cols]
        product = grad * att_wide[:, cols]
        high = product.astype(bf16)
        low = (product - high.astype(f32)).astype(bf16)
        total = nn(jnp.concatenate([high, low], axis=1), ones)
        at = pair * 2 * pair_width
        d_num[:, at : at + pair_width] = (grad * inverse).astype(bf16)
        d_num[:, at + pair_width : at + 2 * pair_width] = (
            total * inverse * (-1.0 / head_size)
        ).astype(bf16)
        both = tn(
            d_num[:, at : at + 2 * pair_width],
            phi[:, pair * 2 * features : (pair + 1) * 2 * features],
        )
        totals = [
            both[pair_width + i * head_size : pair_width + i * head_size + 1, :] * float(head_size)
            for i in range(2)
        ]
        put_summary(pay, pair, pairs, both, totals, head_size, features)
    mine_out[...] = pay[ids[3]]
    sent_out[...] = pay[1 - ids[3]]


def feed_call(
    ids, hidden, cots, phi, mine, other, w_out, b_out, gain, shift, w_up, b_up, w_low, b_low, heads, after=()
):
    genes, width = hidden[0].shape
    tokens = plane * genes
    step = tokens
    features = phi.shape[1] // heads
    wide = w_up.shape[1]
    pairs = heads // 2
    pay = payload_shape(heads, width // heads, features)

    def rows(cols):
        return pl.BlockSpec((step, cols), lambda at, ids: (at, 0))

    ins = list(hidden) + list(cots) + [phi, mine, other, w_out, b_out, gain, shift, w_up, b_up, w_low, b_low]
    in_specs = [whole(a.shape) for a in ins]
    in_specs[2 * plane] = rows(phi.shape[1])
    outs = [(near((genes, width)), whole((genes, width)))] * plane + [
        (near((tokens, wide), bf16), rows(wide)),
        (near((tokens, wide), bf16), rows(wide)),
        (near((tokens, width), bf16), rows(width)),
        (near((tokens, width), bf16), rows(width)),
        (far((tokens, width)), rows(width)),
        (far((tokens, width), bf16), rows(width)),
        (near((tokens, 2 * width), bf16), rows(2 * width)),
        (far((tokens, width), bf16), rows(width)),
        (near(pay), whole(pay)),
        (free(pay), whole(pay)),
        (near((8, width)), whole((8, width))),
        (near((1, wide)), whole((1, wide))),
    ]
    return call(
        feed_kernel,
        "feed_forward",
        (1,),
        in_specs,
        [o[0] for o in outs],
        [o[1] for o in outs],
        [
            pltpu.VMEM((2, *pay), f32),
            pltpu.VMEM((pairs, 2 * width // pairs, 2 * features), bf16),
        ]
        + [pltpu.VMEM((step, width), f32)] * 5,
        ids,
        *ins,
        after=after,
        mib=22,
    )


def feature_back(grad_feat, phi, u, back_matrix, factor):
    pair_width = u.shape[1]
    low = (grad_feat * phi.astype(f32) * factor).astype(bf16)
    both = nn(low, back_matrix[...])
    return both[:, :pair_width] - factor * u.astype(f32) * both[:, pair_width:]


def d_query_kernel(ids, d_num, phi, query, mine, other, back_matrix, weight, d_query, d_normed, sums, matrix, *, factor):
    step = pl.program_id(0)
    pairs = matrix.shape[0]
    features = phi.shape[1] // pairs // 2
    width = query.shape[1]
    pair_width = width // pairs

    @pl.when(step == 0)
    def _():
        block_matrix(matrix, mine, other, ids[3], pairs, pair_width // 2, features, True)
        sums[...] = jnp.zeros_like(sums)

    for pair in range(pairs):
        cols = slice(pair * pair_width, (pair + 1) * pair_width)
        grad_feat = nn(d_num[:, pair * 2 * pair_width : (pair + 1) * 2 * pair_width], matrix[pair])
        grad = feature_back(
            grad_feat,
            phi[:, pair * 2 * features : (pair + 1) * 2 * features],
            query[:, cols],
            back_matrix,
            factor,
        )
        d_query[:, cols] = grad.astype(bf16)
    low = d_query[...]
    d_normed[...] = nt(low, weight[...])
    sums[...] += col_sum(low.astype(f32))


def d_query_call(ids, d_num, phi, joint, mine, other, back_matrix, weight, factor, after=()):
    tokens = joint.shape[0]
    width = joint.shape[1] // 3
    pair_width = back_matrix.shape[1] // 2
    pairs = width // pair_width
    step = tokens // plane * tile
    features = back_matrix.shape[0] // 2

    def rows(cols):
        return pl.BlockSpec((step, cols), lambda at, ids: (at, 0))

    return call(
        functools.partial(d_query_kernel, factor=factor),
        "query_gradient",
        (plane // tile,),
        [
            rows(2 * width),
            rows(phi.shape[1]),
            rows(width),
            whole(mine.shape),
            whole(other.shape),
            whole(back_matrix.shape),
            whole((width, width)),
        ],
        [near((tokens, width), bf16), near((tokens, width)), near((1, width))],
        [rows(width), rows(width), whole((1, width))],
        [pltpu.VMEM((pairs, 2 * pair_width, 2 * features), bf16)],
        ids,
        d_num,
        phi,
        joint,
        mine,
        other,
        back_matrix,
        weight,
        after=after,
        mib=20,
    )


def d_key_kernel(
    ids, h0, h1, h2, h3, joint, phi, d_query, d_normed_q, d_middle, mine, other, back_matrix, weight, gain,
    g0, g1, g2, g3, d_joint, sums, key_sums, matrix, total_ref, hid, *, factor,
):
    step = pl.program_id(0)
    pairs = matrix.shape[0]
    genes, width = h0.shape
    features = phi.shape[1] // pairs // 2
    pair_width = width // pairs
    head_size = pair_width // 2

    @pl.when(step == 0)
    def _():
        block_matrix(matrix, mine, other, ids[3], pairs, head_size, features, False)
        base = pairs * head_size
        for pair in range(pairs):
            half = pair // (pairs // 2)
            at = base + (pair % (pairs // 2)) * 2
            first = (ids[3] ^ half) == 0
            for i in range(2):
                total_ref[pair : pair + 1, i * features : (i + 1) * features] = jnp.where(
                    first, mine[at + i : at + i + 1, :], other[at + i : at + i + 1, :]
                )
        sums[...] = jnp.zeros_like(sums)
        key_sums[...] = jnp.zeros_like(key_sums)

    for k in range(plane // tile):

        @pl.when(step == k)
        def _():
            for i in range(tile):
                hid[i * genes : (i + 1) * genes, :] = (h0, h1, h2, h3)[k * tile + i][...]

    d_joint[:, :width] = d_query[...]
    for pair in range(pairs):
        at = pair * pair_width
        value = joint[:, 2 * width + at : 2 * width + at + pair_width]
        low = phi[:, pair * 2 * features : (pair + 1) * 2 * features]
        grad_feat = nn(value, matrix[pair]) + total_ref[pair : pair + 1, :]
        grad = feature_back(
            grad_feat, low, joint[:, width + at : width + at + pair_width], back_matrix, factor
        )
        d_joint[:, width + at : width + at + pair_width] = grad.astype(bf16)
        d_joint[:, 2 * width + at : 2 * width + at + pair_width] = nt(low, matrix[pair]).astype(bf16)
    low = d_joint[:, width:]
    key_sums[...] += col_sum(low.astype(f32))
    grad_normed = d_normed_q[...] + nt(low, weight[:, width:])
    scaled, inverse = norm_parts(hid[...])
    result = (d_middle[...] + norm_back(grad_normed, scaled, inverse, gain[...])).astype(bf16)
    result = result.astype(f32)
    sums[0:1, :] += col_sum(grad_normed * scaled)
    sums[1:2, :] += col_sum(grad_normed)
    sums[2:3, :] += col_sum(result)
    for k in range(plane // tile):

        @pl.when(step == k)
        def _():
            for i in range(tile):
                (g0, g1, g2, g3)[k * tile + i][...] = result[i * genes : (i + 1) * genes, :]


def d_key_call(ids, hidden, joint, phi, d_query, d_normed_q, d_middle, mine, other, back_matrix, weight, gain, factor, after=()):
    genes, width = hidden[0].shape
    tokens = plane * genes
    step = tile * genes
    pair_width = back_matrix.shape[1] // 2
    pairs = width // pair_width
    features = back_matrix.shape[0] // 2

    def rows(cols):
        return pl.BlockSpec((step, cols), lambda at, ids: (at, 0))

    ins = list(hidden) + [joint, phi, d_query, d_normed_q, d_middle, mine, other, back_matrix, weight, gain]
    in_specs = [whole(a.shape) for a in ins]
    for i in range(5):
        in_specs[plane + i] = rows(ins[plane + i].shape[1])
    outs = [(near((genes, width)), whole((genes, width)))] * plane + [
        (near((tokens, 3 * width), bf16), rows(3 * width)),
        (near((8, width)), whole((8, width))),
        (near((1, 2 * width)), whole((1, 2 * width))),
    ]
    return call(
        functools.partial(d_key_kernel, factor=factor),
        "key_gradient",
        (plane // tile,),
        in_specs,
        [o[0] for o in outs],
        [o[1] for o in outs],
        [
            pltpu.VMEM((pairs, pair_width, 2 * features), bf16),
            pltpu.VMEM((8, 2 * features), f32),
            pltpu.VMEM((step, width), f32),
        ],
        ids,
        *ins,
        after=after,
        mib=28,
    )


def put_shards(out, size, spot, where, first, count, per, rows, at, value):
    if rows % 8:
        out[at * size + first * rows : at * size + (first + count) * rows, :] = value
        return
    for s in range(count):
        to = (where(first + s) ^ spot) * per + at
        to = pl.multiple_of(to, 8)
        out[pl.ds(to, rows), :] = value[s * rows : (s + 1) * rows, :]


def in_slots(bundle, size, me, per, rows, order):
    if rows % 8 == 0:
        return bundle
    body = bundle[: size * per].reshape(per // rows, size, rows, -1).transpose(1, 0, 2, 3)
    place = placed(order, size.bit_length() - 1)
    owner = sorted(range(size), key=place)
    body = body[jnp.array(owner, jnp.int32) ^ me].reshape(size * per, -1)
    return jnp.concatenate([body, bundle[size * per :]], axis=0)


def side_of(sent):
    return (lambda ids: 1 - ids[1]) if sent else (lambda ids: ids[1])


def lower_weights_kernel(ids, a0, a1, c0, c1, out, *, size, where, spot_at):
    step = pl.program_id(0)
    part = size // 4
    rows = out.shape[0] // size
    value = tn(a0[...], c0[...]) + tn(a1[...], c1[...])
    for k in range(4):

        @pl.when(step == k)
        def _():
            put_shards(out, size, ids[spot_at], where, k * part, part, rows, rows, 0, value)


def lower_weights_call(ids, size, sent, where, spot_at, active, cot_low, after=()):
    tokens, wide = active[0].shape
    half = cot_low[0].shape[1] // 2
    side = side_of(sent)
    shape = (wide, half)
    return call(
        functools.partial(lower_weights_kernel, size=size, where=where, spot_at=spot_at),
        "lower_weights",
        (4,),
        [pl.BlockSpec((tokens, wide // 4), lambda at, ids: (0, at))] * 2
        + [pl.BlockSpec((tokens, half), lambda at, ids: (0, side(ids)))] * 2,
        near(shape),
        whole(shape),
        [],
        ids,
        *active,
        *cot_low,
        after=after,
        mib=16,
    )


def upper_weights_kernel(ids, n0, n1, u0, u1, t0, t1, b0, b1, out, *, size, where, spot_at):
    step = pl.program_id(0)
    part = size // 4
    rows = n0.shape[1] // size
    value = tn(n0[...], u0[...]) + tn(n1[...], u1[...])
    last = tn(t0[...], b0[...]) + tn(t1[...], b1[...])
    for k in range(4):

        @pl.when(step == k)
        def _():
            put_shards(out, size, ids[spot_at], where, 0, size, 5 * rows, rows, k * rows, value)
            put_shards(out, size, ids[spot_at], where, k * part, part, 5 * rows, rows, 4 * rows, last)


def upper_weights_call(ids, size, sent, where, spot_at, normed, d_upper, attention, d_branch, after=()):
    tokens, width = normed[0].shape
    half = width // 2
    side = side_of(sent)
    shape = (5 * width, half)
    return call(
        functools.partial(upper_weights_kernel, size=size, where=where, spot_at=spot_at),
        "upper_weights",
        (4,),
        [pl.BlockSpec((tokens, width), lambda at, ids: (0, 0))] * 2
        + [pl.BlockSpec((tokens, half), lambda at, ids: (0, side(ids) * 4 + at))] * 2
        + [pl.BlockSpec((tokens, width // 4), lambda at, ids: (0, at))] * 2
        + [pl.BlockSpec((tokens, half), lambda at, ids: (0, side(ids)))] * 2,
        near(shape),
        whole(shape),
        [],
        ids,
        *normed,
        *d_upper,
        *attention,
        *d_branch,
        after=after,
        mib=16,
    )


def joint_weights_kernel(ids, n0, n1, j0, j1, out, *, size, where, spot_at):
    step = pl.program_id(0)
    rows = n0.shape[1] // size
    value = tn(n0[...], j0[...]) + tn(n1[...], j1[...])
    for k in range(3):

        @pl.when(step == k)
        def _():
            put_shards(out, size, ids[spot_at], where, 0, size, 3 * rows, rows, k * rows, value)


def joint_weights_call(ids, size, sent, where, spot_at, normed, d_joint, after=()):
    tokens, width = normed[0].shape
    half = width // 2
    side = side_of(sent)
    shape = (3 * width, half)
    return call(
        functools.partial(joint_weights_kernel, size=size, where=where, spot_at=spot_at),
        "joint_weights",
        (3,),
        [pl.BlockSpec((tokens, width), lambda at, ids: (0, 0))] * 2
        + [pl.BlockSpec((tokens, half), lambda at, ids: (0, side(ids) * 3 + at))] * 2,
        near(shape),
        whole(shape),
        [],
        ids,
        *normed,
        *d_joint,
        after=after,
        mib=14,
    )


vector_rows = 32


def input_weights_kernel(ids, *refs, size, where, spot_at):
    own = refs[:2]
    merged = refs[2:5]
    r0, r1, v0, v1, f0, f1, u0, u1, k0, k1, q0, q1, s0, s1, d_low, sent, kept, zero_hidden = refs[5:]
    pieces = [own[j] if r == 0 else merged[r - 1].at[j] for r in range(plane) for j in range(2)]
    genes, width = own[0].shape
    half = width // 2
    rows = (sent.shape[0] - vector_rows) // size
    total = None
    for i, piece in enumerate(pieces):
        wide = piece[...]
        d_low[i * genes : (i + 1) * genes, :] = wide.astype(bf16)
        masked = wide * (v0, v1)[i % 2][i // 2][:, :1]
        total = masked if total is None else total + masked
    zero_hidden[...] = total
    parts = [f0[0:4, :] + f1[0:4, :], s0[0:3, :] + s1[0:3, :], q0[...] + q1[...], k0[...] + k1[...], u0[...] + u1[...]]
    for out, side in ((sent, 1 - ids[1]), (kept, ids[1])):
        value = None
        for i in range(8):
            chosen = (r0, r1)[i % 2][i // 2]
            lo = d_low[i * genes : (i + 1) * genes, :half]
            hi = d_low[i * genes : (i + 1) * genes, half:]
            product = tn(chosen, jnp.where(side == 0, lo, hi))
            value = product if value is None else value + product
        put_shards(out, size, ids[spot_at], where, 0, size, rows, rows, 0, value)
        at = size * rows
        for part in parts:
            for row in range(part.shape[0]):
                for c in range(part.shape[1] // half):
                    out[at : at + 1, :] = part[row : row + 1, c * half : (c + 1) * half]
                    at += 1
        out[at:, :] = jnp.zeros((out.shape[0] - at, half), f32)


def input_weights_call(ids, size, where, spot_at, own, came, rows, vacant, sums, after=()):
    genes, width = own[0].shape
    width_in = rows[0].shape[2]
    ins = [*own, *came, *rows, *vacant, *sums]
    shape = (width_in + vector_rows, width // 2)
    outs = [near((8 * genes, width), bf16), free(shape), near(shape), free((genes, width))]
    return call(
        functools.partial(input_weights_kernel, size=size, where=where, spot_at=spot_at),
        "input_weights",
        (1,),
        [whole(a.shape) for a in ins],
        outs,
        [whole(o.shape) for o in outs],
        [],
        ids,
        *ins,
        after=after,
        mib=28,
    )


def finish_kernel(ids, *refs, parts):
    first_core = ids[1] == 0
    outs = refs[-len(parts) :]
    for out, (bundle, rows, groups, at) in zip(outs, parts):
        mine, came = refs[2 * bundle : 2 * bundle + 2]
        half = mine.shape[1]
        for g in range(groups):
            one = mine[at + g * rows : at + (g + 1) * rows, :]
            two = came[at + g * rows : at + (g + 1) * rows, :]
            out[:, g * half : (g + 1) * half] = jnp.where(first_core, one, two)
            out[:, (groups + g) * half : (groups + g + 1) * half] = jnp.where(first_core, two, one)


def finish_call(ids, bundles, parts, after=()):
    ins = [array for pair in bundles for array in pair]
    half = ins[0].shape[1]
    outs = [far((rows, 2 * groups * half)) for _, rows, groups, _ in parts]
    return call(
        functools.partial(finish_kernel, parts=parts),
        "weight_results",
        (1,),
        [whole(a.shape) for a in ins],
        outs,
        [whole(o.shape) for o in outs],
        [],
        ids,
        *ins,
        after=after,
        mib=12,
    )


def out_kernel(ids, *refs):
    out = refs[-1]
    merged = refs[-plane:-1]
    group = len(refs) - plane
    for j in range(group):
        out[ids[2] * group + j] = refs[j][...].astype(bf16)
        for r in range(1, plane):
            out[(ids[2] ^ r) * group + j] = merged[r - 1][j].astype(bf16)


def out_call(ids, own, came, after=()):
    genes, width = own[0].shape
    shape = (plane * len(own), genes, width)
    ins = [*own, *came]
    return call(
        out_kernel,
        "block_out",
        (1,),
        [whole(p.shape) for p in ins],
        far(shape, bf16),
        whole(shape),
        [],
        ids,
        *ins,
        after=after,
        mib=14,
    )


def token_kernel(ids, d_low, index, weight, token_grad):
    slots, _ = index.shape
    width = d_low.shape[1]
    genes = d_low.shape[0] // 8
    slot = lax.broadcasted_iota(jnp.int32, (slots, 1), 0)
    picked = jnp.zeros((slots, width), f32)
    gene = lax.broadcasted_iota(jnp.int32, (slots, genes), 1)
    match = (index[...] - ids[0] * genes) == gene
    for i in range(8):
        cell = i ^ (2 * ids[2])
        here = (slot >= ids[8 + cell]) & (slot < ids[9 + cell])
        chosen = jnp.where(match & here, 1.0, 0.0).astype(bf16)
        picked = picked + nn(chosen, d_low[i * genes : (i + 1) * genes, :])
    token_grad[0] = nt(picked.astype(bf16), weight[...])


def token_call(ids, d_low, index, weight, after=()):
    ins = [d_low, index, weight]
    shape = (1, index.shape[0], weight.shape[0])
    return call(
        token_kernel,
        "token_gradient",
        (1,),
        [whole(a.shape) for a in ins],
        far(shape),
        whole(shape),
        [],
        ids,
        *ins,
        after=after,
        mib=24,
    )


def zero_kernel(ids, mine, other, weight, out):
    total = mine[...] + other[...]
    high = total.astype(bf16)
    rest = total - high.astype(f32)
    low = rest.astype(bf16)
    out[...] = nt(high, weight[...]) + nt(low, weight[...])


def zero_call(ids, mine, other, weight, after=()):
    genes, width = mine.shape
    ins = [mine, other, weight]
    shape = (genes, weight.shape[0])
    return call(
        zero_kernel,
        "zero_gradient",
        (1,),
        [whole(a.shape) for a in ins],
        far(shape),
        whole(shape),
        [],
        ids,
        *ins,
        after=after,
        mib=12,
    )


def local(
    encoder_packed_tokens,
    token_gene_index,
    cell_counts,
    zero_embed,
    random_features,
    input_weight,
    input_bias,
    first_gain,
    first_shift,
    joint_weight,
    joint_bias,
    output_weight,
    output_bias,
    second_gain,
    second_shift,
    upper_weight,
    upper_bias,
    lower_weight,
    lower_bias,
    cotangent,
):
    placed_at.clear()
    size = lax.axis_size("gene")
    me = lax.axis_index("gene")
    core = lax.axis_index("cell")
    cells_here, genes, width = cotangent.shape
    head_size, features = random_features.shape
    heads = width // head_size
    factor = head_size ** (-0.25)
    group = cells_here // plane
    log = size.bit_length() - 1
    rest = list(range(3, log))
    orders = ([2, 0, 1] + rest, [2, 0, 1] + rest, [1, 0, 2] + rest, [0, 1, 2] + rest)
    where = [placed(order, log) for order in orders]
    ends = jnp.cumsum(cell_counts[0]).astype(jnp.int32)
    ids = jnp.concatenate(
        [
            jnp.stack([me, core, me % plane, (me // plane) % 2]).astype(jnp.int32),
            jnp.stack([placed(order, log)(me) for order in orders]).astype(jnp.int32),
            jnp.zeros((1,), jnp.int32),
            ends,
        ]
    )
    nothing = jnp.zeros((head_size, features), bf16)
    minus = jnp.full((head_size, features), -1.0, bf16)
    feats = jnp.concatenate(
        [
            jnp.concatenate([random_features, nothing], axis=1),
            jnp.concatenate([nothing, random_features], axis=1),
            jnp.concatenate([minus, nothing], axis=1),
            jnp.concatenate([nothing, minus], axis=1),
        ],
        axis=0,
    )
    back_matrix = jnp.concatenate([feats[: 2 * head_size].T, -feats[2 * head_size :].T], axis=1)

    def row(vector):
        return vector.reshape(1, -1)

    high = [1 << b for b in range(2, log)]
    last = ()

    def then(made, token, *more):
        nonlocal last
        last = (token, *more)
        return made

    def gene_swap(value, bit):
        return swap(value, "gene", size, bit)

    def out_and_in(blocks):
        return [block if r == 0 else gene_swap(block, r) for r, block in enumerate(blocks)]

    class Halves:
        def __init__(self, mine, sent):
            self.mine = mine
            self.came = gene_swap(sent, high[0])
            self.left = high[1:]

        def add(self):
            self.mine = add_call(ids, self.mine, self.came, after=last)
            then(None, self.mine)
            if self.left:
                self.came = gene_swap(self.mine, self.left.pop(0))
            else:
                self.other = gene_swap(self.mine, high[0])

        def coming(self):
            return getattr(self, "other", self.came)

        def finish(self):
            while not hasattr(self, "other"):
                self.add()
            return self.mine, self.other

    class Scatter:
        def __init__(self, sent, kept, order, rows, extra=0):
            per = (kept.shape[0] - extra) // size
            self.mine = in_slots(kept, size, me, per, rows, order)
            self.came = swap(in_slots(sent, size, me, per, rows, order), "cell", 2, 1)
            self.order = list(order)
            self.extra = extra

        def add(self):
            if self.order:
                self.mine, send = split_call(ids, self.mine, self.came, self.extra, after=last)
                then(None, self.mine)
                self.came = gene_swap(send, 1 << self.order.pop(0))

        def close(self):
            while self.order:
                self.add()
            self.mine = add_call(ids, self.mine, self.came, after=last)
            then(None, self.mine)
            self.other = swap(self.mine, "cell", 2, 1)

    shard = width // size
    wide_shard = upper_weight.shape[1] // size
    in_shard = input_weight.shape[0] // size
    hidden, rows, vacant = [], [], []
    for j in range(group):
        made = rows_call(
            ids, j, group, encoder_packed_tokens[0], token_gene_index, zero_embed, input_weight, row(input_bias),
            after=last,
        )
        hidden.append(out_and_in(made[:plane]))
        rows.append(made[plane])
        vacant.append(made[plane + 1])
        then(None, made[plane + 1])
    normed, joint, key_phi, sums = [], [], [], []

    def keys_of(j):
        made = key_call(
            ids, hidden[j], joint_weight, row(joint_bias), row(first_gain), row(first_shift), feats, factor,
            after=last,
        )
        normed.append(made[0])
        joint.append(made[1])
        key_phi.append(made[2])
        sums.append(Halves(made[3], made[4]))
        then(None, made[0])

    query_phi = []

    def query_of(j):
        query_phi.append(query_call(ids, joint[j], feats, factor, after=last))
        then(None, query_phi[j])

    keys_of(0)
    w_up, w_low, w_out, w_joint = hold_call(
        ids, upper_weight, lower_weight, output_weight, joint_weight, after=last
    )
    then(None, w_out)
    sums[0].add()
    cots = []

    def cotangent_of(j):
        wide = cotangent_call(ids, j, group, cotangent, after=last)
        then(None, wide[0])
        cots.append(out_and_in(wide))

    keys_of(1)
    cotangent_of(0)
    sums[0].add()
    sums[1].add()
    query_of(0)
    query_of(1)
    then(None, *last, *cots[0][1:])
    cotangent_of(1)
    sums[1].finish()
    sums = [s.finish() for s in sums]
    fed, d_sums = [], []
    for j in range(group):
        made = feed_call(
            ids, hidden[j], cots[j], query_phi[j], *sums[j], w_out, row(output_bias), row(second_gain),
            row(second_shift), w_up, row(upper_bias), w_low, row(lower_bias), heads,
            after=last,
        )
        fed.append(made)
        d_sums.append(Halves(made[plane + 8], made[plane + 9]))
        then(None, made[plane + 2])
    active, d_upper, normed_two, attention, d_middle, d_branch, d_num, cot_low, _, _, sums_two, up_sums = list(
        zip(*fed)
    )[plane:]
    queries = []

    def d_query_of(j):
        queries.append(
            d_query_call(
                ids, d_num[j], query_phi[j], joint[j], *sums[j], back_matrix, w_joint, factor, after=last
            )
        )
        then(None, queries[j][1])

    def lower_of(sent):
        made = lower_weights_call(ids, size, sent, where[0], 4, active, cot_low, after=last)
        return then(made, made)

    def upper_of(sent):
        made = upper_weights_call(
            ids, size, sent, where[1], 5, normed_two, d_upper, attention, d_branch, after=last
        )
        return then(made, made)

    def joint_of(sent):
        made = joint_weights_call(ids, size, sent, where[2], 6, normed, d_joint, after=last)
        return then(made, made)

    def pass_on(*arrays):
        made = pass_call(ids, *arrays, after=last)
        then(None, made[0])
        return made

    def release(blocks):
        sent = release_call(ids, [block[r] for block in blocks for r in range(1, plane)], after=last)
        then(None, sent[0])
        return [gene_swap(block, r) for r, block in enumerate(sent, 1)]

    keys = []

    def d_key_of(j):
        made = d_key_call(
            ids, hidden[j], joint[j], key_phi[j], queries[j][0], queries[j][1], d_middle[j], *d_sums[j].finish(),
            back_matrix, w_joint, row(first_gain), factor,
            after=last,
        )
        keys.append(made)
        then(None, made[plane])

    back_out = release([made[:plane] for made in fed])
    d_sums[0].add()
    d_query_of(0)
    d_query_of(1)
    d_sums[1].add()
    upper_sent = upper_of(True)
    d_sums[0].add()
    upper_kept = upper_of(False)
    d_sums[1].add()
    then(None, *last, *back_out, d_sums[0].coming())
    (upper_sent,) = pass_on(upper_sent)
    upper_sum = Scatter(upper_sent, upper_kept, orders[1], shard)
    d_key_of(0)
    d_key_of(1)
    backs = release([k[:plane] for k in keys])
    upper_sum.add()
    d_joint = [k[plane] for k in keys]
    joint_sent = joint_of(True)
    joint_kept = joint_of(False)
    lower_sent = lower_of(True)
    lower_kept = lower_of(False)
    block_out = out_call(ids, [made[0] for made in fed], back_out, after=last)
    then(None, block_out)
    sums_one = [k[plane + 1] for k in keys]
    key_sums = [k[plane + 2] for k in keys]
    query_sums = [q[2] for q in queries]
    then(None, *last, upper_sum.came, *backs)
    joint_sent, lower_sent = pass_on(joint_sent, lower_sent)
    lower_sum = Scatter(lower_sent, lower_kept, orders[0], wide_shard)
    joint_sum = Scatter(joint_sent, joint_kept, orders[2], shard)
    d_low, input_sent, input_kept, zero_hidden = input_weights_call(
        ids, size, where[3], 7, [k[0] for k in keys], backs, rows, vacant,
        [*sums_two, *up_sums, *key_sums, *query_sums, *sums_one],
        after=last,
    )
    then(None, zero_hidden)
    input_sum = Scatter(input_sent, input_kept, orders[3], in_shard, vector_rows)
    zero_came = swap(zero_hidden, "cell", 2, 1)
    joint_sum.add()
    upper_sum.add()
    lower_sum.add()
    input_sum.add()
    token_grad = token_call(ids, d_low, token_gene_index.reshape(-1, 1), input_weight, after=last)
    then(None, token_grad)
    zero_grad = zero_call(ids, zero_hidden, zero_came, input_weight, after=last)
    then(None, zero_grad)
    upper_sum.add()
    joint_sum.add()
    lower_sum.add()
    input_sum.add()
    upper_sum.add()
    input_sum.add()
    input_sum.add()
    upper_sum.close()
    joint_sum.add()
    lower_sum.add()
    input_sum.close()
    joint_sum.add()
    lower_sum.add()
    flat = input_sum.mine[in_shard:].reshape(-1)
    lengths = [width] * 7 + [3 * width, upper_weight.shape[1]]
    found = []
    at = 0
    for length in lengths:
        part = length // size
        found.append(lax.dynamic_slice(flat, (at + me * part,), (part,)))
        at += length
    then(None, *last, *found)
    joint_sum.close()
    lower_sum.close()
    g_lower, g_upper, g_output, g_joint, g_input = finish_call(
        ids,
        [(b.mine, b.other) for b in (lower_sum, upper_sum, joint_sum, input_sum)],
        [
            (0, wide_shard, 1, 0),
            (1, shard, 4, 0),
            (1, shard, 1, 4 * shard),
            (2, shard, 3, 0),
            (3, in_shard, 1, 0),
        ],
        after=last,
    )
    small_out = [found[i] for i in (6, 4, 5, 7, 2, 0, 1, 8, 3)]
    return (
        block_out,
        token_grad,
        zero_grad,
        g_input,
        small_out[0],
        small_out[1],
        small_out[2],
        g_joint,
        small_out[3],
        g_output,
        small_out[4],
        small_out[5],
        small_out[6],
        g_upper,
        small_out[7],
        g_lower,
        small_out[8],
    )


def solution(mesh):
    return jax.shard_map(
        local,
        mesh=mesh,
        in_specs=(
            P("cell", "gene", None),
            P("cell", "gene"),
            P("cell", "gene"),
            P("gene", None),
            P(),
            P(),
            P(),
            P(),
            P(),
            P(),
            P(),
            P(),
            P(),
            P(),
            P(),
            P(),
            P(),
            P(),
            P(),
            P("cell", "gene", None),
        ),
        out_specs=(
            P("cell", "gene", None),
            P("cell", "gene", None),
            P("gene", None),
            P("gene", None),
            P("gene"),
            P("gene"),
            P("gene"),
            P("gene", None),
            P("gene"),
            P("gene", None),
            P("gene"),
            P("gene"),
            P("gene"),
            P("gene", None),
            P("gene"),
            P("gene", None),
            P("gene"),
        ),
        check_vma=False,
    )
```
